128 devices in a mesh: seq: 16 (over x_lo, z, core), head: 8 (over x_hi, y).
Axes of the slice: x: 4 (x_hi: 2, x_lo: 2; x = x_hi * 2 + x_lo), y: 4, z: 4, core: 2. Of those that a mesh axis runs over, the one named last changes fastest.
Arguments:
- queries: bfloat16 [4096, 3072], P('seq', 'head'), may hold values from -8 to 8
- keys: bfloat16 [4096, 3072], P('seq', 'head'), may hold values from -8 to 8
- values: bfloat16 [4096, 3072], P('seq', 'head'), may hold values from -6 to 6
- slide_ids: int32 [16384], P('seq'), may hold values from 0 to 15, never falling along the last dimension, each value on 1 to 10240 neighbouring positions
- head_shift_list: int32 [16], replicated, may hold values from 0 to 3
- out_weight: bfloat16 [768, 768], P('head'), may hold values from -0.625 to 0.625
- d_y: bfloat16 [16384, 768], P(('seq', 'head')), may hold values from -6 to 6
Outputs:
- layer_out: bfloat16 [16384, 768], P(('seq', 'head'))
- d_queries: bfloat16 [4096, 3072], P('seq', 'head')
- d_keys: bfloat16 [4096, 3072], P('seq', 'head')
- d_values: bfloat16 [4096, 3072], P('seq', 'head')
- d_weight: bfloat16 [768, 768], P('head')
The draws below stay inside these ranges and needn't reach their ends.
Inputs may be any that keep to these rules, and one draw needn't show every extreme that they name: `slide_ids`: slide numbers never fall along the tokens; each slide holds 1 to 10240 tokens, and one holds exactly (10) * 1024.
All inputs are finite; a program needn't handle non-finite values.
Results may differ from the reference program's by a relative error of at most 0.012.
The reference program's roundings to bfloat16 on the way count: a program that leaves them out, or rounds other values in their place, can miss the bound.
Values may be sent and summed in bfloat16 or wider, within the bound.
A program may use at most 128 MiB of HBM per device.

```python
import math
import jax
import jax.numpy as jnp
import numpy as np
from jax import lax

MODEL_WIDTH = 768
ATTENTION_HEADS = 16
HEAD_SIZE = 48
TOK_DEV = 1024
SEG_A = 1024
DILATION_RATE = 4
TILE_TOKENS = 16384
SLIDES = 16
N_SEQ = 16


def from_drawn_drawn(weight_matrix):
    return weight_matrix.reshape(TILE_TOKENS // DILATION_RATE, DILATION_RATE, ATTENTION_HEADS, HEAD_SIZE).transpose(0, 2, 1, 3).reshape(TILE_TOKENS // DILATION_RATE, ATTENTION_HEADS * DILATION_RATE * HEAD_SIZE)


def draw_queries(key, part):
    key = jax.random.fold_in(key, 3)
    base_rows = jnp.clip(1.3 * jax.random.normal(key, (TILE_TOKENS, MODEL_WIDTH), jnp.float32), -6.0, 6.0)
    return from_drawn_drawn(base_rows).astype(jnp.bfloat16)


def draw_keys(key, part):
    key = jax.random.fold_in(key, 4)
    base_rows = jnp.clip(1.3 * jax.random.normal(key, (TILE_TOKENS, MODEL_WIDTH), jnp.float32), -6.0, 6.0)
    return from_drawn_drawn(base_rows).astype(jnp.bfloat16)


def touch_ends(values, own_key, smallest, top_value):
    longest = values.shape.index(max(values.shape))
    spots = []
    for shift in (0, 1):
        where = [jax.random.randint(jax.random.fold_in(own_key, axis), (), 0, length) for axis, length in enumerate(values.shape)]
        where[longest] = (where[longest] + shift) % values.shape[longest]
        spots.append(tuple(where))
    return values.at[spots[0]].set(smallest).at[spots[1]].set(top_value)


def level_of(key, extent, split, low, largest):
    def one(axis_at, parts):
        heights = jax.random.uniform(jax.random.fold_in(jax.random.fold_in(key, 6), axis_at), (parts,), jnp.float32, low / len(split), largest / len(split))
        return jnp.repeat(jnp.exp(heights), extent[axis_at] // parts).reshape((-1,) + (1,) * (len(extent) - axis_at - 1))

    level = one(*split[0])
    for cut in split[1:]:
        level = level * one(*cut)
    return level


def profile(count, total, most, slope):
    portions = [(1 << 20) // math.isqrt(standing ** slope) + 1 for standing in range(2, count + 1)]
    spare, holding = total - most - (count - 1), [1] * (count - 1)
    while spare > 0:
        movable = [i for i in range(count - 1) if holding[i] < most]
        mass, budget = sum([portions[i] for i in movable]), spare
        for i in movable:
            addition = min(most - holding[i], max(1, budget * portions[i] // mass), spare)
            holding[i] = holding[i] + addition
            spare = spare - addition
    return np.array([most] + holding)


def uneven(own_key, amount, total, limit, skew):
    if amount == 2:
        one = jax.random.randint(own_key, (), max(1, total - limit), min(limit, total - 1) + 1)
        return jnp.stack([one, total - one])
    tallies = jnp.asarray(profile(amount, total, limit, skew), jnp.int32)
    pairs = (amount - 1) // 2
    source_of, receiver = tallies[1:1 + 2 * pairs:2], tallies[2:2 + 2 * pairs:2]
    slack = jnp.minimum(source_of - 1, limit - receiver)
    passed = jax.random.randint(jax.random.fold_in(own_key, 1), (pairs,), 0, 1 << 20) % (slack + 1)
    tallies = tallies.at[1:1 + 2 * pairs:2].set(source_of - passed).at[2:2 + 2 * pairs:2].set(receiver + passed)
    return tallies[jax.random.permutation(jax.random.fold_in(own_key, 2), amount)]


def normal_values(own_key, extent, deviation, reach, shards=(), kind=jnp.bfloat16):
    entries = jax.random.normal(own_key, extent, jnp.float32) * deviation
    if len(shards) > 0:
        entries = level_of(own_key, extent, shards, -0.22, 0.18) * entries
    return jnp.clip(entries, min=-reach, max=reach).astype(kind)


def setup_inputs(seed: int = 0) -> dict:
    splits = jax.random.split(jax.random.key(seed), 8)
    return {
        "queries": draw_queries(jax.random.fold_in(splits[7], 71), 0),
        "keys": draw_keys(jax.random.fold_in(splits[7], 71), 0),
        "values": normal_values(splits[2], (TILE_TOKENS // DILATION_RATE, ATTENTION_HEADS * DILATION_RATE * HEAD_SIZE), 1.0, 6.0, ((0, 16), (1, 8))),
        "slide_ids": jnp.searchsorted(jnp.cumsum(uneven(splits[3], SLIDES, TILE_TOKENS, (N_SEQ // 2 + 2) * TOK_DEV, 2)), jnp.arange(TILE_TOKENS), side="right").astype(jnp.int32),
        "head_shift_list": touch_ends(jax.random.randint(splits[4], (ATTENTION_HEADS,), 0, DILATION_RATE), jax.random.fold_in(splits[4], 1), 0, DILATION_RATE - 1).astype(jnp.int32),
        "out_weight": normal_values(splits[5], (MODEL_WIDTH, MODEL_WIDTH), (2 * HEAD_SIZE) ** -0.5, 0.625, ((0, 8),)),
        "d_y": normal_values(splits[6], (TILE_TOKENS, MODEL_WIDTH), 1.0, 6.0, ((0, 128),)),
    }


def to_plain(weight_matrix):
    return weight_matrix.reshape(TILE_TOKENS // DILATION_RATE, ATTENTION_HEADS, DILATION_RATE, HEAD_SIZE).transpose(0, 2, 1, 3).reshape(TILE_TOKENS, MODEL_WIDTH)

def from_plain(weight_matrix):
    return weight_matrix.reshape(TILE_TOKENS // DILATION_RATE, DILATION_RATE, ATTENTION_HEADS, HEAD_SIZE).transpose(0, 2, 1, 3).reshape(TILE_TOKENS // DILATION_RATE, ATTENTION_HEADS * DILATION_RATE * HEAD_SIZE)

def pick_rows(weight_matrix, head_shift):
    reshaped_input = weight_matrix.reshape((weight_matrix.shape[0] // DILATION_RATE, DILATION_RATE) + weight_matrix.shape[1:])
    return lax.dynamic_index_in_dim(reshaped_input, head_shift, 1, keepdims=False)

def place_rows(weight_matrix, chosen, head_shift, combine):
    reshaped_input = weight_matrix.reshape((weight_matrix.shape[0] // DILATION_RATE, DILATION_RATE) + weight_matrix.shape[1:])
    flag_value = (jnp.arange(DILATION_RATE) == head_shift).reshape((1, DILATION_RATE) + (1,) * (weight_matrix.ndim - 1))
    return jnp.where(flag_value, combine(reshaped_input, jnp.expand_dims(chosen, 1)), reshaped_input).reshape(weight_matrix.shape)

def add_terms(first_term, second_term):
    return first_term + second_term

def round_trip(float_rows):
    return lax.optimization_barrier(float_rows.astype(jnp.bfloat16)).astype(jnp.float32)

def one_head(query_cols, key_cols, value_cols, grad_cols, slide_ids, head_shift):
    inv_scale = 1.0 / math.sqrt(HEAD_SIZE)
    q_all = query_cols.astype(jnp.float32)
    k_all = key_cols.astype(jnp.float32)
    v_all = value_cols.astype(jnp.float32)
    g_all = grad_cols.astype(jnp.float32)
    q_near = q_all.reshape(-1, SEG_A, HEAD_SIZE)
    k_near = k_all.reshape(-1, SEG_A, HEAD_SIZE)
    v_near = v_all.reshape(-1, SEG_A, HEAD_SIZE)
    g_near = g_all.reshape(-1, SEG_A, HEAD_SIZE)
    id_near = slide_ids.reshape(-1, SEG_A)
    near_mask = id_near[:, :, None] == id_near[:, None, :]
    near_scores = jnp.einsum('gqe,gke->gqk', q_near, k_near) * inv_scale
    q_far = pick_rows(q_all, head_shift)
    k_far = pick_rows(k_all, head_shift)
    v_far = pick_rows(v_all, head_shift)
    g_far = pick_rows(g_all, head_shift)
    id_far = pick_rows(slide_ids, head_shift)
    far_mask = id_far[:, None] == id_far[None, :]
    far_scores = jnp.dot(q_far, k_far.T) * inv_scale
    near_top = lax.optimization_barrier(jnp.max(jnp.where(near_mask, near_scores, -jnp.inf), axis=2)).reshape(TILE_TOKENS)
    far_top = lax.optimization_barrier(jnp.max(jnp.where(far_mask, far_scores, -jnp.inf), axis=1))
    row_top = place_rows(near_top, far_top, head_shift, jnp.maximum)
    near_exp = jnp.where(near_mask, jnp.exp(near_scores - row_top.reshape(-1, SEG_A)[:, :, None]), 0.0)
    far_exp = jnp.where(far_mask, jnp.exp(far_scores - pick_rows(row_top, head_shift)[:, None]), 0.0)
    row_total = place_rows(lax.optimization_barrier(jnp.sum(near_exp, axis=2)).reshape(TILE_TOKENS), lax.optimization_barrier(jnp.sum(far_exp, axis=1)), head_shift, add_terms)
    near_prob = near_exp / row_total.reshape(-1, SEG_A)[:, :, None]
    far_prob = far_exp / pick_rows(row_total, head_shift)[:, None]
    near_round = round_trip(near_prob)
    far_round = round_trip(far_prob)
    near_value = jnp.einsum('gqk,gke->gqe', near_round, v_near).reshape(TILE_TOKENS, HEAD_SIZE)
    attn_out = place_rows(near_value, jnp.dot(far_round, v_far), head_shift, add_terms).astype(jnp.bfloat16)
    attn_float = lax.optimization_barrier(attn_out).astype(jnp.float32)
    row_delta = lax.optimization_barrier(jnp.sum(g_all * attn_float, axis=1))
    near_dprob = jnp.einsum('gqe,gke->gqk', g_near, v_near)
    near_grad = round_trip(near_prob * (near_dprob - row_delta.reshape(-1, SEG_A)[:, :, None]))
    far_grad = round_trip(far_prob * (jnp.dot(g_far, v_far.T) - pick_rows(row_delta, head_shift)[:, None]))
    d_query = place_rows(jnp.einsum('gqk,gke->gqe', near_grad, k_near).reshape(TILE_TOKENS, HEAD_SIZE), jnp.dot(far_grad, k_far), head_shift, add_terms) * inv_scale
    d_key = place_rows(jnp.einsum('gqk,gqe->gke', near_grad, q_near).reshape(TILE_TOKENS, HEAD_SIZE), jnp.dot(far_grad.T, q_far), head_shift, add_terms) * inv_scale
    d_value = place_rows(jnp.einsum('gqk,gqe->gke', near_round, g_near).reshape(TILE_TOKENS, HEAD_SIZE), jnp.dot(far_round.T, g_far), head_shift, add_terms)
    return (attn_out, d_query.astype(jnp.bfloat16), d_key.astype(jnp.bfloat16), d_value.astype(jnp.bfloat16))

def reference(queries, keys, values, slide_ids, head_shift_list, out_weight, d_y):
    plain_queries = to_plain(queries)
    plain_keys = to_plain(keys)
    plain_values = to_plain(values)
    d_attn = jnp.dot(d_y, out_weight.T, preferred_element_type=jnp.float32).astype(jnp.bfloat16)
    outcomes = []
    for head_idx in range(ATTENTION_HEADS):
        col_start = head_idx * HEAD_SIZE
        col_end = col_start + HEAD_SIZE
        outcomes.append(one_head(plain_queries[:, col_start:col_end], plain_keys[:, col_start:col_end], plain_values[:, col_start:col_end], d_attn[:, col_start:col_end], slide_ids, head_shift_list[head_idx]))
    attn_out = jnp.concatenate([outcome[0] for outcome in outcomes], axis=1)
    d_queries = from_plain(jnp.concatenate([outcome[1] for outcome in outcomes], axis=1))
    d_keys = from_plain(jnp.concatenate([outcome[2] for outcome in outcomes], axis=1))
    d_values = from_plain(jnp.concatenate([outcome[3] for outcome in outcomes], axis=1))
    layer_out = jnp.dot(attn_out, out_weight, preferred_element_type=jnp.float32).astype(jnp.bfloat16)
    d_weight = jnp.dot(attn_out.T, d_y, preferred_element_type=jnp.float32).astype(jnp.bfloat16)
    return (layer_out, d_queries, d_keys, d_values, d_weight)
```

```python
import functools
import math

import jax
import jax.numpy as jnp
from jax import lax
from jax.experimental import pallas as pl
from jax.experimental.pallas import tpu as pltpu
from jax.sharding import PartitionSpec as P

HEAD = 48
HALF = 64
RATE = 4
ROWS = 256
WIDTH = 768
NSEQ = 16
NHEAD = 8
SAME = 8192.0
SCALE = 1.0 / math.sqrt(HEAD)
EXP2 = SCALE * math.log2(math.e)
F32 = jnp.float32
BF16 = jnp.bfloat16


def nt(a, b):
    return lax.dot_general(a, b, (((1,), (1,)), ((), ())), preferred_element_type=F32)


def nn(a, b):
    return jnp.dot(a, b, preferred_element_type=F32)


def iota(shape, dim):
    return lax.broadcasted_iota(jnp.int32, shape, dim)


def remote(src, dst, send, recv, axis, index):
    return pltpu.make_async_remote_copy(
        src_ref=src,
        dst_ref=dst,
        send_sem=send,
        recv_sem=recv,
        device_id={axis: index},
        device_id_type=pl.DeviceIdType.MESH,
    )


def kernel(
    q_ref,
    k_ref,
    v_ref,
    id_ref,
    shift_ref,
    w_ref,
    dy_ref,
    lo_ref,
    dq_ref,
    dk_ref,
    dv_ref,
    dw_ref,
    perm,
    near_k,
    near_v,
    kv,
    q_t,
    q_n,
    qf_t,
    qf_n,
    g_t,
    g_n,
    gf_t,
    gf_n,
    e_near,
    e_far,
    top_n,
    sum_n,
    out_n,
    top_f,
    sum_f,
    out_f,
    fac_n,
    fac_f,
    delta_n,
    delta_f,
    attn_t,
    attn_n,
    attn_r,
    dys,
    ws,
    dwp,
    dwr,
    dws,
    dwf,
    gkv_s,
    gkv_r,
    acc_k,
    acc_v,
    acc_q,
    acc_qf,
    kv_send,
    kv_recv,
    dy_send,
    dy_recv,
    w_send,
    w_recv,
    at_send,
    at_recv,
    dw_send,
    dw_recv,
    df_send,
    df_recv,
    g_send,
    g_recv,
):
    seq = lax.axis_index("seq")
    head = lax.axis_index("head")

    def peer_s(i):
        return lax.rem(seq + i, NSEQ)

    def peer_h(i):
        return lax.rem(head + i, NHEAD)

    barrier = pltpu.get_barrier_semaphore()

    @pl.loop(1, NSEQ)
    def _(i):
        pl.semaphore_signal(
            barrier, inc=1, device_id={"seq": peer_s(i)}, device_id_type=pl.DeviceIdType.MESH
        )

    @pl.loop(1, NHEAD)
    def _(i):
        pl.semaphore_signal(
            barrier, inc=1, device_id={"head": peer_h(i)}, device_id_type=pl.DeviceIdType.MESH
        )

    row = iota((4 * 128, 384), 0)
    col = iota((4 * 128, 384), 1)
    lane = lax.rem(row, 128)
    within = lax.rem(lane, HALF)
    source = (lane // HALF) * (RATE * HEAD) + (row // 128) * HEAD + within
    perm[...] = jnp.where((within < HEAD) & (source == col), 1.0, 0.0).astype(BF16)

    slide_col = lax.rem(iota((128, 128), 0), HALF) - HEAD
    below = jnp.zeros((128, 128), F32)
    upto = jnp.zeros((128, 128), F32)
    for s in range(8):
        ids = id_ref[s : s + 1, :]
        below = below + jnp.where(ids < slide_col, 1.0, 0.0)
        upto = upto + jnp.where(ids <= slide_col, 1.0, 0.0)
    ones = jnp.ones((8, 128), BF16)
    first_row = nt(ones, below.astype(BF16))[0:1, :]
    last_row = nt(ones, upto.astype(BF16))[0:1, :]
    first_col = jnp.sum(below, axis=1, keepdims=True)
    last_col = jnp.sum(upto, axis=1, keepdims=True)

    shift0 = shift_ref[2 * head]
    shift1 = shift_ref[2 * head + 1]
    lane_row = iota((1, 128), 1)
    lane_col = iota((128, 1), 0)
    shift_row = jnp.where(lane_row < HALF, shift0, shift1)
    shift_col = jnp.where(lane_col < HALF, shift0, shift1)
    hot_row = lax.rem(lane_row, HALF) >= HEAD
    hot_col = lax.rem(lane_col, HALF) >= HEAD
    shift_q = [jnp.full((1, ROWS), shift0, jnp.int32), jnp.full((1, ROWS), shift1, jnp.int32)]

    k_p = nt(k_ref[...], perm[...])
    v_p = nt(v_ref[...], perm[...])
    far_k = jnp.zeros((ROWS, 128), F32)
    far_v = jnp.zeros((ROWS, 128), F32)
    for r in range(RATE):
        at = (iota((ROWS, 128), 0) * RATE + r).astype(F32)
        hot = jnp.where(hot_row & (at >= first_row) & (at < last_row), 1.0, 0.0)
        k_r = k_p[:, r * 128 : (r + 1) * 128] + hot
        v_r = v_p[:, r * 128 : (r + 1) * 128]
        near_k[r] = k_r.astype(BF16)
        near_v[r] = v_r.astype(BF16)
        far_k = jnp.where(shift_row == r, k_r, far_k)
        far_v = jnp.where(shift_row == r, v_r, far_v)
    kv[seq, 0] = far_k.astype(BF16)
    kv[seq, 1] = far_v.astype(BF16)

    rm_row = iota((128, 128), 0)
    rm_col = iota((128, 128), 1)
    to_rm = jnp.where(rm_col == lax.rem(rm_row, 32) * RATE + rm_row // 32, 1.0, 0.0).astype(BF16)
    dy_own = nn(to_rm, dy_ref[...]).astype(BF16)
    own_rows = pl.ds(pl.multiple_of(head * 32, 32), 32)
    for r in range(RATE):
        dys[r, own_rows, :] = dy_own[r * 32 : (r + 1) * 32]

    zeros16 = jnp.zeros((16, WIDTH), BF16)

    ws[head, 0:48] = w_ref[0:48]
    ws[head, 48:64] = zeros16
    ws[head, 64:112] = w_ref[48:96]
    for h in range(NHEAD):
        ws[h, 112:128] = zeros16

    pl.semaphore_wait(barrier, NSEQ - 1 + NHEAD - 1)

    def kv_copy(slot, i):
        return remote(kv.at[slot], kv.at[slot], kv_send.at[i], kv_recv.at[slot], "seq", peer_s(i))

    def dy_copy(owner, i):
        rows = pl.ds(pl.multiple_of(owner * 32, 32), 32)
        part = dys.at[:, rows, :]
        return remote(part, part, dy_send.at[i], dy_recv.at[owner], "head", peer_h(i))

    def w_copy(owner, i):
        part = ws.at[owner, 0:112]
        return remote(part, part, w_send.at[i], w_recv.at[owner], "head", peer_h(i))

    @pl.loop(1, NSEQ)
    def _(i):
        kv_copy(seq, i).start()

    @pl.loop(1, NHEAD)
    def _(i):
        dy_copy(head, i).start()

    @pl.loop(1, NHEAD)
    def _(i):
        w_copy(head, i).start()

    q_p = nt(q_ref[...], perm[...])
    q_pt = nt(perm[...], q_ref[...])
    far_q = jnp.zeros((ROWS, 128), F32)
    far_qt = jnp.zeros((128, ROWS), F32)
    for r in range(RATE):
        at = (iota((128, ROWS), 1) * RATE + r).astype(F32)
        hot = jnp.where(hot_col & (at >= first_col) & (at < last_col), SAME, 0.0)
        q_r = q_p[:, r * 128 : (r + 1) * 128]
        q_rt = q_pt[r * 128 : (r + 1) * 128, :] + hot
        q_n[0, r] = jnp.where(lane_row < HALF, q_r, 0.0).astype(BF16)
        q_n[1, r] = jnp.where(lane_row < HALF, 0.0, q_r).astype(BF16)
        q_t[0, r] = jnp.where(lane_col < HALF, q_rt, 0.0).astype(BF16)
        q_t[1, r] = jnp.where(lane_col < HALF, 0.0, q_rt).astype(BF16)
        far_q = jnp.where(shift_row == r, q_r, far_q)
        far_qt = jnp.where(shift_col == r, q_rt, far_qt)
    qf_n[0] = jnp.where(lane_row < HALF, far_q, 0.0).astype(BF16)
    qf_n[1] = jnp.where(lane_row < HALF, 0.0, far_q).astype(BF16)
    qf_t[0] = jnp.where(lane_col < HALF, far_qt, 0.0).astype(BF16)
    qf_t[1] = jnp.where(lane_col < HALF, 0.0, far_qt).astype(BF16)

    def forward(keys, vals, q_of, e_of, h):
        top = None
        for b in range(4):
            s = nn(keys(b), q_of)
            e_of[b] = s
            m = jnp.max(s, axis=0, keepdims=True)
            top = m if top is None else jnp.maximum(top, m)
        total = jnp.zeros((1, ROWS), F32)
        out = jnp.zeros((HALF, ROWS), F32)
        for b in range(4):
            e = jnp.exp2((e_of[b] - top) * EXP2)
            e_of[b] = e
            total = total + jnp.sum(e, axis=0, keepdims=True)
            v_t = vals(b).T[h * HALF : (h + 1) * HALF]
            out = out + nn(v_t, e.astype(BF16))
        return top, total, out

    @pl.loop(0, RATE)
    def _(r):
        for h in range(2):
            top, total, out = forward(
                lambda b: near_k[b], lambda b: near_v[b], q_t[h, r], e_near.at[h, r], h
            )
            top_n[h, r] = top
            sum_n[h, r] = total
            out_n[h, r] = out

    group = seq // 4

    @pl.loop(0, 4)
    def _(i):
        g = lax.rem(group + i, 4)
        for b in range(4):

            @pl.when(g * 4 + b != seq)
            def _():
                kv_copy(g * 4 + b, 1).wait_recv()

        for h in range(2):
            top, total, out = forward(
                lambda b: kv[g * 4 + b, 0], lambda b: kv[g * 4 + b, 1], qf_t[h], e_far.at[h, g], h
            )
            top_f[h, g] = top
            sum_f[h, g] = total
            out_f[h, g] = out

    for h in range(2):
        half = slice(h * HALF, (h + 1) * HALF)
        far_top = top_f[h, 0]
        for g in range(1, 4):
            far_top = jnp.maximum(far_top, top_f[h, g])
        sel_top = top_n[h, 0]
        for r in range(1, RATE):
            sel_top = jnp.where(shift_q[h] == r, top_n[h, r], sel_top)
        sel_top = jnp.maximum(sel_top, far_top)
        far_total = jnp.zeros((1, ROWS), F32)
        far_out = jnp.zeros((HALF, ROWS), F32)
        weights = []
        for g in range(4):
            weight = jnp.exp2((top_f[h, g] - sel_top) * EXP2)
            weights.append(weight)
            far_total = far_total + weight * sum_f[h, g]
            far_out = far_out + weight * out_f[h, g]
        far_inv = jnp.zeros((1, ROWS), F32)
        for r in range(RATE):
            mine = shift_q[h] == r
            top = jnp.where(mine, sel_top, top_n[h, r])
            weight = jnp.exp2((top_n[h, r] - top) * EXP2)
            total = weight * sum_n[h, r] + jnp.where(mine, far_total, 0.0)
            inverse = 1.0 / total
            fac_n[h, r] = weight * inverse
            far_inv = jnp.where(mine, inverse, far_inv)
            out = weight * out_n[h, r] + jnp.where(mine, far_out, 0.0)
            attn_t[r, half] = (out * inverse).astype(BF16)
        for g in range(4):
            fac_f[h, g] = weights[g] * far_inv

    for r in range(RATE):
        attn_n[r] = attn_t[r].astype(F32).T.astype(BF16)

    def at_copy(slot, i):
        rows = pl.ds(pl.multiple_of(peer_h(i) * 32, 32), 32)
        return remote(
            attn_n.at[:, rows, :], attn_r.at[slot], at_send.at[i], at_recv.at[slot], "head", peer_h(i)
        )

    @pl.loop(1, NHEAD)
    def _(i):
        at_copy(head, i).start()

    for r in range(RATE):
        attn_r[head, r] = attn_n[r, own_rows, :]

    @pl.loop(1, NHEAD)
    def _(i):
        dy_copy(peer_h(i), i).wait_recv()

    w_own = ws[head]
    far_g = jnp.zeros((ROWS, 128), F32)
    far_gt = jnp.zeros((128, ROWS), F32)
    weight_grad = jnp.zeros((128, WIDTH), F32)
    far_d = [jnp.zeros((1, ROWS), F32), jnp.zeros((1, ROWS), F32)]
    for r in range(RATE):
        g_r = nt(dys[r], w_own)
        g_rt = nt(w_own, dys[r])
        weight_grad = weight_grad + nn(attn_t[r], dys[r])
        g_n[0, r] = jnp.where(lane_row < HALF, g_r, 0.0).astype(BF16)
        g_n[1, r] = jnp.where(lane_row < HALF, 0.0, g_r).astype(BF16)
        g_t[0, r] = jnp.where(lane_col < HALF, g_rt, 0.0).astype(BF16)
        g_t[1, r] = jnp.where(lane_col < HALF, 0.0, g_rt).astype(BF16)
        far_g = jnp.where(shift_row == r, g_r, far_g)
        far_gt = jnp.where(shift_col == r, g_rt, far_gt)
        product = g_rt.astype(BF16).astype(F32) * attn_t[r].astype(F32)
        for h in range(2):
            half = slice(h * HALF, (h + 1) * HALF)
            d = jnp.sum(product[half], axis=0, keepdims=True)
            delta_n[h, r] = d
            far_d[h] = jnp.where(shift_q[h] == r, d, far_d[h])
    gf_n[0] = jnp.where(lane_row < HALF, far_g, 0.0).astype(BF16)
    gf_n[1] = jnp.where(lane_row < HALF, 0.0, far_g).astype(BF16)
    gf_t[0] = jnp.where(lane_col < HALF, far_gt, 0.0).astype(BF16)
    gf_t[1] = jnp.where(lane_col < HALF, 0.0, far_gt).astype(BF16)
    delta_f[0] = far_d[0]
    delta_f[1] = far_d[1]

    for j in range(NSEQ):
        dwp[j] = weight_grad[j * 8 : (j + 1) * 8]
    dwr[seq] = dwp[seq]

    def dw_copy(slot, i):
        return remote(
            dwp.at[peer_s(i)], dwr.at[slot], dw_send.at[i], dw_recv.at[slot], "seq", peer_s(i)
        )

    @pl.loop(1, NSEQ)
    def _(i):
        dw_copy(seq, i).start()

    def backward(keys, vals, g_tr, g_na, q_na, e_of, factor, delta, put):
        dq = [jnp.zeros((HALF, ROWS), F32), jnp.zeros((HALF, ROWS), F32)]
        for b in range(4):
            k_t = keys(b).T
            val = vals(b)
            dk = jnp.zeros((ROWS, 128), F32)
            dv = jnp.zeros((ROWS, 128), F32)
            for h in range(2):
                p = e_of(h)[b] * factor(h)
                ds = (p * (nn(val, g_tr(h)) - delta(h))).astype(BF16)
                dv = dv + nn(p.astype(BF16), g_na(h))
                dk = dk + nn(ds, q_na(h))
                dq[h] = dq[h] + nn(k_t[h * HALF : (h + 1) * HALF], ds)
            put(b, dk, dv)
        return dq

    def grad_copy(slot, dst):
        return remote(
            gkv_s.at[dst], gkv_r.at[slot], g_send.at[dst], g_recv.at[slot], "seq", dst
        )

    acc_qf[...] = jnp.zeros((128, ROWS), F32)

    @pl.loop(0, 4)
    def _(i):
        g = lax.rem(group + 1 + i, 4)

        def put(b, dk, dv):
            dst = g * 4 + b
            gkv_s[dst, 0] = dk.astype(BF16)
            gkv_s[dst, 1] = dv.astype(BF16)

            @pl.when(dst != seq)
            def _():
                grad_copy(seq, dst).start()

        dq = backward(
            lambda b: kv[g * 4 + b, 0],
            lambda b: kv[g * 4 + b, 1],
            lambda h: gf_t[h],
            lambda h: gf_n[h],
            lambda h: qf_n[h],
            lambda h: e_far.at[h, g],
            lambda h: fac_f[h, g],
            lambda h: delta_f[h],
            put,
        )
        for h in range(2):
            half = slice(h * HALF, (h + 1) * HALF)
            acc_qf[half] = acc_qf[half] + dq[h]

    @pl.loop(1, NSEQ)
    def _(i):
        dw_copy(peer_s(i), i).wait_recv()

    part = dwr[0]
    for j in range(1, NSEQ):
        part = part + dwr[j]
    dws[...] = part
    dwf[seq] = part

    def df_copy(slot, i):
        return remote(dws, dwf.at[slot], df_send.at[i], df_recv.at[slot], "seq", peer_s(i))

    @pl.loop(1, NSEQ)
    def _(i):
        df_copy(seq, i).start()

    acc_k[...] = jnp.zeros((4, ROWS, 128), F32)
    acc_v[...] = jnp.zeros((4, ROWS, 128), F32)

    @pl.loop(0, RATE)
    def _(r):
        def put(b, dk, dv):
            acc_k[b] = acc_k[b] + dk
            acc_v[b] = acc_v[b] + dv

        dq = backward(
            lambda b: near_k[b],
            lambda b: near_v[b],
            lambda h: g_t[h, r],
            lambda h: g_n[h, r],
            lambda h: q_n[h, r],
            lambda h: e_near.at[h, r],
            lambda h: fac_n[h, r],
            lambda h: delta_n[h, r],
            put,
        )
        for h in range(2):
            acc_q[r, h * HALF : (h + 1) * HALF] = dq[h]

    dq_parts = []
    for r in range(RATE):
        dq_r = (acc_q[r] + jnp.where(shift_col == r, acc_qf[...], 0.0)) * SCALE
        dq_parts.append(dq_r.T.astype(BF16))
    dq_ref[...] = nn(jnp.concatenate(dq_parts, axis=1), perm[...]).astype(BF16)

    @pl.loop(1, NHEAD)
    def _(i):
        w_copy(peer_h(i), i).wait_recv()
        at_copy(peer_h(i), i).wait_recv()

    from_rm = jnp.where(rm_row == lax.rem(rm_col, 32) * RATE + rm_col // 32, 1.0, 0.0).astype(BF16)
    result = jnp.zeros((128, WIDTH), F32)
    for h in range(NHEAD):
        rows = nn(from_rm, attn_r[h].reshape(128, 128)).astype(BF16)
        result = result + nn(rows, ws[h])
    lo_ref[...] = result.astype(BF16)

    @pl.loop(1, NSEQ)
    def _(i):
        grad_copy(peer_s(i), peer_s(i)).wait_recv()

    gkv_r[seq] = gkv_s[seq]
    sum_k = gkv_r[0, 0].astype(F32)
    sum_v = gkv_r[0, 1].astype(F32)
    for j in range(1, NSEQ):
        sum_k = sum_k + gkv_r[j, 0].astype(F32)
        sum_v = sum_v + gkv_r[j, 1].astype(F32)
    dk_parts = []
    dv_parts = []
    for r in range(RATE):
        mine = shift_row == r
        dk_parts.append(((acc_k[r] + jnp.where(mine, sum_k, 0.0)) * SCALE).astype(BF16))
        dv_parts.append((acc_v[r] + jnp.where(mine, sum_v, 0.0)).astype(BF16))
    dk_ref[...] = nn(jnp.concatenate(dk_parts, axis=1), perm[...]).astype(BF16)
    dv_ref[...] = nn(jnp.concatenate(dv_parts, axis=1), perm[...]).astype(BF16)

    @pl.loop(1, NSEQ)
    def _(i):
        df_copy(peer_s(i), i).wait_recv()

    whole = dwf[...].reshape(128, WIDTH)
    dw_ref[0:48] = whole[0:48].astype(BF16)
    dw_ref[48:96] = whole[64:112].astype(BF16)

    @pl.loop(1, NSEQ)
    def _(i):
        kv_copy(seq, i).wait_send()
        dw_copy(seq, i).wait_send()
        df_copy(seq, i).wait_send()
        grad_copy(seq, peer_s(i)).wait_send()

    @pl.loop(1, NHEAD)
    def _(i):
        dy_copy(head, i).wait_send()
        w_copy(head, i).wait_send()
        at_copy(head, i).wait_send()


def body(queries, keys, values, slide_ids, head_shift_list, out_weight, d_y):
    vmem = pl.BlockSpec(memory_space=pltpu.VMEM)
    smem = pl.BlockSpec(memory_space=pltpu.SMEM)
    sems = pltpu.SemaphoreType.DMA
    return pl.pallas_call(
        kernel,
        out_shape=(
            jax.ShapeDtypeStruct((128, WIDTH), BF16),
            jax.ShapeDtypeStruct((ROWS, 384), BF16),
            jax.ShapeDtypeStruct((ROWS, 384), BF16),
            jax.ShapeDtypeStruct((ROWS, 384), BF16),
            jax.ShapeDtypeStruct((96, WIDTH), BF16),
        ),
        in_specs=[vmem, vmem, vmem, vmem, smem, vmem, vmem],
        out_specs=(vmem,) * 5,
        scratch_shapes=[
            pltpu.VMEM((4 * 128, 384), BF16),
            pltpu.VMEM((4, ROWS, 128), BF16),
            pltpu.VMEM((4, ROWS, 128), BF16),
            pltpu.VMEM((NSEQ, 2, ROWS, 128), BF16),
            pltpu.VMEM((2, RATE, 128, ROWS), BF16),
            pltpu.VMEM((2, RATE, ROWS, 128), BF16),
            pltpu.VMEM((2, 128, ROWS), BF16),
            pltpu.VMEM((2, ROWS, 128), BF16),
            pltpu.VMEM((2, RATE, 128, ROWS), BF16),
            pltpu.VMEM((2, RATE, ROWS, 128), BF16),
            pltpu.VMEM((2, 128, ROWS), BF16),
            pltpu.VMEM((2, ROWS, 128), BF16),
            pltpu.VMEM((2, RATE, 4, ROWS, ROWS), F32),
            pltpu.VMEM((2, 4, 4, ROWS, ROWS), F32),
            pltpu.VMEM((2, RATE, 1, ROWS), F32),
            pltpu.VMEM((2, RATE, 1, ROWS), F32),
            pltpu.VMEM((2, RATE, HALF, ROWS), F32),
            pltpu.VMEM((2, 4, 1, ROWS), F32),
            pltpu.VMEM((2, 4, 1, ROWS), F32),
            pltpu.VMEM((2, 4, HALF, ROWS), F32),
            pltpu.VMEM((2, RATE, 1, ROWS), F32),
            pltpu.VMEM((2, 4, 1, ROWS), F32),
            pltpu.VMEM((2, RATE, 1, ROWS), F32),
            pltpu.VMEM((2, 1, ROWS), F32),
            pltpu.VMEM((RATE, 128, ROWS), BF16),
            pltpu.VMEM((RATE, ROWS, 128), BF16),
            pltpu.VMEM((NHEAD, RATE, 32, 128), BF16),
            pltpu.VMEM((RATE, ROWS, WIDTH), BF16),
            pltpu.VMEM((NHEAD, 128, WIDTH), BF16),
            pltpu.VMEM((NSEQ, 8, WIDTH), F32),
            pltpu.VMEM((NSEQ, 8, WIDTH), F32),
            pltpu.VMEM((8, WIDTH), F32),
            pltpu.VMEM((NSEQ, 8, WIDTH), F32),
            pltpu.VMEM((NSEQ, 2, ROWS, 128), BF16),
            pltpu.VMEM((NSEQ, 2, ROWS, 128), BF16),
            pltpu.VMEM((4, ROWS, 128), F32),
            pltpu.VMEM((4, ROWS, 128), F32),
            pltpu.VMEM((RATE, 128, ROWS), F32),
            pltpu.VMEM((128, ROWS), F32),
            sems((NSEQ,)),
            sems((NSEQ,)),
            sems((NHEAD,)),
            sems((NHEAD,)),
            sems((NHEAD,)),
            sems((NHEAD,)),
            sems((NHEAD,)),
            sems((NHEAD,)),
            sems((NSEQ,)),
            sems((NSEQ,)),
            sems((NSEQ,)),
            sems((NSEQ,)),
            sems((NSEQ,)),
            sems((NSEQ,)),
        ],
        compiler_params=pltpu.CompilerParams(
            collective_id=0, has_side_effects=True, vmem_limit_bytes=56 * 1024 * 1024
        ),
        cost_estimate=pl.CostEstimate(
            flops=3_000_000_000, bytes_accessed=4_000_000, transcendentals=5_000_000
        ),
    )(
        queries,
        keys,
        values,
        slide_ids.reshape(8, 128),
        head_shift_list,
        out_weight,
        d_y,
    )


def solution(mesh):
    placed = (
        P("seq", "head"),
        P("seq", "head"),
        P("seq", "head"),
        P("seq"),
        P(),
        P("head", None),
        P(("seq", "head"), None),
    )
    return jax.shard_map(
        body,
        mesh=mesh,
        in_specs=placed,
        out_specs=(
            P(("seq", "head"), None),
            P("seq", "head"),
            P("seq", "head"),
            P("seq", "head"),
            P("head", None),
        ),
        check_vma=False,
    )
```

```python
import functools
import math

import jax
import jax.numpy as jnp
from jax import lax
from jax.experimental import pallas as pl
from jax.experimental.pallas import tpu as pltpu
from jax.sharding import PartitionSpec as P

HEAD = 48
HALF = 64
RATE = 4
ROWS = 256
WIDTH = 768
NSEQ = 16
NHEAD = 8
SAME = 8192.0
SCALE = 1.0 / math.sqrt(HEAD)
EXP2 = SCALE * math.log2(math.e)
F32 = jnp.float32
BF16 = jnp.bfloat16


def nt(a, b):
    return lax.dot_general(a, b, (((1,), (1,)), ((), ())), preferred_element_type=F32)


def nn(a, b):
    return jnp.dot(a, b, preferred_element_type=F32)


def iota(shape, dim):
    return lax.broadcasted_iota(jnp.int32, shape, dim)


def remote(src, dst, send, recv, axis, index):
    return pltpu.make_async_remote_copy(
        src_ref=src,
        dst_ref=dst,
        send_sem=send,
        recv_sem=recv,
        device_id={axis: index},
        device_id_type=pl.DeviceIdType.MESH,
    )


def kernel(
    q_ref,
    k_ref,
    v_ref,
    id_ref,
    shift_ref,
    w_ref,
    dy_ref,
    lo_ref,
    dq_ref,
    dk_ref,
    dv_ref,
    dw_ref,
    perm,
    near_k,
    near_v,
    kv,
    q_t,
    q_n,
    qf_t,
    qf_n,
    g_t,
    g_n,
    gf_t,
    gf_n,
    e_near,
    e_far,
    top_n,
    sum_n,
    out_n,
    top_f,
    sum_f,
    out_f,
    fac_n,
    fac_f,
    delta_n,
    delta_f,
    attn_t,
    attn_n,
    attn_r,
    dys,
    ws,
    dwp,
    dwx,
    dwm,
    dwr,
    dwf,
    gkv_s,
    gkv_x,
    gkv_r,
    acc_k,
    acc_v,
    acc_q,
    acc_qf,
    kv_send,
    kv_recv,
    dy_send,
    dy_recv,
    w_send,
    w_recv,
    ws_send,
    ws_recv,
    at_send,
    at_recv,
    dx_sem,
    dw_send,
    dw_recv,
    df_send,
    df_recv,
    dc_sem,
    gx_send,
    gx_recv,
    g_send,
    g_recv,
):
    seq = lax.axis_index("seq")
    head = lax.axis_index("head")

    x_lo, z, core = seq // 8, lax.rem(seq // 2, 4), lax.rem(seq, 2)
    x_hi, y = head // 4, lax.rem(head, 4)
    chip = seq // 2

    def at_chip(j):
        return j * 2 + core

    def in_seq(x, dz, c):
        return x * 8 + lax.rem(z + dz, 4) * 2 + c

    def in_head(x, dy):
        return x * 4 + lax.rem(y + dy, 4)

    def peer_c(i):
        return lax.rem(chip + i, 8)

    def peer_h(i):
        return lax.rem(head + i, NHEAD)

    sibling = in_seq(x_lo, 0, 1 - core)
    partner = in_seq(1 - x_lo, 0, core)
    partner_h = in_head(1 - x_hi, 0)
    turns = (1, 3, 2)

    barrier = pltpu.get_barrier_semaphore()
    pl.semaphore_signal(
        barrier, inc=1, device_id={"seq": sibling}, device_id_type=pl.DeviceIdType.MESH
    )

    @pl.loop(1, 8)
    def _(i):
        pl.semaphore_signal(
            barrier,
            inc=1,
            device_id={"seq": at_chip(peer_c(i))},
            device_id_type=pl.DeviceIdType.MESH,
        )
        pl.semaphore_signal(
            barrier, inc=1, device_id={"head": peer_h(i)}, device_id_type=pl.DeviceIdType.MESH
        )

    row = iota((4 * 128, 384), 0)
    col = iota((4 * 128, 384), 1)
    lane = lax.rem(row, 128)
    within = lax.rem(lane, HALF)
    source = (lane // HALF) * (RATE * HEAD) + (row // 128) * HEAD + within
    perm[...] = jnp.where((within < HEAD) & (source == col), 1.0, 0.0).astype(BF16)

    slide_col = lax.rem(iota((128, 128), 0), HALF) - HEAD
    below = jnp.zeros((128, 128), F32)
    upto = jnp.zeros((128, 128), F32)
    for s in range(8):
        ids = id_ref[s : s + 1, :]
        below = below + jnp.where(ids < slide_col, 1.0, 0.0)
        upto = upto + jnp.where(ids <= slide_col, 1.0, 0.0)
    ones = jnp.ones((8, 128), BF16)
    first_row = nt(ones, below.astype(BF16))[0:1, :]
    last_row = nt(ones, upto.astype(BF16))[0:1, :]
    first_col = jnp.sum(below, axis=1, keepdims=True)
    last_col = jnp.sum(upto, axis=1, keepdims=True)

    shift0 = shift_ref[2 * head]
    shift1 = shift_ref[2 * head + 1]
    lane_row = iota((1, 128), 1)
    lane_col = iota((128, 1), 0)
    shift_row = jnp.where(lane_row < HALF, shift0, shift1)
    shift_col = jnp.where(lane_col < HALF, shift0, shift1)
    hot_row = lax.rem(lane_row, HALF) >= HEAD
    hot_col = lax.rem(lane_col, HALF) >= HEAD
    shift_q = [jnp.full((1, ROWS), shift0, jnp.int32), jnp.full((1, ROWS), shift1, jnp.int32)]

    k_p = nt(k_ref[...], perm[...])
    v_p = nt(v_ref[...], perm[...])
    far_k = jnp.zeros((ROWS, 128), F32)
    far_v = jnp.zeros((ROWS, 128), F32)
    for r in range(RATE):
        at = (iota((ROWS, 128), 0) * RATE + r).astype(F32)
        hot = jnp.where(hot_row & (at >= first_row) & (at < last_row), 1.0, 0.0)
        k_r = k_p[:, r * 128 : (r + 1) * 128] + hot
        v_r = v_p[:, r * 128 : (r + 1) * 128]
        near_k[r] = k_r.astype(BF16)
        near_v[r] = v_r.astype(BF16)
        far_k = jnp.where(shift_row == r, k_r, far_k)
        far_v = jnp.where(shift_row == r, v_r, far_v)
    kv[seq, 0] = far_k.astype(BF16)
    kv[seq, 1] = far_v.astype(BF16)

    rm_row = iota((128, 128), 0)
    rm_col = iota((128, 128), 1)
    to_rm = jnp.where(rm_col == lax.rem(rm_row, 32) * RATE + rm_row // 32, 1.0, 0.0).astype(BF16)
    dy_own = nn(to_rm, dy_ref[...]).astype(BF16)
    own_rows = pl.ds(pl.multiple_of(head * 32, 32), 32)
    for r in range(RATE):
        dys[r, own_rows, :] = dy_own[r * 32 : (r + 1) * 32]

    zeros16 = jnp.zeros((16, WIDTH), BF16)

    ws[head, 0:48] = w_ref[0:48]
    ws[head, 64:112] = w_ref[48:96]
    for h in range(NHEAD):
        ws[h, 48:64] = zeros16
        ws[h, 112:128] = zeros16

    pl.semaphore_wait(barrier, 15)

    def kv_copy(slot, i, dst):
        return remote(kv.at[slot], kv.at[slot], kv_send.at[i], kv_recv.at[slot], "seq", dst)

    def dy_copy(owner, i, dst):
        rows = pl.ds(pl.multiple_of(owner * 32, 32), 32)
        part = dys.at[:, rows, :]
        return remote(part, part, dy_send.at[i], dy_recv.at[owner], "head", dst)

    def w_copy(owner, i):
        part = ws.at[owner, pl.ds(pl.multiple_of(core * HALF, HALF), HEAD)]
        return remote(part, part, w_send.at[i], w_recv.at[owner], "head", peer_h(i))

    def w_share(owner, half):
        part = ws.at[owner, pl.ds(pl.multiple_of(half * HALF, HALF), HEAD)]
        return remote(part, part, ws_send.at[owner], ws_recv.at[owner], "seq", sibling)

    kv_copy(seq, 0, partner).start()
    for j, turn in enumerate(turns):
        kv_copy(seq, 1 + j, in_seq(x_lo, turn, core)).start()
    kv_copy(seq, 4, sibling).start()
    dy_copy(head, 0, partner_h).start()
    for j, turn in enumerate(turns):
        dy_copy(head, 1 + j, in_head(x_hi, turn)).start()

    q_p = nt(q_ref[...], perm[...])
    q_pt = nt(perm[...], q_ref[...])
    far_q = jnp.zeros((ROWS, 128), F32)
    far_qt = jnp.zeros((128, ROWS), F32)
    for r in range(RATE):
        at = (iota((128, ROWS), 1) * RATE + r).astype(F32)
        hot = jnp.where(hot_col & (at >= first_col) & (at < last_col), SAME, 0.0)
        q_r = q_p[:, r * 128 : (r + 1) * 128]
        q_rt = q_pt[r * 128 : (r + 1) * 128, :] + hot
        q_n[0, r] = jnp.where(lane_row < HALF, q_r, 0.0).astype(BF16)
        q_n[1, r] = jnp.where(lane_row < HALF, 0.0, q_r).astype(BF16)
        q_t[0, r] = jnp.where(lane_col < HALF, q_rt, 0.0).astype(BF16)
        q_t[1, r] = jnp.where(lane_col < HALF, 0.0, q_rt).astype(BF16)
        far_q = jnp.where(shift_row == r, q_r, far_q)
        far_qt = jnp.where(shift_col == r, q_rt, far_qt)
    qf_n[0] = jnp.where(lane_row < HALF, far_q, 0.0).astype(BF16)
    qf_n[1] = jnp.where(lane_row < HALF, 0.0, far_q).astype(BF16)
    qf_t[0] = jnp.where(lane_col < HALF, far_qt, 0.0).astype(BF16)
    qf_t[1] = jnp.where(lane_col < HALF, 0.0, far_qt).astype(BF16)

    def forward(keys, vals, q_of, e_of, h):
        top = None
        for b in range(4):
            s = nn(keys(b), q_of)
            e_of[b] = s
            m = jnp.max(s, axis=0, keepdims=True)
            top = m if top is None else jnp.maximum(top, m)
        total = jnp.zeros((1, ROWS), F32)
        out = jnp.zeros((HALF, ROWS), F32)
        for b in range(4):
            e = jnp.exp2((e_of[b] - top) * EXP2)
            e_of[b] = e
            total = total + jnp.sum(e, axis=0, keepdims=True)
            v_t = vals(b).T[h * HALF : (h + 1) * HALF]
            out = out + nn(v_t, e.astype(BF16))
        return top, total, out

    @pl.loop(0, RATE)
    def _(r):
        for h in range(2):
            top, total, out = forward(
                lambda b: near_k[b], lambda b: near_v[b], q_t[h, r], e_near.at[h, r], h
            )
            top_n[h, r] = top
            sum_n[h, r] = total
            out_n[h, r] = out

        @pl.when(r == 0)
        def _():
            kv_copy(partner, 0, partner).wait_recv()
            for j, turn in enumerate(turns):
                kv_copy(partner, 5 + j, in_seq(x_lo, turn, core)).start()
            kv_copy(partner, 8, sibling).start()

        @pl.when(r == 1)
        def _():
            dy_copy(partner_h, 0, partner_h).wait_recv()
            for j, turn in enumerate(turns):
                dy_copy(partner_h, 4 + j, in_head(x_hi, turn)).start()

    def share(i):
        dz = i + i // 2 - 2 * (i // 3)
        for x in range(2):
            slot = in_seq(x, dz, core)
            kv_copy(slot, 0, partner).wait_recv()
            kv_copy(slot, 9 + 2 * (i - 1) + x, sibling).start()

    def w_start():
        @pl.loop(1, NHEAD)
        def _(i):
            w_copy(head, i).start()

    @pl.loop(0, 4)
    def _(i):
        dz = i + i // 2 - 2 * (i // 3)

        @pl.when(i == 1)
        def _():
            share(1)
            w_start()

        @pl.when((i == 1) | (i == 2))
        def _():
            share(i + 1)

        for x in range(2):
            kv_copy(in_seq(x, dz, 1 - core), 0, partner).wait_recv()

        for h in range(2):
            top, total, out = forward(
                lambda b: kv[in_seq(b // 2, dz, b % 2), 0],
                lambda b: kv[in_seq(b // 2, dz, b % 2), 1],
                qf_t[h],
                e_far.at[h, i],
                h,
            )
            top_f[h, i] = top
            sum_f[h, i] = total
            out_f[h, i] = out

    for h in range(2):
        half = slice(h * HALF, (h + 1) * HALF)
        far_top = top_f[h, 0]
        for g in range(1, 4):
            far_top = jnp.maximum(far_top, top_f[h, g])
        sel_top = top_n[h, 0]
        for r in range(1, RATE):
            sel_top = jnp.where(shift_q[h] == r, top_n[h, r], sel_top)
        sel_top = jnp.maximum(sel_top, far_top)
        far_total = jnp.zeros((1, ROWS), F32)
        far_out = jnp.zeros((HALF, ROWS), F32)
        weights = []
        for g in range(4):
            weight = jnp.exp2((top_f[h, g] - sel_top) * EXP2)
            weights.append(weight)
            far_total = far_total + weight * sum_f[h, g]
            far_out = far_out + weight * out_f[h, g]
        far_inv = jnp.zeros((1, ROWS), F32)
        for r in range(RATE):
            mine = shift_q[h] == r
            top = jnp.where(mine, sel_top, top_n[h, r])
            weight = jnp.exp2((top_n[h, r] - top) * EXP2)
            total = weight * sum_n[h, r] + jnp.where(mine, far_total, 0.0)
            inverse = 1.0 / total
            fac_n[h, r] = weight * inverse
            far_inv = jnp.where(mine, inverse, far_inv)
            out = weight * out_n[h, r] + jnp.where(mine, far_out, 0.0)
            attn_t[r, half] = (out * inverse).astype(BF16)
        for g in range(4):
            fac_f[h, g] = weights[g] * far_inv

    for r in range(RATE):
        attn_n[r] = attn_t[r].astype(F32).T.astype(BF16)

    def at_copy(slot, i):
        rows = pl.ds(pl.multiple_of(peer_h(i) * 32, 32), 32)
        return remote(
            attn_n.at[:, rows, :], attn_r.at[slot], at_send.at[i], at_recv.at[slot], "head", peer_h(i)
        )

    @pl.loop(1, NHEAD)
    def _(i):
        at_copy(head, i).start()

    for r in range(RATE):
        attn_r[head, r] = attn_n[r, own_rows, :]

    for turn in turns:
        for x in range(2):
            dy_copy(in_head(x, turn), 0, partner_h).wait_recv()

    w_own = ws[head]
    far_g = jnp.zeros((ROWS, 128), F32)
    far_gt = jnp.zeros((128, ROWS), F32)
    weight_grad = jnp.zeros((128, WIDTH), F32)
    far_d = [jnp.zeros((1, ROWS), F32), jnp.zeros((1, ROWS), F32)]
    for r in range(RATE):
        g_r = nt(dys[r], w_own)
        g_rt = nt(w_own, dys[r])
        weight_grad = weight_grad + nn(attn_t[r], dys[r])
        g_n[0, r] = jnp.where(lane_row < HALF, g_r, 0.0).astype(BF16)
        g_n[1, r] = jnp.where(lane_row < HALF, 0.0, g_r).astype(BF16)
        g_t[0, r] = jnp.where(lane_col < HALF, g_rt, 0.0).astype(BF16)
        g_t[1, r] = jnp.where(lane_col < HALF, 0.0, g_rt).astype(BF16)
        far_g = jnp.where(shift_row == r, g_r, far_g)
        far_gt = jnp.where(shift_col == r, g_rt, far_gt)
        product = g_rt.astype(BF16).astype(F32) * attn_t[r].astype(F32)
        for h in range(2):
            half = slice(h * HALF, (h + 1) * HALF)
            d = jnp.sum(product[half], axis=0, keepdims=True)
            delta_n[h, r] = d
            far_d[h] = jnp.where(shift_q[h] == r, d, far_d[h])
    gf_n[0] = jnp.where(lane_row < HALF, far_g, 0.0).astype(BF16)
    gf_n[1] = jnp.where(lane_row < HALF, 0.0, far_g).astype(BF16)
    gf_t[0] = jnp.where(lane_col < HALF, far_gt, 0.0).astype(BF16)
    gf_t[1] = jnp.where(lane_col < HALF, 0.0, far_gt).astype(BF16)
    delta_f[0] = far_d[0]
    delta_f[1] = far_d[1]

    for half in range(2):
        for j in range(8):
            dwp[half, j] = weight_grad[j * 16 : (j + 1) * 16, half * 384 : (half + 1) * 384]

    def dx_copy(half):
        return remote(dwp.at[half], dwx, dx_sem.at[0], dx_sem.at[1], "seq", sibling)

    def dw_copy(slot, i):
        dst = peer_c(i)
        return remote(dwm.at[dst], dwr.at[slot], dw_send.at[i], dw_recv.at[slot], "seq", at_chip(dst))

    def df_copy(slot, i):
        part = dwf.at[core, slot]
        return remote(part, part, df_send.at[i], df_recv.at[slot], "seq", at_chip(peer_c(i)))

    def dc_copy(half):
        return remote(dwf.at[half], dwf.at[half], dc_sem.at[0], dc_sem.at[1], "seq", sibling)

    dx_copy(1 - core).start()

    def backward(keys, vals, g_tr, g_na, q_na, e_of, factor, delta, put):
        dq = [jnp.zeros((HALF, ROWS), F32), jnp.zeros((HALF, ROWS), F32)]
        for b in range(4):
            k_t = keys(b).T
            val = vals(b)
            dk = jnp.zeros((ROWS, 128), F32)
            dv = jnp.zeros((ROWS, 128), F32)
            for h in range(2):
                p = e_of(h)[b] * factor(h)
                ds = (p * (nn(val, g_tr(h)) - delta(h))).astype(BF16)
                dv = dv + nn(p.astype(BF16), g_na(h))
                dk = dk + nn(ds, q_na(h))
                dq[h] = dq[h] + nn(k_t[h * HALF : (h + 1) * HALF], ds)
            put(b, dk, dv)
        return dq

    def gx_copy(slot):
        return remote(
            gkv_s.at[slot], gkv_x.at[slot], gx_send.at[slot], gx_recv.at[slot], "seq", sibling
        )

    def grad_copy(slot, sender, dst):
        return remote(
            gkv_s.at[slot], gkv_r.at[sender], g_send.at[slot // 2], g_recv.at[sender], "seq", dst
        )

    def merge(i):
        dz = i + i // 2 - 2 * (i // 3)
        for x in range(2):
            slot = in_seq(x, dz, core)
            gx_copy(slot).wait_recv()
            for j in range(2):
                gkv_s[slot, j] = (
                    gkv_s[slot, j].astype(F32) + gkv_x[slot, j].astype(F32)
                ).astype(BF16)

            @pl.when(slot != seq)
            def _():
                grad_copy(slot, chip, slot).start()

    acc_qf[...] = jnp.zeros((128, ROWS), F32)

    @pl.loop(0, 4)
    def _(back):
        i = 3 - back
        dz = i + i // 2 - 2 * (i // 3)

        def put(b, dk, dv):
            slot = in_seq(b // 2, dz, b % 2)
            gkv_s[slot, 0] = dk.astype(BF16)
            gkv_s[slot, 1] = dv.astype(BF16)

            @pl.when(core != b % 2)
            def _():
                gx_copy(slot).start()

        dq = backward(
            lambda b: kv[in_seq(b // 2, dz, b % 2), 0],
            lambda b: kv[in_seq(b // 2, dz, b % 2), 1],
            lambda h: gf_t[h],
            lambda h: gf_n[h],
            lambda h: qf_n[h],
            lambda h: e_far.at[h, i],
            lambda h: fac_f[h, i],
            lambda h: delta_f[h],
            put,
        )
        for h in range(2):
            half = slice(h * HALF, (h + 1) * HALF)
            acc_qf[half] = acc_qf[half] + dq[h]

        @pl.when(back > 0)
        def _():
            merge(i + 1)

        @pl.when(back == 0)
        def _():
            dx_copy(core).wait_recv()
            dwm[...] = dwp[core] + dwx[...]
            for n in range(1, 8):
                dw_copy(chip, n).start()

        @pl.when(back == 3)
        def _():
            for n in range(1, 8):
                dw_copy(peer_c(n), n).wait_recv()
            dwr[chip] = dwm[chip]
            part = dwr[0]
            for n in range(1, 8):
                part = part + dwr[n]
            dwf[core, chip] = part.astype(BF16)
            for n in range(1, 8):
                df_copy(chip, n).start()

    acc_k[...] = jnp.zeros((4, ROWS, 128), F32)
    acc_v[...] = jnp.zeros((4, ROWS, 128), F32)

    @pl.loop(0, RATE)
    def _(r):
        @pl.when(r == 1)
        def _():
            merge(0)

        @pl.when(r == 2)
        def _():
            for n in range(1, 8):
                w_copy(peer_h(n), n).wait_recv()
                w_share(peer_h(n), core).start()

        @pl.when(r == 3)
        def _():
            for n in range(1, 8):
                df_copy(peer_c(n), n).wait_recv()
            dc_copy(core).start()

        def put(b, dk, dv):
            acc_k[b] = acc_k[b] + dk
            acc_v[b] = acc_v[b] + dv

        dq = backward(
            lambda b: near_k[b],
            lambda b: near_v[b],
            lambda h: g_t[h, r],
            lambda h: g_n[h, r],
            lambda h: q_n[h, r],
            lambda h: e_near.at[h, r],
            lambda h: fac_n[h, r],
            lambda h: delta_n[h, r],
            put,
        )
        for h in range(2):
            acc_q[r, h * HALF : (h + 1) * HALF] = dq[h]

    dq_parts = []
    for r in range(RATE):
        dq_r = (acc_q[r] + jnp.where(shift_col == r, acc_qf[...], 0.0)) * SCALE
        dq_parts.append(dq_r.T.astype(BF16))
    dq_ref[...] = nn(jnp.concatenate(dq_parts, axis=1), perm[...]).astype(BF16)

    @pl.loop(1, NHEAD)
    def _(i):
        w_share(peer_h(i), 1 - core).wait_recv()
        at_copy(peer_h(i), i).wait_recv()

    from_rm = jnp.where(rm_row == lax.rem(rm_col, 32) * RATE + rm_col // 32, 1.0, 0.0).astype(BF16)
    result = jnp.zeros((128, WIDTH), F32)
    for h in range(NHEAD):
        rows = nn(from_rm, attn_r[h].reshape(128, 128)).astype(BF16)
        result = result + nn(rows, ws[h])
    lo_ref[...] = result.astype(BF16)

    @pl.loop(1, 8)
    def _(i):
        grad_copy(seq, peer_c(i), partner).wait_recv()

    gkv_r[chip] = gkv_s[seq]
    sum_k = gkv_r[0, 0].astype(F32)
    sum_v = gkv_r[0, 1].astype(F32)
    for j in range(1, 8):
        sum_k = sum_k + gkv_r[j, 0].astype(F32)
        sum_v = sum_v + gkv_r[j, 1].astype(F32)
    dk_parts = []
    dv_parts = []
    for r in range(RATE):
        mine = shift_row == r
        dk_parts.append(((acc_k[r] + jnp.where(mine, sum_k, 0.0)) * SCALE).astype(BF16))
        dv_parts.append((acc_v[r] + jnp.where(mine, sum_v, 0.0)).astype(BF16))
    dk_ref[...] = nn(jnp.concatenate(dk_parts, axis=1), perm[...]).astype(BF16)
    dv_ref[...] = nn(jnp.concatenate(dv_parts, axis=1), perm[...]).astype(BF16)

    dc_copy(1 - core).wait_recv()
    for half in range(2):
        whole = dwf[half].reshape(128, 384)
        dw_ref[0:48, half * 384 : (half + 1) * 384] = whole[0:48]
        dw_ref[48:96, half * 384 : (half + 1) * 384] = whole[64:112]

    dx_copy(1 - core).wait_send()
    dc_copy(core).wait_send()

    @pl.loop(0, 15)
    def _(i):
        kv_copy(seq, i, partner).wait_send()

    @pl.loop(0, 7)
    def _(i):
        dy_copy(head, i, partner_h).wait_send()

    @pl.loop(1, 8)
    def _(i):
        w_copy(head, i).wait_send()
        w_share(peer_h(i), core).wait_send()
        at_copy(head, i).wait_send()
        dw_copy(chip, i).wait_send()
        df_copy(chip, i).wait_send()
        grad_copy(at_chip(peer_c(i)), chip, partner).wait_send()

    @pl.loop(0, 8)
    def _(i):
        gx_copy(i * 2 + 1 - core).wait_send()


def body(queries, keys, values, slide_ids, head_shift_list, out_weight, d_y):
    vmem = pl.BlockSpec(memory_space=pltpu.VMEM)
    smem = pl.BlockSpec(memory_space=pltpu.SMEM)
    sems = pltpu.SemaphoreType.DMA
    return pl.pallas_call(
        kernel,
        out_shape=(
            jax.ShapeDtypeStruct((128, WIDTH), BF16),
            jax.ShapeDtypeStruct((ROWS, 384), BF16),
            jax.ShapeDtypeStruct((ROWS, 384), BF16),
            jax.ShapeDtypeStruct((ROWS, 384), BF16),
            jax.ShapeDtypeStruct((96, WIDTH), BF16),
        ),
        in_specs=[vmem, vmem, vmem, vmem, smem, vmem, vmem],
        out_specs=(vmem,) * 5,
        scratch_shapes=[
            pltpu.VMEM((4 * 128, 384), BF16),
            pltpu.VMEM((4, ROWS, 128), BF16),
            pltpu.VMEM((4, ROWS, 128), BF16),
            pltpu.VMEM((NSEQ, 2, ROWS, 128), BF16),
            pltpu.VMEM((2, RATE, 128, ROWS), BF16),
            pltpu.VMEM((2, RATE, ROWS, 128), BF16),
            pltpu.VMEM((2, 128, ROWS), BF16),
            pltpu.VMEM((2, ROWS, 128), BF16),
            pltpu.VMEM((2, RATE, 128, ROWS), BF16),
            pltpu.VMEM((2, RATE, ROWS, 128), BF16),
            pltpu.VMEM((2, 128, ROWS), BF16),
            pltpu.VMEM((2, ROWS, 128), BF16),
            pltpu.VMEM((2, RATE, 4, ROWS, ROWS), F32),
            pltpu.VMEM((2, 4, 4, ROWS, ROWS), F32),
            pltpu.VMEM((2, RATE, 1, ROWS), F32),
            pltpu.VMEM((2, RATE, 1, ROWS), F32),
            pltpu.VMEM((2, RATE, HALF, ROWS), F32),
            pltpu.VMEM((2, 4, 1, ROWS), F32),
            pltpu.VMEM((2, 4, 1, ROWS), F32),
            pltpu.VMEM((2, 4, HALF, ROWS), F32),
            pltpu.VMEM((2, RATE, 1, ROWS), F32),
            pltpu.VMEM((2, 4, 1, ROWS), F32),
            pltpu.VMEM((2, RATE, 1, ROWS), F32),
            pltpu.VMEM((2, 1, ROWS), F32),
            pltpu.VMEM((RATE, 128, ROWS), BF16),
            pltpu.VMEM((RATE, ROWS, 128), BF16),
            pltpu.VMEM((NHEAD, RATE, 32, 128), BF16),
            pltpu.VMEM((RATE, ROWS, WIDTH), BF16),
            pltpu.VMEM((NHEAD, 128, WIDTH), BF16),
            pltpu.VMEM((2, 8, 16, 384), F32),
            pltpu.VMEM((8, 16, 384), F32),
            pltpu.VMEM((8, 16, 384), F32),
            pltpu.VMEM((8, 16, 384), F32),
            pltpu.VMEM((2, 8, 16, 384), BF16),
            pltpu.VMEM((NSEQ, 2, ROWS, 128), BF16),
            pltpu.VMEM((NSEQ, 2, ROWS, 128), BF16),
            pltpu.VMEM((8, 2, ROWS, 128), BF16),
            pltpu.VMEM((4, ROWS, 128), F32),
            pltpu.VMEM((4, ROWS, 128), F32),
            pltpu.VMEM((RATE, 128, ROWS), F32),
            pltpu.VMEM((128, ROWS), F32),
            sems((NSEQ,)),
            sems((NSEQ,)),
            sems((NHEAD,)),
            sems((NHEAD,)),
            sems((NHEAD,)),
            sems((NHEAD,)),
            sems((NHEAD,)),
            sems((NHEAD,)),
            sems((NHEAD,)),
            sems((NHEAD,)),
            sems((2,)),
            sems((8,)),
            sems((8,)),
            sems((8,)),
            sems((8,)),
            sems((2,)),
            sems((NSEQ,)),
            sems((NSEQ,)),
            sems((8,)),
            sems((8,)),
        ],
        compiler_params=pltpu.CompilerParams(
            collective_id=0, has_side_effects=True, vmem_limit_bytes=56 * 1024 * 1024
        ),
        cost_estimate=pl.CostEstimate(
            flops=3_000_000_000, bytes_accessed=4_000_000, transcendentals=5_000_000
        ),
    )(
        queries,
        keys,
        values,
        slide_ids.reshape(8, 128),
        head_shift_list,
        out_weight,
        d_y,
    )


def solution(mesh):
    placed = (
        P("seq", "head"),
        P("seq", "head"),
        P("seq", "head"),
        P("seq"),
        P(),
        P("head", None),
        P(("seq", "head"), None),
    )
    return jax.shard_map(
        body,
        mesh=mesh,
        in_specs=placed,
        out_specs=(
            P(("seq", "head"), None),
            P("seq", "head"),
            P("seq", "head"),
            P("seq", "head"),
            P("head", None),
        ),
        check_vma=False,
    )
```

```python
import math

import jax
import jax.numpy as jnp
from jax import lax
from jax.experimental import pallas as pl
from jax.experimental.pallas import tpu as pltpu
from jax.sharding import PartitionSpec as P

HEAD = 48
HALF = 64
RATE = 4
ROWS = 256
WIDTH = 768
NSEQ = 16
NHEAD = 8
SAME = 8192.0
SCALE = 1.0 / math.sqrt(HEAD)
EXP2 = SCALE * math.log2(math.e)
F32 = jnp.float32
BF16 = jnp.bfloat16


def nt(a, b):
    return lax.dot_general(a, b, (((1,), (1,)), ((), ())), preferred_element_type=F32)


def nn(a, b):
    return jnp.dot(a, b, preferred_element_type=F32)


def iota(shape, dim):
    return lax.broadcasted_iota(jnp.int32, shape, dim)


def remote(src, dst, send, recv, axis, index):
    return pltpu.make_async_remote_copy(
        src_ref=src,
        dst_ref=dst,
        send_sem=send,
        recv_sem=recv,
        device_id={axis: index},
        device_id_type=pl.DeviceIdType.MESH,
    )


def kernel(
    q_ref,
    k_ref,
    v_ref,
    id_ref,
    shift_ref,
    w_ref,
    dy_ref,
    lo_ref,
    dq_ref,
    dk_ref,
    dv_ref,
    dw_ref,
    perm,
    near_k,
    near_v,
    kv,
    q_t,
    q_n,
    g_t,
    g_n,
    e_near,
    e_far,
    top_n,
    sum_n,
    out_n,
    top_f,
    sum_f,
    out_f,
    fac_n,
    fac_f,
    delta,
    attn_t,
    attn_n,
    attn_r,
    dys,
    ws,
    dwp,
    dwx,
    dwm,
    dwr,
    dwf,
    gkv_s,
    gkv_x,
    gkv_r,
    gkv_p,
    gkv_y,
    acc_k,
    acc_v,
    acc_q,
    kv_send,
    kv_recv,
    dy_send,
    dy_recv,
    w_send,
    w_recv,
    ws_send,
    ws_recv,
    at_send,
    at_recv,
    dx_sem,
    dw_send,
    dw_recv,
    df_send,
    df_recv,
    dc_sem,
    gx_send,
    gx_recv,
    g_send,
    g_recv,
    gy_sem,
):
    seq = lax.axis_index("seq")
    head = lax.axis_index("head")

    x_lo, z, core = seq // 8, lax.rem(seq // 2, 4), lax.rem(seq, 2)
    x_hi, y = head // 4, lax.rem(head, 4)
    chip = seq // 2

    def at_chip(j):
        return j * 2 + core

    def in_seq(x, dz, c):
        return x * 8 + lax.rem(z + dz, 4) * 2 + c

    def in_head(x, dy):
        return x * 4 + lax.rem(y + dy, 4)

    def peer_c(i):
        return lax.rem(chip + i, 8)

    def peer_h(i):
        return lax.rem(head + i, NHEAD)

    sibling = in_seq(x_lo, 0, 1 - core)
    partner = in_seq(1 - x_lo, 0, core)
    partner_h = in_head(1 - x_hi, 0)
    turns = (1, 3, 2)

    barrier = pltpu.get_barrier_semaphore()
    pl.semaphore_signal(
        barrier, inc=1, device_id={"seq": sibling}, device_id_type=pl.DeviceIdType.MESH
    )

    @pl.loop(1, 8)
    def _(i):
        pl.semaphore_signal(
            barrier,
            inc=1,
            device_id={"seq": at_chip(peer_c(i))},
            device_id_type=pl.DeviceIdType.MESH,
        )
        pl.semaphore_signal(
            barrier, inc=1, device_id={"head": peer_h(i)}, device_id_type=pl.DeviceIdType.MESH
        )

    slide_col = lax.rem(iota((128, 128), 0), HALF) - HEAD
    below = jnp.zeros((128, 128), F32)
    upto = jnp.zeros((128, 128), F32)
    for s in range(8):
        ids = id_ref[s : s + 1, :]
        below = below + jnp.where(ids < slide_col, 1.0, 0.0)
        upto = upto + jnp.where(ids <= slide_col, 1.0, 0.0)
    ones = jnp.ones((8, 128), BF16)
    first_row = nt(ones, below.astype(BF16))[0:1, :]
    last_row = nt(ones, upto.astype(BF16))[0:1, :]
    first_col = jnp.sum(below, axis=1, keepdims=True)
    last_col = jnp.sum(upto, axis=1, keepdims=True)

    shift0 = shift_ref[2 * head]
    shift1 = shift_ref[2 * head + 1]
    lane_row = iota((1, 128), 1)
    lane_col = iota((128, 1), 0)
    shift_row = jnp.where(lane_row < HALF, shift0, shift1)
    shift_col = jnp.where(lane_col < HALF, shift0, shift1)
    hot_row = lax.rem(lane_row, HALF) >= HEAD
    hot_col = lax.rem(lane_col, HALF) >= HEAD

    def turned(shift, j):
        return jnp.bitwise_and(shift + 1 + j, RATE - 1)

    def to_slot(parts, shift, j):
        out = parts[0]
        for r in range(1, RATE):
            out = jnp.where(turned(shift, j) == r, parts[r], out)
        return out

    def from_slot(parts, shift, r):
        out = parts[0]
        for j in range(1, RATE):
            out = jnp.where(turned(shift, j) == r, parts[j], out)
        return out

    within = lax.rem(lane_col, HALF)
    source = (lane_col // HALF) * (RATE * HEAD) + within
    given = iota((128, 384), 1)
    for r in range(RATE):
        held = jnp.where(within < HEAD, source + r * HEAD, -1)
        perm[r * 128 : (r + 1) * 128] = jnp.where(given == held, 1.0, 0.0).astype(BF16)
    k_p = nt(k_ref[...], perm[...])
    v_p = nt(v_ref[...], perm[...])
    far_k = jnp.zeros((ROWS, 128), F32)
    far_v = jnp.zeros((ROWS, 128), F32)
    for r in range(RATE):
        at = (iota((ROWS, 128), 0) * RATE + r).astype(F32)
        hot = jnp.where(hot_row & (at >= first_row) & (at < last_row), 1.0, 0.0)
        k_r = k_p[:, r * 128 : (r + 1) * 128] + hot
        v_r = v_p[:, r * 128 : (r + 1) * 128]
        near_k[r] = k_r.astype(BF16)
        near_v[r] = v_r.astype(BF16)
        far_k = jnp.where(shift_row == r, k_r, far_k)
        far_v = jnp.where(shift_row == r, v_r, far_v)
    kv[seq, 0] = far_k.astype(BF16)
    kv[seq, 1] = far_v.astype(BF16)

    rm_row = iota((128, 128), 0)
    rm_col = iota((128, 128), 1)
    to_rm = jnp.where(rm_col == lax.rem(rm_row, 32) * RATE + rm_row // 32, 1.0, 0.0).astype(BF16)
    dy_own = nn(to_rm, dy_ref[...]).astype(BF16)
    own_rows = pl.ds(pl.multiple_of(head * 32, 32), 32)
    for r in range(RATE):
        dys[r, own_rows, :] = dy_own[r * 32 : (r + 1) * 32]

    zeros16 = jnp.zeros((16, WIDTH), BF16)
    ws[head, 0:48] = w_ref[0:48]
    ws[head, 64:112] = w_ref[48:96]
    for h in range(NHEAD):
        ws[h, 48:64] = zeros16
        ws[h, 112:128] = zeros16

    pl.semaphore_wait(barrier, 15)

    def kv_copy(slot, i, dst):
        return remote(kv.at[slot], kv.at[slot], kv_send.at[i], kv_recv.at[slot], "seq", dst)

    def dy_copy(owner, i, dst):
        rows = pl.ds(pl.multiple_of(owner * 32, 32), 32)
        part = dys.at[:, rows, :]
        return remote(part, part, dy_send.at[i], dy_recv.at[owner], "head", dst)

    def w_copy(owner, i):
        part = ws.at[owner, pl.ds(pl.multiple_of(core * HALF, HALF), HEAD)]
        return remote(part, part, w_send.at[i], w_recv.at[owner], "head", peer_h(i))

    def w_share(owner, half):
        part = ws.at[owner, pl.ds(pl.multiple_of(half * HALF, HALF), HEAD)]
        return remote(part, part, ws_send.at[owner], ws_recv.at[owner], "seq", sibling)

    kv_copy(seq, 0, partner).start()
    for j, turn in enumerate(turns):
        kv_copy(seq, 1 + j, in_seq(x_lo, turn, core)).start()
    kv_copy(seq, 4, sibling).start()
    dy_copy(head, 0, partner_h).start()
    for n, turn in enumerate(turns):
        dy_copy(head, 1 + n, in_head(x_hi, turn)).start()

    q_p = nt(q_ref[...], perm[...])
    q_pt = nt(perm[...], q_ref[...])
    q_rows = []
    q_cols = []
    for r in range(RATE):
        at = (iota((128, ROWS), 1) * RATE + r).astype(F32)
        hot = jnp.where(hot_col & (at >= first_col) & (at < last_col), SAME, 0.0)
        q_rows.append(q_p[:, r * 128 : (r + 1) * 128])
        q_cols.append(q_pt[r * 128 : (r + 1) * 128, :] + hot)
    for j in range(RATE):
        q_j = to_slot(q_rows, shift_row, j)
        q_jt = to_slot(q_cols, shift_col, j)
        q_n[0, j] = jnp.where(lane_row < HALF, q_j, 0.0).astype(BF16)
        q_n[1, j] = jnp.where(lane_row < HALF, 0.0, q_j).astype(BF16)
        q_t[0, j] = jnp.where(lane_col < HALF, q_jt, 0.0).astype(BF16)
        q_t[1, j] = jnp.where(lane_col < HALF, 0.0, q_jt).astype(BF16)

    def forward(keys, vals, q_of, e_of, h):
        top = None
        for b in range(4):
            s = nn(keys(b), q_of)
            e_of[b] = s
            m = jnp.max(s, axis=0, keepdims=True)
            top = m if top is None else jnp.maximum(top, m)
        total = jnp.zeros((1, ROWS), F32)
        out = jnp.zeros((HALF, ROWS), F32)
        for b in range(4):
            e = jnp.exp2((e_of[b] - top) * EXP2)
            e_of[b] = e
            total = total + jnp.sum(e, axis=0, keepdims=True)
            v_t = vals(b).T[h * HALF : (h + 1) * HALF]
            out = out + nn(v_t, e.astype(BF16))
        return top, total, out

    halves = (slice(0, HALF), slice(HALF, 2 * HALF))

    @pl.loop(0, RATE)
    def _(j):
        for h in range(2):
            top, total, out = forward(
                lambda b: near_k[b], lambda b: near_v[b], q_t[h, j], e_near.at[h, j], h
            )
            top_n[h] = top
            sum_n[h] = total
            out_n[h] = out
            inverse = 1.0 / total
            fac_n[h, j] = inverse
            attn_t[j, halves[h]] = (out * inverse).astype(BF16)

        @pl.when(j == 0)
        def _():
            kv_copy(partner, 0, partner).wait_recv()
            for n, turn in enumerate(turns):
                kv_copy(partner, 5 + n, in_seq(x_lo, turn, core)).start()
            kv_copy(partner, 8, sibling).start()

        @pl.when(j == 1)
        def _():
            dy_copy(partner_h, 0, partner_h).wait_recv()
            for n, turn in enumerate(turns):
                dy_copy(partner_h, 4 + n, in_head(x_hi, turn)).start()

    def share(i):
        dz = i + i // 2 - 2 * (i // 3)
        for x in range(2):
            slot = in_seq(x, dz, core)
            kv_copy(slot, 0, partner).wait_recv()
            kv_copy(slot, 9 + 2 * (i - 1) + x, sibling).start()

    def far_forward(i):
        dz = i + i // 2 - 2 * (i // 3)
        for x in range(2):
            kv_copy(in_seq(x, dz, 1 - core), 0, partner).wait_recv()
        for h in range(2):
            top, total, out = forward(
                lambda b: kv[in_seq(b // 2, dz, b % 2), 0],
                lambda b: kv[in_seq(b // 2, dz, b % 2), 1],
                q_t[h, 3],
                e_far.at[h, i],
                h,
            )
            top_f[h, i] = top
            sum_f[h, i] = total
            out_f[h, i] = out

    @pl.loop(0, 4)
    def _(i):
        @pl.when(i == 1)
        def _():
            share(1)

        @pl.when((i == 1) | (i == 2))
        def _():
            share(i + 1)

        far_forward(i)

    for h in range(2):
        top = top_n[h]
        for i in range(4):
            top = jnp.maximum(top, top_f[h, i])
        weight = jnp.exp2((top_n[h] - top) * EXP2)
        total = weight * sum_n[h]
        out = weight * out_n[h]
        weights = []
        for i in range(4):
            w_i = jnp.exp2((top_f[h, i] - top) * EXP2)
            weights.append(w_i)
            total = total + w_i * sum_f[h, i]
            out = out + w_i * out_f[h, i]
        inverse = 1.0 / total
        fac_n[h, 3] = weight * inverse
        for i in range(4):
            fac_f[h, i] = weights[i] * inverse
        attn_t[3, halves[h]] = (out * inverse).astype(BF16)

    attn_slots = [attn_t[j].astype(F32) for j in range(RATE)]
    attn_rt = [from_slot(attn_slots, shift_col, r) for r in range(RATE)]
    for r in range(RATE):
        attn_n[r] = attn_rt[r].T.astype(BF16)

    def at_copy(slot, i):
        rows = pl.ds(pl.multiple_of(peer_h(i) * 32, 32), 32)
        return remote(
            attn_n.at[:, rows, :], attn_r.at[slot], at_send.at[i], at_recv.at[slot], "head", peer_h(i)
        )

    for n in range(1, NHEAD):
        at_copy(head, n).start()
    for r in range(RATE):
        attn_r[head, r] = attn_n[r, own_rows, :]

    for turn in turns:
        for x in range(2):
            dy_copy(in_head(x, turn), 0, partner_h).wait_recv()
    for n in range(1, NHEAD):
        w_copy(head, n).start()

    w_own = ws[head]
    g_rows = []
    g_cols = []
    weight_grad = jnp.zeros((128, WIDTH), F32)
    for r in range(RATE):
        g_rows.append(nt(dys[r], w_own))
        g_cols.append(nt(w_own, dys[r]))
        weight_grad = weight_grad + nn(attn_rt[r].astype(BF16), dys[r])
    for j in range(RATE):
        g_j = to_slot(g_rows, shift_row, j)
        g_jt = to_slot(g_cols, shift_col, j)
        g_n[0, j] = jnp.where(lane_row < HALF, g_j, 0.0).astype(BF16)
        g_n[1, j] = jnp.where(lane_row < HALF, 0.0, g_j).astype(BF16)
        g_t[0, j] = jnp.where(lane_col < HALF, g_jt, 0.0).astype(BF16)
        g_t[1, j] = jnp.where(lane_col < HALF, 0.0, g_jt).astype(BF16)
        for h in range(2):
            product = g_t[h, j, halves[h], :].astype(F32) * attn_t[j, halves[h]].astype(F32)
            delta[h, j] = jnp.sum(product, axis=0, keepdims=True)

    for half in range(2):
        for n in range(8):
            dwp[half, n] = weight_grad[n * 16 : (n + 1) * 16, half * 384 : (half + 1) * 384]

    def dx_copy(half):
        return remote(dwp.at[half], dwx, dx_sem.at[0], dx_sem.at[1], "seq", sibling)

    def dw_copy(sender, i):
        dst = peer_c(i)
        return remote(dwm.at[dst], dwr.at[sender], dw_send.at[i], dw_recv.at[sender], "seq", at_chip(dst))

    def df_copy(sender, i):
        part = dwf.at[core, sender]
        return remote(part, part, df_send.at[i], df_recv.at[sender], "seq", at_chip(peer_c(i)))

    def dc_copy(half):
        return remote(dwf.at[half], dwf.at[half], dc_sem.at[0], dc_sem.at[1], "seq", sibling)

    dx_copy(1 - core).start()

    def weight_over_cores():
        dx_copy(core).wait_recv()
        dwm[...] = dwp[core] + dwx[...]
        for n in range(1, 8):
            dw_copy(chip, n).start()

    def weight_over_chips():
        for n in range(1, 8):
            dw_copy(peer_c(n), n).wait_recv()
        dwr[chip] = dwm[chip]
        part = dwr[0]
        for n in range(1, 8):
            part = part + dwr[n]
        dwf[core, chip] = part.astype(BF16)
        for n in range(1, 8):
            df_copy(chip, n).start()

    def weight_to_sibling():
        for n in range(1, 8):
            df_copy(peer_c(n), n).wait_recv()
        dc_copy(core).start()

    def backward(keys, vals, j, e_of, factor, put):
        dq = [jnp.zeros((HALF, ROWS), F32), jnp.zeros((HALF, ROWS), F32)]
        for b in range(4):
            k_t = keys(b).T
            val = vals(b)
            dk = jnp.zeros((ROWS, 128), F32)
            dv = jnp.zeros((ROWS, 128), F32)
            for h in range(2):
                p = e_of(h)[b] * factor(h)
                ds = (p * (nn(val, g_t[h, j]) - delta[h, j])).astype(BF16)
                dv = dv + nn(p.astype(BF16), g_n[h, j])
                dk = dk + nn(ds, q_n[h, j])
                dq[h] = dq[h] + nn(k_t[halves[h]], ds)
            put(b, dk, dv)
        return dq

    acc_k[...] = jnp.zeros((4, ROWS, 128), F32)
    acc_v[...] = jnp.zeros((4, ROWS, 128), F32)

    def near_backward(j):
        def put(b, dk, dv):
            acc_k[b] = acc_k[b] + dk
            acc_v[b] = acc_v[b] + dv

        dq = backward(
            lambda b: near_k[b],
            lambda b: near_v[b],
            j,
            lambda h: e_near.at[h, j],
            lambda h: fac_n[h, j],
            put,
        )
        for h in range(2):
            acc_q[j, halves[h]] = dq[h]

    def gx_copy(slot):
        return remote(
            gkv_s.at[slot], gkv_x.at[slot], gx_send.at[slot], gx_recv.at[slot], "seq", sibling
        )

    def grad_copy(x, dz):
        slot = in_seq(x, dz, core)
        index = dz + 4 * (x != x_lo)
        return remote(
            gkv_s.at[slot],
            gkv_r.at[index],
            g_send.at[index],
            g_recv.at[index],
            "seq",
            in_seq(x_lo, dz, core),
        )

    def gy_copy():
        return remote(gkv_p, gkv_y, gy_sem.at[0], gy_sem.at[1], "seq", partner)

    def merge(i):
        dz = i + i // 2 - 2 * (i // 3)
        for x in range(2):
            slot = in_seq(x, dz, core)
            gx_copy(slot).wait_recv()
            for n in range(2):
                gkv_s[slot, n] = (
                    gkv_s[slot, n].astype(F32) + gkv_x[slot, n].astype(F32)
                ).astype(BF16)

            @pl.when(dz != 0)
            def _():
                grad_copy(x, dz).start()

    def sum_partner():
        for turn in turns:
            grad_copy(1 - x_lo, turn).wait_recv()
        for n in range(2):
            total = gkv_s[partner, n].astype(F32)
            for turn in turns:
                total = total + gkv_r[4 + turn, n].astype(F32)
            gkv_p[n] = total.astype(BF16)
        gy_copy().start()

    acc_q[3] = jnp.zeros((128, ROWS), F32)

    @pl.loop(0, 4)
    def _(back):
        i = 3 - back
        dz = i + i // 2 - 2 * (i // 3)

        def put(b, dk, dv):
            slot = in_seq(b // 2, dz, b % 2)
            gkv_s[slot, 0] = dk.astype(BF16)
            gkv_s[slot, 1] = dv.astype(BF16)

            @pl.when(core != b % 2)
            def _():
                gx_copy(slot).start()

        dq = backward(
            lambda b: kv[in_seq(b // 2, dz, b % 2), 0],
            lambda b: kv[in_seq(b // 2, dz, b % 2), 1],
            3,
            lambda h: e_far.at[h, i],
            lambda h: fac_f[h, i],
            put,
        )
        for h in range(2):
            acc_q[3, halves[h]] = acc_q[3, halves[h]] + dq[h]

        @pl.when(back > 0)
        def _():
            merge(i + 1)

        @pl.when(back == 0)
        def _():
            weight_over_cores()

        @pl.when(back == 3)
        def _():
            weight_over_chips()

    acc_far = acc_q[3]
    merge(0)

    @pl.loop(0, RATE)
    def _(j):
        near_backward(j)

        @pl.when(j == 1)
        def _():
            weight_to_sibling()
            for n in range(1, NHEAD):
                w_copy(peer_h(n), n).wait_recv()
                w_share(peer_h(n), core).start()

        @pl.when(j == 2)
        def _():
            sum_partner()

    acc_q[3] = acc_q[3] + acc_far
    dq_slots = [(acc_q[j] * SCALE).T for j in range(RATE)]
    dq_parts = [from_slot(dq_slots, shift_row, r).astype(BF16) for r in range(RATE)]
    dq_ref[...] = nn(jnp.concatenate(dq_parts, axis=1), perm[...]).astype(BF16)

    for n in range(1, NHEAD):
        w_share(peer_h(n), 1 - core).wait_recv()
        at_copy(peer_h(n), n).wait_recv()
    from_rm = jnp.where(rm_row == lax.rem(rm_col, 32) * RATE + rm_col // 32, 1.0, 0.0).astype(BF16)
    result = jnp.zeros((128, WIDTH), F32)
    for h in range(NHEAD):
        rows = nn(from_rm, attn_r[h].reshape(128, 128)).astype(BF16)
        result = result + nn(rows, ws[h])
    lo_ref[...] = result.astype(BF16)

    for turn in turns:
        grad_copy(x_lo, turn).wait_recv()
    gy_copy().wait_recv()
    far = []
    for n in range(2):
        total = gkv_s[seq, n].astype(F32) + gkv_y[n].astype(F32)
        for turn in turns:
            total = total + gkv_r[turn, n].astype(F32)
        far.append(total)
    sum_k, sum_v = far
    dk_parts = []
    dv_parts = []
    for r in range(RATE):
        mine = shift_row == r
        dk_parts.append(((acc_k[r] + jnp.where(mine, sum_k, 0.0)) * SCALE).astype(BF16))
        dv_parts.append((acc_v[r] + jnp.where(mine, sum_v, 0.0)).astype(BF16))
    dk_ref[...] = nn(jnp.concatenate(dk_parts, axis=1), perm[...]).astype(BF16)
    dv_ref[...] = nn(jnp.concatenate(dv_parts, axis=1), perm[...]).astype(BF16)

    dc_copy(1 - core).wait_recv()
    for half in range(2):
        whole = dwf[half].reshape(128, 384)
        dw_ref[0:48, half * 384 : (half + 1) * 384] = whole[0:48]
        dw_ref[48:96, half * 384 : (half + 1) * 384] = whole[64:112]

    dx_copy(1 - core).wait_send()
    dc_copy(core).wait_send()

    @pl.loop(0, 15)
    def _(i):
        kv_copy(seq, i, partner).wait_send()

    @pl.loop(1, 8)
    def _(i):
        w_copy(head, i).wait_send()
        w_share(peer_h(i), core).wait_send()
        dy_copy(head, i - 1, partner_h).wait_send()
        at_copy(head, i).wait_send()
        dw_copy(chip, i).wait_send()
        df_copy(chip, i).wait_send()

    @pl.loop(0, 8)
    def _(i):
        gx_copy(i * 2 + 1 - core).wait_send()

    gy_copy().wait_send()
    for turn in turns:
        for x in range(2):
            grad_copy(x, turn).wait_send()


def finish(*refs):
    for source, target in zip(refs[:5], refs[5:], strict=True):
        target[...] = source[...]


def body(queries, keys, values, slide_ids, head_shift_list, out_weight, d_y):
    vmem = pl.BlockSpec(memory_space=pltpu.VMEM)
    smem = pl.BlockSpec(memory_space=pltpu.SMEM)
    sems = pltpu.SemaphoreType.DMA
    results = pl.pallas_call(
        kernel,
        out_shape=(
            jax.ShapeDtypeStruct((128, WIDTH), BF16),
            jax.ShapeDtypeStruct((ROWS, 384), BF16),
            jax.ShapeDtypeStruct((ROWS, 384), BF16),
            jax.ShapeDtypeStruct((ROWS, 384), BF16),
            jax.ShapeDtypeStruct((96, WIDTH), BF16),
        ),
        in_specs=[vmem, vmem, vmem, vmem, smem, vmem, vmem],
        out_specs=(vmem,) * 5,
        scratch_shapes=[
            pltpu.VMEM((4 * 128, 384), BF16),
            pltpu.VMEM((4, ROWS, 128), BF16),
            pltpu.VMEM((4, ROWS, 128), BF16),
            pltpu.VMEM((NSEQ, 2, ROWS, 128), BF16),
            pltpu.VMEM((2, RATE, 128, ROWS), BF16),
            pltpu.VMEM((2, RATE, ROWS, 128), BF16),
            pltpu.VMEM((2, RATE, 128, ROWS), BF16),
            pltpu.VMEM((2, RATE, ROWS, 128), BF16),
            pltpu.VMEM((2, RATE, 4, ROWS, ROWS), F32),
            pltpu.VMEM((2, 4, 4, ROWS, ROWS), F32),
            pltpu.VMEM((2, 1, ROWS), F32),
            pltpu.VMEM((2, 1, ROWS), F32),
            pltpu.VMEM((2, HALF, ROWS), F32),
            pltpu.VMEM((2, 4, 1, ROWS), F32),
            pltpu.VMEM((2, 4, 1, ROWS), F32),
            pltpu.VMEM((2, 4, HALF, ROWS), F32),
            pltpu.VMEM((2, RATE, 1, ROWS), F32),
            pltpu.VMEM((2, 4, 1, ROWS), F32),
            pltpu.VMEM((2, RATE, 1, ROWS), F32),
            pltpu.VMEM((RATE, 128, ROWS), BF16),
            pltpu.VMEM((RATE, ROWS, 128), BF16),
            pltpu.VMEM((NHEAD, RATE, 32, 128), BF16),
            pltpu.VMEM((RATE, ROWS, WIDTH), BF16),
            pltpu.VMEM((NHEAD, 128, WIDTH), BF16),
            pltpu.VMEM((2, 8, 16, 384), F32),
            pltpu.VMEM((8, 16, 384), F32),
            pltpu.VMEM((8, 16, 384), F32),
            pltpu.VMEM((8, 16, 384), F32),
            pltpu.VMEM((2, 8, 16, 384), BF16),
            pltpu.VMEM((NSEQ, 2, ROWS, 128), BF16),
            pltpu.VMEM((NSEQ, 2, ROWS, 128), BF16),
            pltpu.VMEM((8, 2, ROWS, 128), BF16),
            pltpu.VMEM((2, ROWS, 128), BF16),
            pltpu.VMEM((2, ROWS, 128), BF16),
            pltpu.VMEM((4, ROWS, 128), F32),
            pltpu.VMEM((4, ROWS, 128), F32),
            pltpu.VMEM((RATE, 128, ROWS), F32),
            sems((NSEQ,)),
            sems((NSEQ,)),
            sems((NHEAD,)),
            sems((NHEAD,)),
            sems((NHEAD,)),
            sems((NHEAD,)),
            sems((NHEAD,)),
            sems((NHEAD,)),
            sems((NHEAD,)),
            sems((NHEAD,)),
            sems((2,)),
            sems((8,)),
            sems((8,)),
            sems((8,)),
            sems((8,)),
            sems((2,)),
            sems((NSEQ,)),
            sems((NSEQ,)),
            sems((8,)),
            sems((8,)),
            sems((2,)),
        ],
        compiler_params=pltpu.CompilerParams(
            collective_id=0, has_side_effects=True, vmem_limit_bytes=56 * 1024 * 1024
        ),
        cost_estimate=pl.CostEstimate(
            flops=3_000_000_000, bytes_accessed=4_000_000, transcendentals=5_000_000
        ),
    )(
        queries,
        keys,
        values,
        slide_ids.reshape(8, 128),
        head_shift_list,
        out_weight,
        d_y,
    )
    return pl.pallas_call(
        finish,
        out_shape=tuple(jax.ShapeDtypeStruct(r.shape, r.dtype) for r in results),
        in_specs=[vmem] * 5,
        out_specs=(vmem,) * 5,
    )(*results)


def solution(mesh):
    placed = (
        P("seq", "head"),
        P("seq", "head"),
        P("seq", "head"),
        P("seq"),
        P(),
        P("head", None),
        P(("seq", "head"), None),
    )
    return jax.shard_map(
        body,
        mesh=mesh,
        in_specs=placed,
        out_specs=(
            P(("seq", "head"), None),
            P("seq", "head"),
            P("seq", "head"),
            P("seq", "head"),
            P("head", None),
        ),
        check_vma=False,
    )
```

```python
import math

import jax
import jax.numpy as jnp
from jax import lax
from jax.experimental import pallas as pl
from jax.experimental.pallas import tpu as pltpu
from jax.sharding import PartitionSpec as P

HEAD = 48
HALF = 64
RATE = 4
ROWS = 256
WIDTH = 768
NSEQ = 16
NHEAD = 8
EARLY = 2
SAME = 8192.0
SCALE = 1.0 / math.sqrt(HEAD)
EXP2 = SCALE * math.log2(math.e)
F32 = jnp.float32
BF16 = jnp.bfloat16


def nt(a, b):
    return lax.dot_general(a, b, (((1,), (1,)), ((), ())), preferred_element_type=F32)


def nn(a, b):
    return jnp.dot(a, b, preferred_element_type=F32)


def iota(shape, dim):
    return lax.broadcasted_iota(jnp.int32, shape, dim)


def remote(src, dst, send, recv, axis, index):
    return pltpu.make_async_remote_copy(
        src_ref=src,
        dst_ref=dst,
        send_sem=send,
        recv_sem=recv,
        device_id={axis: index},
        device_id_type=pl.DeviceIdType.MESH,
    )


def kernel(
    q_ref,
    k_ref,
    v_ref,
    id_ref,
    shift_ref,
    w_ref,
    dy_ref,
    lo_ref,
    dq_ref,
    dk_ref,
    dv_ref,
    dw_ref,
    q_in,
    k_in,
    v_in,
    raw,
    perm,
    near_k,
    near_v,
    kv,
    q_t,
    q_n,
    g_t,
    g_n,
    e_near,
    e_far,
    top_n,
    sum_n,
    out_n,
    top_f,
    sum_f,
    out_f,
    fac_n,
    fac_f,
    delta,
    attn_t,
    attn_n,
    attn_r,
    dys,
    ws,
    dwp,
    dwx,
    dwm,
    dwr,
    dwf,
    gkv_s,
    gkv_x,
    gkv_r,
    q_far,
    q_got,
    g_far,
    g_got,
    o_far,
    o_got,
    m_far,
    m_got,
    t_far,
    t_got,
    dq_far,
    dq_got,
    acc_k,
    acc_v,
    acc_q,
    in_sem,
    kv_send,
    kv_recv,
    dy_send,
    dy_recv,
    w_send,
    w_recv,
    ws_send,
    ws_recv,
    at_send,
    at_recv,
    dx_sem,
    dw_send,
    dw_recv,
    df_send,
    df_recv,
    dc_sem,
    gx_send,
    gx_recv,
    g_send,
    g_recv,
    swap_send,
    swap_recv,
):
    seq = lax.axis_index("seq")
    head = lax.axis_index("head")

    x_lo, z, core = seq // 8, lax.rem(seq // 2, 4), lax.rem(seq, 2)
    x_hi, y = head // 4, lax.rem(head, 4)
    chip = seq // 2

    def at_chip(j):
        return j * 2 + core

    def in_seq(x, dz, c):
        return x * 8 + lax.rem(z + dz, 4) * 2 + c

    def in_z(dz, c):
        return lax.rem(z + dz, 4) * 2 + c

    def in_head(x, dy):
        return x * 4 + lax.rem(y + dy, 4)

    def peer_c(i):
        return lax.rem(chip + i, 8)

    def peer_h(i):
        return lax.rem(head + i, NHEAD)

    sibling = in_seq(x_lo, 0, 1 - core)
    partner = in_seq(1 - x_lo, 0, core)
    partner_h = in_head(1 - x_hi, 0)
    turns = (1, 3, 2)

    barrier = pltpu.get_barrier_semaphore()
    pl.semaphore_signal(
        barrier, inc=1, device_id={"seq": sibling}, device_id_type=pl.DeviceIdType.MESH
    )

    @pl.loop(1, 8)
    def _(i):
        pl.semaphore_signal(
            barrier,
            inc=1,
            device_id={"seq": at_chip(peer_c(i))},
            device_id_type=pl.DeviceIdType.MESH,
        )
        pl.semaphore_signal(
            barrier, inc=1, device_id={"head": peer_h(i)}, device_id_type=pl.DeviceIdType.MESH
        )

    loads = [
        pltpu.make_async_copy(source, target, in_sem.at[n])
        for n, (source, target) in enumerate(
            (
                (k_ref, k_in),
                (v_ref, v_in),
                (q_ref, q_in),
                (dy_ref, raw.at[head]),
                (w_ref.at[0:48], ws.at[head, 0:48]),
                (w_ref.at[48:96], ws.at[head, 64:112]),
            )
        )
    ]
    for load in loads:
        load.start()

    slide_col = lax.rem(iota((128, 128), 0), HALF) - HEAD
    below = jnp.zeros((128, 128), F32)
    upto = jnp.zeros((128, 128), F32)
    for s in range(8):
        ids = id_ref[s : s + 1, :]
        below = below + jnp.where(ids < slide_col, 1.0, 0.0)
        upto = upto + jnp.where(ids <= slide_col, 1.0, 0.0)
    ones = jnp.ones((8, 128), BF16)
    first_row = nt(ones, below.astype(BF16))[0:1, :]
    last_row = nt(ones, upto.astype(BF16))[0:1, :]
    first_col = jnp.sum(below, axis=1, keepdims=True)
    last_col = jnp.sum(upto, axis=1, keepdims=True)

    shift0 = shift_ref[2 * head]
    shift1 = shift_ref[2 * head + 1]
    lane_row = iota((1, 128), 1)
    lane_col = iota((128, 1), 0)
    shift_row = jnp.where(lane_row < HALF, shift0, shift1)
    shift_col = jnp.where(lane_col < HALF, shift0, shift1)
    hot_row = lax.rem(lane_row, HALF) >= HEAD
    hot_col = lax.rem(lane_col, HALF) >= HEAD

    def turned(shift, j):
        return jnp.bitwise_and(shift + 1 + j, RATE - 1)

    def to_slot(parts, shift, j):
        out = parts[0]
        for r in range(1, RATE):
            out = jnp.where(turned(shift, j) == r, parts[r], out)
        return out

    def from_slot(parts, shift, r):
        out = parts[0]
        for j in range(1, RATE):
            out = jnp.where(turned(shift, j) == r, parts[j], out)
        return out

    within = lax.rem(lane_col, HALF)
    source = (lane_col // HALF) * (RATE * HEAD) + within
    given = iota((128, 384), 1)
    for r in range(RATE):
        held = jnp.where(within < HEAD, source + r * HEAD, -1)
        perm[r * 128 : (r + 1) * 128] = jnp.where(given == held, 1.0, 0.0).astype(BF16)
    pl.semaphore_wait(barrier, 15)

    def dy_copy(owner, i, dst, first=False):
        source = dy_ref if first else raw.at[owner]
        return remote(source, raw.at[owner], dy_send.at[i], dy_recv.at[owner], "head", dst)

    dy_copy(head, 0, partner_h, True).start()
    for n, turn in enumerate((2, 1, 3)):
        dy_copy(head, 1 + n, in_head(x_hi, turn), True).start()

    loads[0].wait()
    loads[1].wait()
    k_p = nt(k_in[...], perm[...])
    v_p = nt(v_in[...], perm[...])
    far_k = jnp.zeros((ROWS, 128), F32)
    far_v = jnp.zeros((ROWS, 128), F32)
    for r in range(RATE):
        at = (iota((ROWS, 128), 0) * RATE + r).astype(F32)
        hot = jnp.where(hot_row & (at >= first_row) & (at < last_row), 1.0, 0.0)
        k_r = k_p[:, r * 128 : (r + 1) * 128] + hot
        v_r = v_p[:, r * 128 : (r + 1) * 128]
        near_k[r] = k_r.astype(BF16)
        near_v[r] = v_r.astype(BF16)
        far_k = jnp.where(shift_row == r, k_r, far_k)
        far_v = jnp.where(shift_row == r, v_r, far_v)
    own = in_z(0, core)
    kv[own, 0] = far_k.astype(BF16)
    kv[own, 1] = far_v.astype(BF16)

    def kv_copy(slot, i, dst):
        return remote(kv.at[slot], kv.at[slot], kv_send.at[i], kv_recv.at[slot], "seq", dst)

    def swap(i, source, target):
        return remote(source, target, swap_send.at[i], swap_recv.at[i], "seq", partner)

    def w_copy(owner, i):
        part = ws.at[owner, pl.ds(pl.multiple_of(core * HALF, HALF), HEAD)]
        return remote(part, part, w_send.at[i], w_recv.at[owner], "head", peer_h(i))

    def w_share(owner, half):
        part = ws.at[owner, pl.ds(pl.multiple_of(half * HALF, HALF), HEAD)]
        return remote(part, part, ws_send.at[owner], ws_recv.at[owner], "seq", sibling)

    for n, turn in enumerate(turns):
        kv_copy(own, n, in_seq(x_lo, turn, core)).start()
    kv_copy(own, 3, sibling).start()
    loads[2].wait()
    q_p = nt(q_in[...], perm[...])
    q_pt = nt(perm[...], q_in[...])
    q_rows = []
    q_cols = []
    for r in range(RATE):
        at = (iota((128, ROWS), 1) * RATE + r).astype(F32)
        hot = jnp.where(hot_col & (at >= first_col) & (at < last_col), SAME, 0.0)
        q_rows.append(q_p[:, r * 128 : (r + 1) * 128])
        q_cols.append(q_pt[r * 128 : (r + 1) * 128, :] + hot)
    for j in reversed(range(RATE)):
        q_j = to_slot(q_rows, shift_row, j)
        q_jt = to_slot(q_cols, shift_col, j)
        q_n[0, j] = jnp.where(lane_row < HALF, q_j, 0.0).astype(BF16)
        q_n[1, j] = jnp.where(lane_row < HALF, 0.0, q_j).astype(BF16)
        if j == 3:
            at = (iota((ROWS, 128), 0) * RATE + shift_row).astype(F32)
            hot = jnp.where(hot_row & (at >= first_row) & (at < last_row), SAME, 0.0)
            q_far[...] = (q_j + hot).astype(BF16)
            swap(0, q_far, q_got).start()
        q_t[0, j] = jnp.where(lane_col < HALF, q_jt, 0.0).astype(BF16)
        q_t[1, j] = jnp.where(lane_col < HALF, 0.0, q_jt).astype(BF16)

    def forward(keys, vals, q_of, e_of, h):
        top = None
        for b in range(4):
            s = nn(keys(b), q_of)
            e_of[b] = s
            m = jnp.max(s, axis=0, keepdims=True)
            top = m if top is None else jnp.maximum(top, m)
        total = jnp.zeros((1, ROWS), F32)
        out = jnp.zeros((HALF, ROWS), F32)
        for b in range(4):
            e = jnp.exp2((e_of[b] - top) * EXP2)
            e_of[b] = e
            total = total + jnp.sum(e, axis=0, keepdims=True)
            v_t = vals(b).T[h * HALF : (h + 1) * HALF]
            out = out + nn(v_t, e.astype(BF16))
        return top, total, out

    halves = (slice(0, HALF), slice(HALF, 2 * HALF))

    @pl.loop(0, RATE)
    def _(j):
        for h in range(2):
            top, total, out = forward(
                lambda b: near_k[b], lambda b: near_v[b], q_t[h, j], e_near.at[h, j], h
            )
            top_n[h] = top
            sum_n[h] = total
            out_n[h] = out
            inverse = 1.0 / total
            fac_n[h, j] = inverse
            attn_t[j, halves[h]] = (out * inverse).astype(BF16)

        @pl.when(j == 0)
        def _():
            dy_copy(partner_h, 0, partner_h).wait_recv()
            for n, turn in enumerate((1, 3)):
                dy_copy(partner_h, 4 + n, in_head(x_hi, turn)).start()

    def share(i):
        slot = in_z(i + i // 2 - 2 * (i // 3), core)
        kv_copy(slot, 0, partner).wait_recv()
        kv_copy(slot, 3 + i, sibling).start()

    share(1)
    swap(0, q_far, q_got).wait_recv()
    q_j = q_got[...].astype(F32)
    q_jt = q_j.T
    q_n[0, 4] = jnp.where(lane_row < HALF, q_j, 0.0).astype(BF16)
    q_n[1, 4] = jnp.where(lane_row < HALF, 0.0, q_j).astype(BF16)
    q_t[0, 4] = jnp.where(lane_col < HALF, q_jt, 0.0).astype(BF16)
    q_t[1, 4] = jnp.where(lane_col < HALF, 0.0, q_jt).astype(BF16)

    def far_block(n):
        i = n // 2
        return in_z(i + i // 2 - 2 * (i // 3), lax.rem(n, 2))

    kv_copy(in_z(0, 1 - core), 0, partner).wait_recv()
    kv_copy(in_z(1, 1 - core), 0, partner).wait_recv()

    @pl.loop(0, 4)
    def _(step):
        g = lax.rem(step, 2)
        own_q = step // 2

        @pl.when(step == 1)
        def _():
            dy_copy(in_head(x_hi, 2), 0, partner_h).wait_recv()
            dy_copy(in_head(x_hi, 2), 6, partner_h).start()
            for i in (2, 3):
                share(i)
            for dz in (3, 2):
                kv_copy(in_z(dz, 1 - core), 0, partner).wait_recv()

        @pl.when(step == 2)
        def _():
            for h in range(2):
                top = jnp.maximum(top_f[0, h, 0], top_f[0, h, 1])
                w0 = jnp.exp2((top_f[0, h, 0] - top) * EXP2)
                w1 = jnp.exp2((top_f[0, h, 1] - top) * EXP2)
                m_far[h : h + 1] = top
                m_far[2 + h : 3 + h] = w0 * sum_f[0, h, 0] + w1 * sum_f[0, h, 1]
                o_far[halves[h]] = (w0 * out_f[0, h, 0] + w1 * out_f[0, h, 1]).astype(BF16)
            m_far[4:8] = jnp.zeros((4, ROWS), F32)
            swap(1, m_far, m_got).start()
            swap(2, o_far, o_got).start()

        for h in range(2):
            top, total, out = forward(
                lambda b: kv[far_block(4 * g + b), 0],
                lambda b: kv[far_block(4 * g + b), 1],
                q_t[h, 4 - own_q],
                e_far.at[own_q, h, pl.ds(4 * g, 4)],
                h,
            )
            top_f[own_q, h, g] = top
            sum_f[own_q, h, g] = total
            out_f[own_q, h, g] = out

    for turn in (1, 3):
        for x in range(2):
            dy_copy(in_head(x, turn), 0, partner_h).wait_recv()
    dy_copy(in_head(1 - x_hi, 2), 0, partner_h).wait_recv()
    loads[3].wait()
    loads[4].wait()
    loads[5].wait()
    zeros16 = jnp.zeros((16, WIDTH), BF16)
    for h in range(NHEAD):
        ws[h, 48:64] = zeros16
        ws[h, 112:128] = zeros16
    rm_row = iota((128, 128), 0)
    rm_col = iota((128, 128), 1)
    to_rm = jnp.where(rm_col == lax.rem(rm_row, 32) * RATE + rm_row // 32, 1.0, 0.0).astype(BF16)

    for h in range(NHEAD):
        rows = nn(to_rm, raw[h]).astype(BF16)
        for r in range(RATE):
            dys[r, h * 32 : (h + 1) * 32] = rows[r * 32 : (r + 1) * 32]
    w_own = ws[head]
    g_rows = []
    g_cols = []
    for r in range(RATE):
        g_rows.append(nt(dys[r], w_own))
        g_cols.append(nt(w_own, dys[r]))
    for j in reversed(range(RATE)):
        g_j = to_slot(g_rows, shift_row, j)
        g_jt = to_slot(g_cols, shift_col, j)
        g_n[0, j] = jnp.where(lane_row < HALF, g_j, 0.0).astype(BF16)
        g_n[1, j] = jnp.where(lane_row < HALF, 0.0, g_j).astype(BF16)
        g_t[0, j] = jnp.where(lane_col < HALF, g_jt, 0.0).astype(BF16)
        g_t[1, j] = jnp.where(lane_col < HALF, 0.0, g_jt).astype(BF16)
        if j == 3:
            g_far[...] = g_j.astype(BF16)
            swap(3, g_far, g_got).start()
    swap(1, m_far, m_got).wait_recv()
    swap(2, o_far, o_got).wait_recv()
    for h in range(2):
        tops = [top_n[h], top_f[1, h, 0], top_f[1, h, 1], m_got[h : h + 1]]
        sums = [sum_n[h], sum_f[1, h, 0], sum_f[1, h, 1], m_got[2 + h : 3 + h]]
        outs = [out_n[h], out_f[1, h, 0], out_f[1, h, 1], o_got[halves[h]].astype(F32)]
        top = tops[0]
        for other in tops[1:]:
            top = jnp.maximum(top, other)
        weights = [jnp.exp2((other - top) * EXP2) for other in tops]
        total = weights[0] * sums[0]
        out = weights[0] * outs[0]
        for n in range(1, 4):
            total = total + weights[n] * sums[n]
            out = out + weights[n] * outs[n]
        inverse = 1.0 / total
        fac_n[h, 3] = weights[0] * inverse
        for g in range(2):
            fac_f[1, h, g] = weights[1 + g] * inverse
        t_far[h : h + 1] = top
        t_far[2 + h : 3 + h] = inverse
        attn_t[3, halves[h]] = (out * inverse).astype(BF16)

    for j in range(RATE):
        for h in range(2):
            product = g_t[h, j, halves[h], :].astype(F32) * attn_t[j, halves[h]].astype(F32)
            delta[h, j] = jnp.sum(product, axis=0, keepdims=True)
    t_far[4:5] = delta[0, 3]
    t_far[5:6] = delta[1, 3]
    t_far[6:8] = jnp.zeros((2, ROWS), F32)
    swap(4, t_far, t_got).start()

    attn_slots = [attn_t[j].astype(F32) for j in range(RATE)]
    attn_rt = [from_slot(attn_slots, shift_col, r) for r in range(RATE)]
    for r in range(RATE):
        attn_n[r] = attn_rt[r].T.astype(BF16)

    own_rows = pl.ds(pl.multiple_of(head * 32, 32), 32)

    def at_copy(slot, i):
        rows = pl.ds(pl.multiple_of(peer_h(i) * 32, 32), 32)
        return remote(
            attn_n.at[:, rows, :], attn_r.at[slot], at_send.at[i], at_recv.at[slot], "head", peer_h(i)
        )

    for n in range(1, NHEAD):
        at_copy(head, n).start()
    for r in range(RATE):
        attn_r[head, r] = attn_n[r, own_rows, :]

    weight_grad = jnp.zeros((128, WIDTH), F32)
    for r in range(RATE):
        weight_grad = weight_grad + nn(attn_rt[r].astype(BF16), dys[r])

    for half in range(2):
        for n in range(8):
            dwp[half, n] = weight_grad[n * 16 : (n + 1) * 16, half * 384 : (half + 1) * 384]

    def dx_copy(half):
        return remote(dwp.at[half], dwx, dx_sem.at[0], dx_sem.at[1], "seq", sibling)

    def dw_copy(sender, i):
        dst = peer_c(i)
        return remote(dwm.at[dst], dwr.at[sender], dw_send.at[i], dw_recv.at[sender], "seq", at_chip(dst))

    def df_copy(sender, i):
        part = dwf.at[core, sender]
        return remote(part, part, df_send.at[i], df_recv.at[sender], "seq", at_chip(peer_c(i)))

    def dc_copy(half):
        return remote(dwf.at[half], dwf.at[half], dc_sem.at[0], dc_sem.at[1], "seq", sibling)

    dx_copy(1 - core).start()

    def weight_over_cores():
        dx_copy(core).wait_recv()
        dwm[...] = dwp[core] + dwx[...]
        for n in range(1, 8):
            dw_copy(chip, n).start()

    def weight_over_chips():
        for n in range(1, 8):
            dw_copy(peer_c(n), n).wait_recv()
        dwr[chip] = dwm[chip]
        part = dwr[0]
        for n in range(1, 8):
            part = part + dwr[n]
        dwf[core, chip] = part.astype(BF16)
        for n in range(1, 8):
            df_copy(chip, n).start()

    def weight_to_sibling():
        for n in range(1, 8):
            df_copy(peer_c(n), n).wait_recv()
        dc_copy(core).start()

    def backward(count, keys, vals, queries, e_of, factor, put):
        dq = [[jnp.zeros((HALF, ROWS), F32) for h in range(2)] for _ in queries]
        for b in range(count):
            k_t = keys(b).T
            val = vals(b)
            dk = jnp.zeros((ROWS, 128), F32)
            dv = jnp.zeros((ROWS, 128), F32)
            for n, j in enumerate(queries):
                for h in range(2):
                    p = e_of(n, h, b) * factor(n, h)
                    ds = (p * (nn(val, g_t[h, j]) - delta[h, j])).astype(BF16)
                    dv = dv + nn(p.astype(BF16), g_n[h, j])
                    dk = dk + nn(ds, q_n[h, j])
                    dq[n][h] = dq[n][h] + nn(k_t[halves[h]], ds)
            put(b, dk, dv)
        return dq

    acc_k[...] = jnp.zeros((4, ROWS, 128), F32)
    acc_v[...] = jnp.zeros((4, ROWS, 128), F32)

    def near_backward(j):
        def put(b, dk, dv):
            acc_k[b] = acc_k[b] + dk
            acc_v[b] = acc_v[b] + dv

        dq = backward(
            4,
            lambda b: near_k[b],
            lambda b: near_v[b],
            [j],
            lambda n, h, b: e_near[h, j, b],
            lambda n, h: fac_n[h, j],
            put,
        )
        for h in range(2):
            acc_q[j, halves[h]] = dq[0][h]

    @pl.loop(0, EARLY)
    def _(j):
        near_backward(j)

        @pl.when(j == 0)
        def _():
            weight_over_cores()

    swap(3, g_far, g_got).wait_recv()
    swap(4, t_far, t_got).wait_recv()
    g_j = g_got[...].astype(F32)
    g_jt = g_j.T
    g_n[0, 4] = jnp.where(lane_row < HALF, g_j, 0.0).astype(BF16)
    g_n[1, 4] = jnp.where(lane_row < HALF, 0.0, g_j).astype(BF16)
    g_t[0, 4] = jnp.where(lane_col < HALF, g_jt, 0.0).astype(BF16)
    g_t[1, 4] = jnp.where(lane_col < HALF, 0.0, g_jt).astype(BF16)
    for h in range(2):
        delta[h, 4] = t_got[4 + h : 5 + h]
        for g in range(2):
            weight = jnp.exp2((top_f[0, h, g] - t_got[h : h + 1]) * EXP2)
            fac_f[0, h, g] = weight * t_got[2 + h : 3 + h]

    def gx_copy(slot):
        return remote(
            gkv_s.at[slot], gkv_x.at[slot], gx_send.at[slot], gx_recv.at[slot], "seq", sibling
        )

    def grad_copy(dz):
        return remote(
            gkv_s.at[in_z(dz, core)],
            gkv_r.at[dz],
            g_send.at[dz],
            g_recv.at[dz],
            "seq",
            in_seq(x_lo, dz, core),
        )

    def merge(i):
        dz = i + i // 2 - 2 * (i // 3)
        slot = in_z(dz, core)
        gx_copy(slot).wait_recv()
        for n in range(2):
            gkv_s[slot, n] = (gkv_s[slot, n].astype(F32) + gkv_x[slot, n].astype(F32)).astype(BF16)

        @pl.when(dz != 0)
        def _():
            grad_copy(dz).start()

    for j in (3, 4):
        acc_q[j] = jnp.zeros((128, ROWS), F32)

    @pl.loop(0, 4)
    def _(back):
        i = 3 - back
        dz = i + i // 2 - 2 * (i // 3)

        def put(b, dk, dv):
            slot = in_z(dz, b)
            gkv_s[slot, 0] = dk.astype(BF16)
            gkv_s[slot, 1] = dv.astype(BF16)

            @pl.when(core != b)
            def _():
                gx_copy(slot).start()

        dq = backward(
            2,
            lambda b: kv[in_z(dz, b), 0],
            lambda b: kv[in_z(dz, b), 1],
            [4, 3],
            lambda n, h, b: e_far[n, h, 2 * i + b],
            lambda n, h: fac_f[n, h, i // 2],
            put,
        )
        for n, j in enumerate((4, 3)):
            for h in range(2):
                acc_q[j, halves[h]] = acc_q[j, halves[h]] + dq[n][h]

        @pl.when(back > 0)
        def _():
            merge(i + 1)

        @pl.when(back == 0)
        def _():
            for n in range(1, NHEAD):
                w_copy(head, n).start()

        @pl.when(back == 2)
        def _():
            weight_over_chips()

    dq_far[...] = acc_q[4].astype(BF16)
    swap(5, dq_far, dq_got).start()
    acc_q[4] = acc_q[3]
    merge(0)

    @pl.loop(EARLY, RATE)
    def _(j):
        near_backward(j)

    for n in range(1, NHEAD):
        w_copy(peer_h(n), n).wait_recv()
        w_share(peer_h(n), core).start()
    swap(5, dq_far, dq_got).wait_recv()
    acc_q[3] = acc_q[3] + acc_q[4] + dq_got[...].astype(F32)
    dq_slots = [(acc_q[j] * SCALE).T for j in range(RATE)]
    dq_parts = [from_slot(dq_slots, shift_row, r).astype(BF16) for r in range(RATE)]
    dq_ref[...] = nn(jnp.concatenate(dq_parts, axis=1), perm[...]).astype(BF16)

    weight_to_sibling()
    for n in range(1, NHEAD):
        w_share(peer_h(n), 1 - core).wait_recv()
        at_copy(peer_h(n), n).wait_recv()
    from_rm = jnp.where(rm_row == lax.rem(rm_col, 32) * RATE + rm_col // 32, 1.0, 0.0).astype(BF16)
    result = jnp.zeros((128, WIDTH), F32)
    for h in range(NHEAD):
        rows = nn(from_rm, attn_r[h].reshape(128, 128)).astype(BF16)
        result = result + nn(rows, ws[h])
    lo_ref[...] = result.astype(BF16)

    for turn in turns:
        grad_copy(turn).wait_recv()
    far = []
    for n in range(2):
        total = gkv_s[own, n].astype(F32)
        for turn in turns:
            total = total + gkv_r[turn, n].astype(F32)
        far.append(total)
    sum_k, sum_v = far
    dk_parts = []
    dv_parts = []
    for r in range(RATE):
        mine = shift_row == r
        dk_parts.append(((acc_k[r] + jnp.where(mine, sum_k, 0.0)) * SCALE).astype(BF16))
        dv_parts.append((acc_v[r] + jnp.where(mine, sum_v, 0.0)).astype(BF16))
    dk_ref[...] = nn(jnp.concatenate(dk_parts, axis=1), perm[...]).astype(BF16)
    dv_ref[...] = nn(jnp.concatenate(dv_parts, axis=1), perm[...]).astype(BF16)

    dc_copy(1 - core).wait_recv()
    for half in range(2):
        whole = dwf[half].reshape(128, 384)
        dw_ref[0:48, half * 384 : (half + 1) * 384] = whole[0:48]
        dw_ref[48:96, half * 384 : (half + 1) * 384] = whole[64:112]

    dx_copy(1 - core).wait_send()
    dc_copy(core).wait_send()

    @pl.loop(0, 7)
    def _(i):
        kv_copy(own, i, partner).wait_send()

    @pl.loop(1, 8)
    def _(i):
        w_copy(head, i).wait_send()
        w_share(peer_h(i), core).wait_send()
        dy_copy(head, i - 1, partner_h).wait_send()
        at_copy(head, i).wait_send()
        dw_copy(chip, i).wait_send()
        df_copy(chip, i).wait_send()

    @pl.loop(0, 4)
    def _(i):
        gx_copy(i * 2 + 1 - core).wait_send()

    for turn in turns:
        grad_copy(turn).wait_send()
    swaps = ((q_far, q_got), (m_far, m_got), (o_far, o_got), (g_far, g_got), (t_far, t_got), (dq_far, dq_got))
    for i, (source, target) in enumerate(swaps):
        swap(i, source, target).wait_send()


def finish(*refs):
    for source, target in zip(refs[:5], refs[5:], strict=True):
        target[...] = source[...]


def body(queries, keys, values, slide_ids, head_shift_list, out_weight, d_y):
    vmem = pl.BlockSpec(memory_space=pltpu.VMEM)
    hbm = pl.BlockSpec(memory_space=pltpu.HBM)
    smem = pl.BlockSpec(memory_space=pltpu.SMEM)
    sems = pltpu.SemaphoreType.DMA
    results = pl.pallas_call(
        kernel,
        out_shape=(
            jax.ShapeDtypeStruct((128, WIDTH), BF16),
            jax.ShapeDtypeStruct((ROWS, 384), BF16),
            jax.ShapeDtypeStruct((ROWS, 384), BF16),
            jax.ShapeDtypeStruct((ROWS, 384), BF16),
            jax.ShapeDtypeStruct((96, WIDTH), BF16),
        ),
        in_specs=[hbm, hbm, hbm, vmem, smem, hbm, hbm],
        out_specs=(vmem,) * 5,
        scratch_shapes=[
            pltpu.VMEM((ROWS, 384), BF16),
            pltpu.VMEM((ROWS, 384), BF16),
            pltpu.VMEM((ROWS, 384), BF16),
            pltpu.VMEM((NHEAD, 128, WIDTH), BF16),
            pltpu.VMEM((4 * 128, 384), BF16),
            pltpu.VMEM((4, ROWS, 128), BF16),
            pltpu.VMEM((4, ROWS, 128), BF16),
            pltpu.VMEM((8, 2, ROWS, 128), BF16),
            pltpu.VMEM((2, 5, 128, ROWS), BF16),
            pltpu.VMEM((2, 5, ROWS, 128), BF16),
            pltpu.VMEM((2, 5, 128, ROWS), BF16),
            pltpu.VMEM((2, 5, ROWS, 128), BF16),
            pltpu.VMEM((2, RATE, 4, ROWS, ROWS), F32),
            pltpu.VMEM((2, 2, 8, ROWS, ROWS), F32),
            pltpu.VMEM((2, 1, ROWS), F32),
            pltpu.VMEM((2, 1, ROWS), F32),
            pltpu.VMEM((2, HALF, ROWS), F32),
            pltpu.VMEM((2, 2, 2, 1, ROWS), F32),
            pltpu.VMEM((2, 2, 2, 1, ROWS), F32),
            pltpu.VMEM((2, 2, 2, HALF, ROWS), F32),
            pltpu.VMEM((2, RATE, 1, ROWS), F32),
            pltpu.VMEM((2, 2, 2, 1, ROWS), F32),
            pltpu.VMEM((2, 5, 1, ROWS), F32),
            pltpu.VMEM((RATE, 128, ROWS), BF16),
            pltpu.VMEM((RATE, ROWS, 128), BF16),
            pltpu.VMEM((NHEAD, RATE, 32, 128), BF16),
            pltpu.VMEM((RATE, ROWS, WIDTH), BF16),
            pltpu.VMEM((NHEAD, 128, WIDTH), BF16),
            pltpu.VMEM((2, 8, 16, 384), F32),
            pltpu.VMEM((8, 16, 384), F32),
            pltpu.VMEM((8, 16, 384), F32),
            pltpu.VMEM((8, 16, 384), F32),
            pltpu.VMEM((2, 8, 16, 384), BF16),
            pltpu.VMEM((8, 2, ROWS, 128), BF16),
            pltpu.VMEM((8, 2, ROWS, 128), BF16),
            pltpu.VMEM((4, 2, ROWS, 128), BF16),
            pltpu.VMEM((ROWS, 128), BF16),
            pltpu.VMEM((ROWS, 128), BF16),
            pltpu.VMEM((ROWS, 128), BF16),
            pltpu.VMEM((ROWS, 128), BF16),
            pltpu.VMEM((128, ROWS), BF16),
            pltpu.VMEM((128, ROWS), BF16),
            pltpu.VMEM((8, ROWS), F32),
            pltpu.VMEM((8, ROWS), F32),
            pltpu.VMEM((8, ROWS), F32),
            pltpu.VMEM((8, ROWS), F32),
            pltpu.VMEM((128, ROWS), BF16),
            pltpu.VMEM((128, ROWS), BF16),
            pltpu.VMEM((4, ROWS, 128), F32),
            pltpu.VMEM((4, ROWS, 128), F32),
            pltpu.VMEM((5, 128, ROWS), F32),
            sems((6,)),
            sems((8,)),
            sems((8,)),
            sems((NHEAD,)),
            sems((NHEAD,)),
            sems((NHEAD,)),
            sems((NHEAD,)),
            sems((NHEAD,)),
            sems((NHEAD,)),
            sems((NHEAD,)),
            sems((NHEAD,)),
            sems((2,)),
            sems((8,)),
            sems((8,)),
            sems((8,)),
            sems((8,)),
            sems((2,)),
            sems((8,)),
            sems((8,)),
            sems((4,)),
            sems((4,)),
            sems((6,)),
            sems((6,)),
        ],
        compiler_params=pltpu.CompilerParams(
            collective_id=0, has_side_effects=True, vmem_limit_bytes=56 * 1024 * 1024
        ),
        cost_estimate=pl.CostEstimate(
            flops=3_000_000_000, bytes_accessed=4_000_000, transcendentals=5_000_000
        ),
    )(
        queries,
        keys,
        values,
        slide_ids.reshape(8, 128),
        head_shift_list,
        out_weight,
        d_y,
    )
    return pl.pallas_call(
        finish,
        out_shape=tuple(jax.ShapeDtypeStruct(r.shape, r.dtype) for r in results),
        in_specs=[vmem] * 5,
        out_specs=(vmem,) * 5,
    )(*results)


def solution(mesh):
    placed = (
        P("seq", "head"),
        P("seq", "head"),
        P("seq", "head"),
        P("seq"),
        P(),
        P("head", None),
        P(("seq", "head"), None),
    )
    return jax.shard_map(
        body,
        mesh=mesh,
        in_specs=placed,
        out_specs=(
            P(("seq", "head"), None),
            P("seq", "head"),
            P("seq", "head"),
            P("seq", "head"),
            P("head", None),
        ),
        check_vma=False,
    )
```

```python
import math

import jax
import jax.numpy as jnp
from jax import lax
from jax.experimental import pallas as pl
from jax.experimental.pallas import tpu as pltpu
from jax.sharding import PartitionSpec as P

HEAD = 48
HALF = 64
RATE = 4
ROWS = 256
WIDTH = 768
NSEQ = 16
NHEAD = 8
EARLY = 2
SAME = 8192.0
SCALE = 1.0 / math.sqrt(HEAD)
EXP2 = SCALE * math.log2(math.e)
F32 = jnp.float32
BF16 = jnp.bfloat16


def nt(a, b):
    return lax.dot_general(a, b, (((1,), (1,)), ((), ())), preferred_element_type=F32)


def nn(a, b):
    return jnp.dot(a, b, preferred_element_type=F32)


def iota(shape, dim):
    return lax.broadcasted_iota(jnp.int32, shape, dim)


def remote(src, dst, send, recv, axis, index):
    return pltpu.make_async_remote_copy(
        src_ref=src,
        dst_ref=dst,
        send_sem=send,
        recv_sem=recv,
        device_id={axis: index},
        device_id_type=pl.DeviceIdType.MESH,
    )


def kernel(
    q_ref,
    k_ref,
    v_ref,
    id_ref,
    shift_ref,
    w_ref,
    dy_ref,
    lo_ref,
    dq_ref,
    dk_ref,
    dv_ref,
    dw_ref,
    q_in,
    k_in,
    v_in,
    raw,
    perm,
    near_k,
    near_v,
    near_kt,
    near_vt,
    kv,
    far_vt,
    g_raw,
    q_t,
    q_n,
    g_t,
    g_n,
    e_near,
    e_far,
    top_n,
    sum_n,
    out_n,
    top_f,
    sum_f,
    out_f,
    fac_n,
    fac_f,
    delta,
    attn_t,
    attn_n,
    attn_r,
    dys,
    ws,
    dwp,
    dwx,
    dwm,
    dwr,
    dwf,
    gkv_s,
    gkv_x,
    gkv_r,
    q_far,
    q_got,
    g_far,
    g_got,
    o_far,
    o_got,
    m_far,
    m_got,
    t_far,
    t_got,
    dq_far,
    dq_got,
    acc_k,
    acc_v,
    acc_q,
    in_sem,
    kv_send,
    kv_recv,
    dy_send,
    dy_recv,
    w_send,
    w_recv,
    ws_send,
    ws_recv,
    at_send,
    at_recv,
    dx_sem,
    dw_send,
    dw_recv,
    df_send,
    df_recv,
    dc_sem,
    gx_send,
    gx_recv,
    g_send,
    g_recv,
    swap_send,
    swap_recv,
):
    seq = lax.axis_index("seq")
    head = lax.axis_index("head")

    x_lo, z, core = seq // 8, lax.rem(seq // 2, 4), lax.rem(seq, 2)
    x_hi, y = head // 4, lax.rem(head, 4)
    chip = seq // 2

    def at_chip(j):
        return j * 2 + core

    def in_seq(x, dz, c):
        return x * 8 + lax.rem(z + dz, 4) * 2 + c

    def in_z(dz, c):
        return lax.rem(z + dz, 4) * 2 + c

    def in_head(x, dy):
        return x * 4 + lax.rem(y + dy, 4)

    def peer_c(i):
        return lax.rem(chip + i, 8)

    def peer_h(i):
        return lax.rem(head + i, NHEAD)

    sibling = in_seq(x_lo, 0, 1 - core)
    partner = in_seq(1 - x_lo, 0, core)
    partner_h = in_head(1 - x_hi, 0)
    turns = (1, 3, 2)

    barrier = pltpu.get_barrier_semaphore()
    pl.semaphore_signal(
        barrier, inc=1, device_id={"seq": sibling}, device_id_type=pl.DeviceIdType.MESH
    )

    @pl.loop(1, 8)
    def _(i):
        pl.semaphore_signal(
            barrier,
            inc=1,
            device_id={"seq": at_chip(peer_c(i))},
            device_id_type=pl.DeviceIdType.MESH,
        )
        pl.semaphore_signal(
            barrier, inc=1, device_id={"head": peer_h(i)}, device_id_type=pl.DeviceIdType.MESH
        )

    loads = [
        pltpu.make_async_copy(source, target, in_sem.at[n])
        for n, (source, target) in enumerate(
            (
                (k_ref, k_in),
                (v_ref, v_in),
                (q_ref, q_in),
                (dy_ref, raw.at[head]),
                (w_ref.at[0:48], ws.at[head, 0:48]),
                (w_ref.at[48:96], ws.at[head, 64:112]),
            )
        )
    ]
    for load in loads:
        load.start()

    slide_col = lax.rem(iota((128, 128), 0), HALF) - HEAD
    below = jnp.zeros((128, 128), F32)
    upto = jnp.zeros((128, 128), F32)
    for s in range(8):
        ids = id_ref[s : s + 1, :]
        below = below + jnp.where(ids < slide_col, 1.0, 0.0)
        upto = upto + jnp.where(ids <= slide_col, 1.0, 0.0)
    ones = jnp.ones((8, 128), BF16)
    first_row = nt(ones, below.astype(BF16))[0:1, :]
    last_row = nt(ones, upto.astype(BF16))[0:1, :]
    first_col = jnp.sum(below, axis=1, keepdims=True)
    last_col = jnp.sum(upto, axis=1, keepdims=True)

    shift0 = shift_ref[2 * head]
    shift1 = shift_ref[2 * head + 1]
    lane_row = iota((1, 128), 1)
    lane_col = iota((128, 1), 0)
    shift_row = jnp.where(lane_row < HALF, shift0, shift1)
    shift_col = jnp.where(lane_col < HALF, shift0, shift1)
    hot_row = lax.rem(lane_row, HALF) >= HEAD
    hot_col = lax.rem(lane_col, HALF) >= HEAD

    def turned(shift, j):
        return jnp.bitwise_and(shift + 1 + j, RATE - 1)

    def to_slot(parts, shift, j):
        out = parts[0]
        for r in range(1, RATE):
            out = jnp.where(turned(shift, j) == r, parts[r], out)
        return out

    def from_slot(parts, shift, r):
        out = parts[0]
        for j in range(1, RATE):
            out = jnp.where(turned(shift, j) == r, parts[j], out)
        return out

    within = lax.rem(lane_col, HALF)
    source = (lane_col // HALF) * (RATE * HEAD) + within
    given = iota((128, 384), 1)
    for r in range(RATE):
        held = jnp.where(within < HEAD, source + r * HEAD, -1)
        perm[r * 128 : (r + 1) * 128] = jnp.where(given == held, 1.0, 0.0).astype(BF16)
    pl.semaphore_wait(barrier, 15)

    def dy_copy(owner, i, dst, first=False):
        source = dy_ref if first else raw.at[owner]
        return remote(source, raw.at[owner], dy_send.at[i], dy_recv.at[owner], "head", dst)

    dy_copy(head, 0, partner_h, True).start()
    dy_copy(head, 1, in_head(x_hi, 2), True).start()

    loads[0].wait()
    loads[1].wait()
    k_p = nt(k_in[...], perm[...])
    v_p = nt(v_in[...], perm[...])
    one_row = jnp.where(lax.rem(lane_row, HALF) == HEAD, 1.0, 0.0)
    one_col = jnp.where(lax.rem(lane_col, HALF) == HEAD, 1.0, 0.0)
    far_k = jnp.zeros((ROWS, 128), F32)
    far_v = jnp.zeros((ROWS, 128), F32)
    for r in range(RATE):
        at = (iota((ROWS, 128), 0) * RATE + r).astype(F32)
        hot = jnp.where(hot_row & (at >= first_row) & (at < last_row), 1.0, 0.0)
        k_r = k_p[:, r * 128 : (r + 1) * 128] + hot
        v_r = v_p[:, r * 128 : (r + 1) * 128] + one_row
        near_k[r] = k_r.astype(BF16)
        near_v[r] = v_r.astype(BF16)
        far_k = jnp.where(shift_row == r, k_r, far_k)
        far_v = jnp.where(shift_row == r, v_r, far_v)
    own = in_z(0, core)
    kv[own, 0] = far_k.astype(BF16)
    kv[own, 1] = far_v.astype(BF16)

    def kv_copy(slot, i, dst):
        return remote(kv.at[slot], kv.at[slot], kv_send.at[i], kv_recv.at[slot], "seq", dst)

    def swap(i, source, target):
        return remote(source, target, swap_send.at[i], swap_recv.at[i], "seq", partner)

    def w_copy(owner, i):
        part = ws.at[owner, pl.ds(pl.multiple_of(core * HALF, HALF), HEAD)]
        return remote(part, part, w_send.at[i], w_recv.at[owner], "head", peer_h(i))

    def w_share(owner, half):
        part = ws.at[owner, pl.ds(pl.multiple_of(half * HALF, HALF), HEAD)]
        return remote(part, part, ws_send.at[owner], ws_recv.at[owner], "seq", sibling)

    for n, turn in enumerate(turns):
        kv_copy(own, n, in_seq(x_lo, turn, core)).start()
    kv_copy(own, 3, sibling).start()
    for n, turn in enumerate((1, 3)):
        dy_copy(head, 2 + n, in_head(x_hi, turn), True).start()
    loads[2].wait()
    q_p = nt(q_in[...], perm[...])
    q_pt = nt(perm[...], q_in[...])
    k_pt = nt(perm[...], k_in[...])
    v_pt = nt(perm[...], v_in[...])
    for r in range(RATE):
        near_kt[r] = k_pt[r * 128 : (r + 1) * 128].astype(BF16)
        near_vt[r] = (v_pt[r * 128 : (r + 1) * 128] + one_col).astype(BF16)
    q_rows = []
    q_cols = []
    for r in range(RATE):
        at = (iota((128, ROWS), 1) * RATE + r).astype(F32)
        hot = jnp.where(hot_col & (at >= first_col) & (at < last_col), SAME, 0.0)
        q_rows.append(q_p[:, r * 128 : (r + 1) * 128])
        q_cols.append(q_pt[r * 128 : (r + 1) * 128, :] + hot)
    for j in reversed(range(RATE)):
        q_j = to_slot(q_rows, shift_row, j)
        q_jt = to_slot(q_cols, shift_col, j)
        q_n[0, j] = jnp.where(lane_row < HALF, q_j, 0.0).astype(BF16)
        q_n[1, j] = jnp.where(lane_row < HALF, 0.0, q_j).astype(BF16)
        if j == 3:
            at = (iota((ROWS, 128), 0) * RATE + shift_row).astype(F32)
            hot = jnp.where(hot_row & (at >= first_row) & (at < last_row), SAME, 0.0)
            q_far[...] = (q_j + hot).astype(BF16)
            swap(0, q_far, q_got).start()
        q_t[0, j] = jnp.where(lane_col < HALF, q_jt, 0.0).astype(BF16)
        q_t[1, j] = jnp.where(lane_col < HALF, 0.0, q_jt).astype(BF16)

    def forward(keys, vals_t, q_of, e_of, h):
        top = None
        for b in range(4):
            s = nn(keys(b), q_of)
            e_of[b] = s
            m = jnp.max(s, axis=0, keepdims=True)
            top = m if top is None else jnp.maximum(top, m)
        out = jnp.zeros((HALF, ROWS), F32)
        for b in range(4):
            e = jnp.exp2((e_of[b] - top) * EXP2)
            e_of[b] = e
            out = out + nn(vals_t(b)[h * HALF : (h + 1) * HALF], e.astype(BF16))
        return top, out[HEAD : HEAD + 1], out

    halves = (slice(0, HALF), slice(HALF, 2 * HALF))

    @pl.loop(0, RATE)
    def _(j):
        for h in range(2):
            top, total, out = forward(
                lambda b: near_k[b], lambda b: near_vt[b], q_t[h, j], e_near.at[h, j], h
            )
            top_n[h] = top
            sum_n[h] = total
            out_n[h] = out
            inverse = 1.0 / total
            fac_n[h, j] = inverse
            attn_t[j, halves[h]] = (out * inverse).astype(BF16)

        @pl.when(j == 0)
        def _():
            dy_copy(partner_h, 0, partner_h).wait_recv()
            for n, turn in enumerate((1, 3)):
                dy_copy(partner_h, 4 + n, in_head(x_hi, turn)).start()
            dy_copy(in_head(x_hi, 2), 0, partner_h).wait_recv()
            dy_copy(in_head(x_hi, 2), 6, partner_h).start()

    def share(i):
        slot = in_z(i + i // 2 - 2 * (i // 3), core)
        kv_copy(slot, 0, partner).wait_recv()
        kv_copy(slot, 3 + i, sibling).start()

    share(1)
    swap(0, q_far, q_got).wait_recv()
    q_j = q_got[...].astype(F32)
    q_jt = q_j.T
    q_n[0, 4] = jnp.where(lane_row < HALF, q_j, 0.0).astype(BF16)
    q_n[1, 4] = jnp.where(lane_row < HALF, 0.0, q_j).astype(BF16)
    q_t[0, 4] = jnp.where(lane_col < HALF, q_jt, 0.0).astype(BF16)
    q_t[1, 4] = jnp.where(lane_col < HALF, 0.0, q_jt).astype(BF16)

    def far_block(n):
        i = n // 2
        return in_z(i + i // 2 - 2 * (i // 3), lax.rem(n, 2))

    kv_copy(in_z(0, 1 - core), 0, partner).wait_recv()
    kv_copy(in_z(1, 1 - core), 0, partner).wait_recv()

    def turn_values(g):
        for b in range(4):
            far_vt[4 * g + b] = kv[far_block(4 * g + b), 1].T

    turn_values(0)

    @pl.loop(0, 4)
    def _(step):
        g = lax.rem(step, 2)
        own_q = step // 2

        @pl.when(step == 1)
        def _():
            for i in (2, 3):
                share(i)
            for dz in (3, 2):
                kv_copy(in_z(dz, 1 - core), 0, partner).wait_recv()
            turn_values(1)

        @pl.when(step == 2)
        def _():
            for h in range(2):
                top = jnp.maximum(top_f[0, h, 0], top_f[0, h, 1])
                w0 = jnp.exp2((top_f[0, h, 0] - top) * EXP2)
                w1 = jnp.exp2((top_f[0, h, 1] - top) * EXP2)
                m_far[h : h + 1] = top
                m_far[2 + h : 3 + h] = w0 * sum_f[0, h, 0] + w1 * sum_f[0, h, 1]
                o_far[halves[h]] = (w0 * out_f[0, h, 0] + w1 * out_f[0, h, 1]).astype(BF16)
            m_far[4:8] = jnp.zeros((4, ROWS), F32)
            swap(1, m_far, m_got).start()
            swap(2, o_far, o_got).start()

        for h in range(2):
            top, total, out = forward(
                lambda b: kv[far_block(4 * g + b), 0],
                lambda b: far_vt[4 * g + b],
                q_t[h, 4 - own_q],
                e_far.at[own_q, h, pl.ds(4 * g, 4)],
                h,
            )
            top_f[own_q, h, g] = top
            sum_f[own_q, h, g] = total
            out_f[own_q, h, g] = out

    for turn in (1, 3):
        for x in range(2):
            dy_copy(in_head(x, turn), 0, partner_h).wait_recv()
    dy_copy(in_head(1 - x_hi, 2), 0, partner_h).wait_recv()
    loads[3].wait()
    loads[4].wait()
    loads[5].wait()
    zeros16 = jnp.zeros((16, WIDTH), BF16)
    for h in range(NHEAD):
        ws[h, 48:64] = zeros16
        ws[h, 112:128] = zeros16
    rm_row = iota((128, 128), 0)
    rm_col = iota((128, 128), 1)
    to_rm = jnp.where(rm_col == lax.rem(rm_row, 32) * RATE + rm_row // 32, 1.0, 0.0).astype(BF16)

    for h in range(NHEAD):
        rows = nn(to_rm, raw[h]).astype(BF16)
        for r in range(RATE):
            dys[r, h * 32 : (h + 1) * 32] = rows[r * 32 : (r + 1) * 32]
    w_own = ws[head]
    g_rows = []
    g_cols = []
    for r in range(RATE):
        g_rows.append(nt(dys[r], w_own))
        g_cols.append(nt(w_own, dys[r]))
    for j in reversed(range(RATE)):
        g_j = to_slot(g_rows, shift_row, j)
        g_jt = to_slot(g_cols, shift_col, j)
        g_n[0, j] = jnp.where(lane_row < HALF, g_j, 0.0).astype(BF16)
        g_n[1, j] = jnp.where(lane_row < HALF, 0.0, g_j).astype(BF16)
        g_t[0, j] = jnp.where(lane_col < HALF, g_jt, 0.0).astype(BF16)
        g_t[1, j] = jnp.where(lane_col < HALF, 0.0, g_jt).astype(BF16)
        if j == 3:
            g_far[...] = g_j.astype(BF16)
            swap(3, g_far, g_got).start()
    swap(1, m_far, m_got).wait_recv()
    swap(2, o_far, o_got).wait_recv()
    for h in range(2):
        tops = [top_n[h], top_f[1, h, 0], top_f[1, h, 1], m_got[h : h + 1]]
        sums = [sum_n[h], sum_f[1, h, 0], sum_f[1, h, 1], m_got[2 + h : 3 + h]]
        outs = [out_n[h], out_f[1, h, 0], out_f[1, h, 1], o_got[halves[h]].astype(F32)]
        top = tops[0]
        for other in tops[1:]:
            top = jnp.maximum(top, other)
        weights = [jnp.exp2((other - top) * EXP2) for other in tops]
        total = weights[0] * sums[0]
        out = weights[0] * outs[0]
        for n in range(1, 4):
            total = total + weights[n] * sums[n]
            out = out + weights[n] * outs[n]
        inverse = 1.0 / total
        fac_n[h, 3] = weights[0] * inverse
        for g in range(2):
            fac_f[1, h, g] = weights[1 + g] * inverse
        t_far[h : h + 1] = top
        t_far[2 + h : 3 + h] = inverse
        attn_t[3, halves[h]] = (out * inverse).astype(BF16)

    for j in range(RATE):
        for h in range(2):
            product = g_t[h, j, halves[h], :].astype(F32) * attn_t[j, halves[h]].astype(F32)
            delta[h, j] = jnp.sum(product, axis=0, keepdims=True)
    t_far[4:5] = delta[0, 3]
    t_far[5:6] = delta[1, 3]
    t_far[6:8] = jnp.zeros((2, ROWS), F32)
    swap(4, t_far, t_got).start()

    attn_slots = [attn_t[j].astype(F32) for j in range(RATE)]
    attn_rt = [from_slot(attn_slots, shift_col, r) for r in range(RATE)]
    for r in range(RATE):
        attn_n[r] = attn_rt[r].T.astype(BF16)

    own_rows = pl.ds(pl.multiple_of(head * 32, 32), 32)

    def at_copy(slot, i):
        rows = pl.ds(pl.multiple_of(peer_h(i) * 32, 32), 32)
        return remote(
            attn_n.at[:, rows, :], attn_r.at[slot], at_send.at[i], at_recv.at[slot], "head", peer_h(i)
        )

    for n in range(1, NHEAD):
        at_copy(head, n).start()
    for r in range(RATE):
        attn_r[head, r] = attn_n[r, own_rows, :]

    weight_grad = jnp.zeros((128, WIDTH), F32)
    for r in range(RATE):
        weight_grad = weight_grad + nn(attn_rt[r].astype(BF16), dys[r])

    for half in range(2):
        for n in range(8):
            dwp[half, n] = weight_grad[n * 16 : (n + 1) * 16, half * 384 : (half + 1) * 384]

    def dx_copy(half):
        return remote(dwp.at[half], dwx, dx_sem.at[0], dx_sem.at[1], "seq", sibling)

    def dw_copy(sender, i):
        dst = peer_c(i)
        return remote(dwm.at[dst], dwr.at[sender], dw_send.at[i], dw_recv.at[sender], "seq", at_chip(dst))

    def df_copy(sender, i):
        part = dwf.at[core, sender]
        return remote(part, part, df_send.at[i], df_recv.at[sender], "seq", at_chip(peer_c(i)))

    def dc_copy(half):
        return remote(dwf.at[half], dwf.at[half], dc_sem.at[0], dc_sem.at[1], "seq", sibling)

    dx_copy(1 - core).start()

    def weight_over_cores():
        dx_copy(core).wait_recv()
        dwm[...] = dwp[core] + dwx[...]
        for n in range(1, 8):
            dw_copy(chip, n).start()

    def weight_over_chips():
        for n in range(1, 8):
            dw_copy(peer_c(n), n).wait_recv()
        dwr[chip] = dwm[chip]
        part = dwr[0]
        for n in range(1, 8):
            part = part + dwr[n]
        dwf[core, chip] = part.astype(BF16)
        for n in range(1, 8):
            df_copy(chip, n).start()

    def weight_to_sibling():
        for n in range(1, 8):
            df_copy(peer_c(n), n).wait_recv()
        dc_copy(core).start()

    def backward(count, keys_t, vals, queries, e_of, factor, put):
        dq = [[jnp.zeros((HALF, ROWS), F32) for h in range(2)] for _ in queries]
        for b in range(count):
            k_t = keys_t(b)
            val = vals(b)
            dk = jnp.zeros((ROWS, 128), F32)
            dv = jnp.zeros((ROWS, 128), F32)
            for n, j in enumerate(queries):
                for h in range(2):
                    p = e_of(n, h, b) * factor(n, h)
                    ds = (p * (nn(val, g_t[h, j]) - delta[h, j])).astype(BF16)
                    dv = dv + nn(p.astype(BF16), g_n[h, j])
                    dk = dk + nn(ds, q_n[h, j])
                    dq[n][h] = dq[n][h] + nn(k_t[halves[h]], ds)
            put(b, dk, dv)
        return dq

    acc_k[...] = jnp.zeros((4, ROWS, 128), F32)
    acc_v[...] = jnp.zeros((4, ROWS, 128), F32)

    def near_backward(j):
        def put(b, dk, dv):
            acc_k[b] = acc_k[b] + dk
            acc_v[b] = acc_v[b] + dv

        dq = backward(
            4,
            lambda b: near_kt[b],
            lambda b: near_v[b],
            [j],
            lambda n, h, b: e_near[h, j, b],
            lambda n, h: fac_n[h, j],
            put,
        )
        for h in range(2):
            acc_q[j, halves[h]] = dq[0][h]

    @pl.loop(0, EARLY)
    def _(j):
        near_backward(j)

        @pl.when(j == 0)
        def _():
            weight_over_cores()

    swap(3, g_far, g_got).wait_recv()
    swap(4, t_far, t_got).wait_recv()
    g_j = g_got[...].astype(F32)
    g_jt = g_j.T
    g_n[0, 4] = jnp.where(lane_row < HALF, g_j, 0.0).astype(BF16)
    g_n[1, 4] = jnp.where(lane_row < HALF, 0.0, g_j).astype(BF16)
    g_t[0, 4] = jnp.where(lane_col < HALF, g_jt, 0.0).astype(BF16)
    g_t[1, 4] = jnp.where(lane_col < HALF, 0.0, g_jt).astype(BF16)
    for h in range(2):
        delta[h, 4] = t_got[4 + h : 5 + h]
        for g in range(2):
            weight = jnp.exp2((top_f[0, h, g] - t_got[h : h + 1]) * EXP2)
            fac_f[0, h, g] = weight * t_got[2 + h : 3 + h]

    def gx_copy(slot):
        return remote(
            gkv_s.at[slot], gkv_x.at[slot], gx_send.at[slot], gx_recv.at[slot], "seq", sibling
        )

    def grad_copy(dz):
        return remote(
            gkv_s.at[in_z(dz, core)],
            gkv_r.at[dz],
            g_send.at[dz],
            g_recv.at[dz],
            "seq",
            in_seq(x_lo, dz, core),
        )

    def merge(i):
        dz = i + i // 2 - 2 * (i // 3)
        slot = in_z(dz, core)
        gx_copy(slot).wait_recv()
        for n in range(2):
            gkv_s[slot, n] = (gkv_s[slot, n].astype(F32) + gkv_x[slot, n].astype(F32)).astype(BF16)

        @pl.when(dz != 0)
        def _():
            grad_copy(dz).start()

    for j in (3, 4):
        acc_q[j] = jnp.zeros((128, ROWS), F32)

    @pl.loop(0, 4)
    def _(back):
        i = 3 - back
        dz = i + i // 2 - 2 * (i // 3)

        def put(b, dk, dv):
            slot = in_z(dz, b)
            gkv_s[slot, 0] = dk.astype(BF16)
            gkv_s[slot, 1] = dv.astype(BF16)

            @pl.when(core != b)
            def _():
                gx_copy(slot).start()

        dq = backward(
            2,
            lambda b: kv[in_z(dz, b), 0].T,
            lambda b: kv[in_z(dz, b), 1],
            [4, 3],
            lambda n, h, b: e_far[n, h, 2 * i + b],
            lambda n, h: fac_f[n, h, i // 2],
            put,
        )
        for n, j in enumerate((4, 3)):
            for h in range(2):
                acc_q[j, halves[h]] = acc_q[j, halves[h]] + dq[n][h]

        @pl.when(back > 0)
        def _():
            merge(i + 1)

        @pl.when(back == 0)
        def _():
            for n in range(1, NHEAD):
                w_copy(head, n).start()

        @pl.when(back == 2)
        def _():
            weight_over_chips()

    dq_far[...] = acc_q[4].astype(BF16)
    swap(5, dq_far, dq_got).start()
    acc_q[4] = acc_q[3]
    merge(0)

    @pl.loop(EARLY, RATE)
    def _(j):
        near_backward(j)

    for n in range(1, NHEAD):
        w_copy(peer_h(n), n).wait_recv()
        w_share(peer_h(n), core).start()
    swap(5, dq_far, dq_got).wait_recv()
    acc_q[3] = acc_q[3] + acc_q[4] + dq_got[...].astype(F32)
    dq_slots = [(acc_q[j] * SCALE).T for j in range(RATE)]
    dq_parts = [from_slot(dq_slots, shift_row, r).astype(BF16) for r in range(RATE)]
    dq_ref[...] = nn(jnp.concatenate(dq_parts, axis=1), perm[...]).astype(BF16)

    weight_to_sibling()
    for n in range(1, NHEAD):
        w_share(peer_h(n), 1 - core).wait_recv()
        at_copy(peer_h(n), n).wait_recv()
    from_rm = jnp.where(rm_row == lax.rem(rm_col, 32) * RATE + rm_col // 32, 1.0, 0.0).astype(BF16)
    result = jnp.zeros((128, WIDTH), F32)
    for h in range(NHEAD):
        rows = nn(from_rm, attn_r[h].reshape(128, 128)).astype(BF16)
        result = result + nn(rows, ws[h])
    lo_ref[...] = result.astype(BF16)

    for turn in turns:
        grad_copy(turn).wait_recv()
    far = []
    for n in range(2):
        total = gkv_s[own, n].astype(F32)
        for turn in turns:
            total = total + gkv_r[turn, n].astype(F32)
        far.append(total)
    sum_k, sum_v = far
    dk_parts = []
    dv_parts = []
    for r in range(RATE):
        mine = shift_row == r
        dk_parts.append(((acc_k[r] + jnp.where(mine, sum_k, 0.0)) * SCALE).astype(BF16))
        dv_parts.append((acc_v[r] + jnp.where(mine, sum_v, 0.0)).astype(BF16))
    dk_ref[...] = nn(jnp.concatenate(dk_parts, axis=1), perm[...]).astype(BF16)
    dv_ref[...] = nn(jnp.concatenate(dv_parts, axis=1), perm[...]).astype(BF16)

    dc_copy(1 - core).wait_recv()
    for half in range(2):
        whole = dwf[half].reshape(128, 384)
        dw_ref[0:48, half * 384 : (half + 1) * 384] = whole[0:48]
        dw_ref[48:96, half * 384 : (half + 1) * 384] = whole[64:112]

    dx_copy(1 - core).wait_send()
    dc_copy(core).wait_send()

    @pl.loop(0, 7)
    def _(i):
        kv_copy(own, i, partner).wait_send()

    @pl.loop(1, 8)
    def _(i):
        w_copy(head, i).wait_send()
        w_share(peer_h(i), core).wait_send()
        dy_copy(head, i - 1, partner_h).wait_send()
        at_copy(head, i).wait_send()
        dw_copy(chip, i).wait_send()
        df_copy(chip, i).wait_send()

    @pl.loop(0, 4)
    def _(i):
        gx_copy(i * 2 + 1 - core).wait_send()

    for turn in turns:
        grad_copy(turn).wait_send()
    swaps = ((q_far, q_got), (m_far, m_got), (o_far, o_got), (g_far, g_got), (t_far, t_got), (dq_far, dq_got))
    for i, (source, target) in enumerate(swaps):
        swap(i, source, target).wait_send()


def finish(*refs):
    for source, target in zip(refs[:5], refs[5:], strict=True):
        target[...] = source[...]


def body(queries, keys, values, slide_ids, head_shift_list, out_weight, d_y):
    vmem = pl.BlockSpec(memory_space=pltpu.VMEM)
    hbm = pl.BlockSpec(memory_space=pltpu.HBM)
    smem = pl.BlockSpec(memory_space=pltpu.SMEM)
    sems = pltpu.SemaphoreType.DMA
    results = pl.pallas_call(
        kernel,
        out_shape=(
            jax.ShapeDtypeStruct((128, WIDTH), BF16),
            jax.ShapeDtypeStruct((ROWS, 384), BF16),
            jax.ShapeDtypeStruct((ROWS, 384), BF16),
            jax.ShapeDtypeStruct((ROWS, 384), BF16),
            jax.ShapeDtypeStruct((96, WIDTH), BF16),
        ),
        in_specs=[hbm, hbm, hbm, vmem, smem, hbm, hbm],
        out_specs=(vmem,) * 5,
        scratch_shapes=[
            pltpu.VMEM((ROWS, 384), BF16),
            pltpu.VMEM((ROWS, 384), BF16),
            pltpu.VMEM((ROWS, 384), BF16),
            pltpu.VMEM((NHEAD, 128, WIDTH), BF16),
            pltpu.VMEM((4 * 128, 384), BF16),
            pltpu.VMEM((4, ROWS, 128), BF16),
            pltpu.VMEM((4, ROWS, 128), BF16),
            pltpu.VMEM((4, 128, ROWS), BF16),
            pltpu.VMEM((4, 128, ROWS), BF16),
            pltpu.VMEM((8, 2, ROWS, 128), BF16),
            pltpu.VMEM((8, 128, ROWS), BF16),
            pltpu.VMEM((RATE, ROWS, 128), BF16),
            pltpu.VMEM((2, 5, 128, ROWS), BF16),
            pltpu.VMEM((2, 5, ROWS, 128), BF16),
            pltpu.VMEM((2, 5, 128, ROWS), BF16),
            pltpu.VMEM((2, 5, ROWS, 128), BF16),
            pltpu.VMEM((2, RATE, 4, ROWS, ROWS), F32),
            pltpu.VMEM((2, 2, 8, ROWS, ROWS), F32),
            pltpu.VMEM((2, 1, ROWS), F32),
            pltpu.VMEM((2, 1, ROWS), F32),
            pltpu.VMEM((2, HALF, ROWS), F32),
            pltpu.VMEM((2, 2, 2, 1, ROWS), F32),
            pltpu.VMEM((2, 2, 2, 1, ROWS), F32),
            pltpu.VMEM((2, 2, 2, HALF, ROWS), F32),
            pltpu.VMEM((2, RATE, 1, ROWS), F32),
            pltpu.VMEM((2, 2, 2, 1, ROWS), F32),
            pltpu.VMEM((2, 5, 1, ROWS), F32),
            pltpu.VMEM((RATE, 128, ROWS), BF16),
            pltpu.VMEM((RATE, ROWS, 128), BF16),
            pltpu.VMEM((NHEAD, RATE, 32, 128), BF16),
            pltpu.VMEM((RATE, ROWS, WIDTH), BF16),
            pltpu.VMEM((NHEAD, 128, WIDTH), BF16),
            pltpu.VMEM((2, 8, 16, 384), F32),
            pltpu.VMEM((8, 16, 384), F32),
            pltpu.VMEM((8, 16, 384), F32),
            pltpu.VMEM((8, 16, 384), F32),
            pltpu.VMEM((2, 8, 16, 384), BF16),
            pltpu.VMEM((8, 2, ROWS, 128), BF16),
            pltpu.VMEM((8, 2, ROWS, 128), BF16),
            pltpu.VMEM((4, 2, ROWS, 128), BF16),
            pltpu.VMEM((ROWS, 128), BF16),
            pltpu.VMEM((ROWS, 128), BF16),
            pltpu.VMEM((ROWS, 128), BF16),
            pltpu.VMEM((ROWS, 128), BF16),
            pltpu.VMEM((128, ROWS), BF16),
            pltpu.VMEM((128, ROWS), BF16),
            pltpu.VMEM((8, ROWS), F32),
            pltpu.VMEM((8, ROWS), F32),
            pltpu.VMEM((8, ROWS), F32),
            pltpu.VMEM((8, ROWS), F32),
            pltpu.VMEM((128, ROWS), BF16),
            pltpu.VMEM((128, ROWS), BF16),
            pltpu.VMEM((4, ROWS, 128), F32),
            pltpu.VMEM((4, ROWS, 128), F32),
            pltpu.VMEM((5, 128, ROWS), F32),
            sems((6,)),
            sems((8,)),
            sems((8,)),
            sems((NHEAD,)),
            sems((NHEAD,)),
            sems((NHEAD,)),
            sems((NHEAD,)),
            sems((NHEAD,)),
            sems((NHEAD,)),
            sems((NHEAD,)),
            sems((NHEAD,)),
            sems((2,)),
            sems((8,)),
            sems((8,)),
            sems((8,)),
            sems((8,)),
            sems((2,)),
            sems((8,)),
            sems((8,)),
            sems((4,)),
            sems((4,)),
            sems((6,)),
            sems((6,)),
        ],
        compiler_params=pltpu.CompilerParams(
            collective_id=0, has_side_effects=True, vmem_limit_bytes=56 * 1024 * 1024
        ),
        cost_estimate=pl.CostEstimate(
            flops=3_000_000_000, bytes_accessed=4_000_000, transcendentals=5_000_000
        ),
    )(
        queries,
        keys,
        values,
        slide_ids.reshape(8, 128),
        head_shift_list,
        out_weight,
        d_y,
    )
    return pl.pallas_call(
        finish,
        out_shape=tuple(jax.ShapeDtypeStruct(r.shape, r.dtype) for r in results),
        in_specs=[vmem] * 5,
        out_specs=(vmem,) * 5,
    )(*results)


def solution(mesh):
    placed = (
        P("seq", "head"),
        P("seq", "head"),
        P("seq", "head"),
        P("seq"),
        P(),
        P("head", None),
        P(("seq", "head"), None),
    )
    return jax.shard_map(
        body,
        mesh=mesh,
        in_specs=placed,
        out_specs=(
            P(("seq", "head"), None),
            P("seq", "head"),
            P("seq", "head"),
            P("seq", "head"),
            P("head", None),
        ),
        check_vma=False,
    )
```

```python
import math

import jax
import jax.numpy as jnp
from jax import lax
from jax.experimental import pallas as pl
from jax.experimental.pallas import tpu as pltpu
from jax.sharding import PartitionSpec as P

HEAD = 48
HALF = 64
RATE = 4
ROWS = 256
WIDTH = 768
NSEQ = 16
NHEAD = 8
EARLY = 2
SAME = 8192.0
SCALE = 1.0 / math.sqrt(HEAD)
EXP2 = SCALE * math.log2(math.e)
F32 = jnp.float32
BF16 = jnp.bfloat16


def nt(a, b):
    return lax.dot_general(a, b, (((1,), (1,)), ((), ())), preferred_element_type=F32)


def nn(a, b):
    return jnp.dot(a, b, preferred_element_type=F32)


def iota(shape, dim):
    return lax.broadcasted_iota(jnp.int32, shape, dim)


def remote(src, dst, send, recv, axis, index):
    return pltpu.make_async_remote_copy(
        src_ref=src,
        dst_ref=dst,
        send_sem=send,
        recv_sem=recv,
        device_id={axis: index},
        device_id_type=pl.DeviceIdType.MESH,
    )


def kernel(
    q_ref,
    k_ref,
    v_ref,
    id_ref,
    shift_ref,
    w_ref,
    dy_ref,
    lo_ref,
    dq_ref,
    dk_ref,
    dv_ref,
    dw_ref,
    q_in,
    k_in,
    v_in,
    raw,
    perm,
    near_k,
    near_v,
    near_kt,
    near_vt,
    kv,
    far_vt,
    g_raw,
    q_t,
    q_n,
    g_t,
    g_n,
    e_near,
    e_far,
    top_n,
    sum_n,
    out_n,
    top_f,
    sum_f,
    out_f,
    fac_n,
    fac_f,
    delta,
    attn_t,
    attn_n,
    attn_r,
    dys,
    ws,
    dwp,
    dwx,
    dwm,
    dwr,
    dwf,
    gkv_s,
    gkv_x,
    gkv_r,
    q_far,
    q_got,
    g_far,
    g_got,
    o_far,
    o_got,
    m_far,
    m_got,
    t_far,
    t_got,
    dq_far,
    dq_got,
    acc_k,
    acc_v,
    acc_q,
    in_sem,
    kv_send,
    kv_recv,
    dy_send,
    dy_recv,
    w_send,
    w_recv,
    ws_send,
    ws_recv,
    at_send,
    at_recv,
    dx_sem,
    dw_send,
    dw_recv,
    df_send,
    df_recv,
    dc_sem,
    gx_send,
    gx_recv,
    g_send,
    g_recv,
    swap_send,
    swap_recv,
):
    seq = lax.axis_index("seq")
    head = lax.axis_index("head")

    x_lo, z, core = seq // 8, lax.rem(seq // 2, 4), lax.rem(seq, 2)
    x_hi, y = head // 4, lax.rem(head, 4)
    chip = seq // 2

    def at_chip(j):
        return j * 2 + core

    def in_seq(x, dz, c):
        return x * 8 + lax.rem(z + dz, 4) * 2 + c

    def in_z(dz, c):
        return lax.rem(z + dz, 4) * 2 + c

    def in_head(x, dy):
        return x * 4 + lax.rem(y + dy, 4)

    def peer_c(i):
        return lax.rem(chip + i, 8)

    def peer_h(i):
        return lax.rem(head + i, NHEAD)

    sibling = in_seq(x_lo, 0, 1 - core)
    partner = in_seq(1 - x_lo, 0, core)
    partner_h = in_head(1 - x_hi, 0)
    turns = (1, 3, 2)

    barrier = pltpu.get_barrier_semaphore()
    pl.semaphore_signal(
        barrier, inc=1, device_id={"seq": sibling}, device_id_type=pl.DeviceIdType.MESH
    )

    @pl.loop(1, 8)
    def _(i):
        pl.semaphore_signal(
            barrier,
            inc=1,
            device_id={"seq": at_chip(peer_c(i))},
            device_id_type=pl.DeviceIdType.MESH,
        )
        pl.semaphore_signal(
            barrier, inc=1, device_id={"head": peer_h(i)}, device_id_type=pl.DeviceIdType.MESH
        )

    loads = [
        pltpu.make_async_copy(source, target, in_sem.at[n])
        for n, (source, target) in enumerate(
            (
                (k_ref, k_in),
                (v_ref, v_in),
                (q_ref, q_in),
                (dy_ref, raw.at[head]),
                (w_ref.at[0:48], ws.at[head, 0:48]),
                (w_ref.at[48:96], ws.at[head, 64:112]),
            )
        )
    ]
    for load in loads:
        load.start()

    slide_col = lax.rem(iota((128, 128), 0), HALF) - HEAD
    below = jnp.zeros((128, 128), F32)
    upto = jnp.zeros((128, 128), F32)
    for s in range(8):
        ids = id_ref[s : s + 1, :]
        below = below + jnp.where(ids < slide_col, 1.0, 0.0)
        upto = upto + jnp.where(ids <= slide_col, 1.0, 0.0)
    ones = jnp.ones((8, 128), BF16)
    first_row = nt(ones, below.astype(BF16))[0:1, :]
    last_row = nt(ones, upto.astype(BF16))[0:1, :]
    first_col = jnp.sum(below, axis=1, keepdims=True)
    last_col = jnp.sum(upto, axis=1, keepdims=True)

    shift0 = shift_ref[2 * head]
    shift1 = shift_ref[2 * head + 1]
    lane_row = iota((1, 128), 1)
    lane_col = iota((128, 1), 0)
    shift_row = jnp.where(lane_row < HALF, shift0, shift1)
    shift_col = jnp.where(lane_col < HALF, shift0, shift1)
    hot_row = lax.rem(lane_row, HALF) >= HEAD
    hot_col = lax.rem(lane_col, HALF) >= HEAD

    def turned(shift, j):
        return jnp.bitwise_and(shift + 1 + j, RATE - 1)

    def to_slot(parts, shift, j):
        out = parts[0]
        for r in range(1, RATE):
            out = jnp.where(turned(shift, j) == r, parts[r], out)
        return out

    def from_slot(parts, shift, r):
        out = parts[0]
        for j in range(1, RATE):
            out = jnp.where(turned(shift, j) == r, parts[j], out)
        return out

    within = lax.rem(lane_col, HALF)
    source = (lane_col // HALF) * (RATE * HEAD) + within
    given = iota((128, 384), 1)
    for r in range(RATE):
        held = jnp.where(within < HEAD, source + r * HEAD, -1)
        perm[r * 128 : (r + 1) * 128] = jnp.where(given == held, 1.0, 0.0).astype(BF16)
    pl.semaphore_wait(barrier, 15)

    def dy_copy(owner, i, dst, first=False):
        source = dy_ref if first else raw.at[owner]
        return remote(source, raw.at[owner], dy_send.at[i], dy_recv.at[owner], "head", dst)

    dy_copy(head, 0, partner_h, True).start()
    dy_copy(head, 1, in_head(x_hi, 2), True).start()

    loads[0].wait()
    loads[1].wait()
    k_p = nt(k_in[...], perm[...])
    v_p = nt(v_in[...], perm[...])
    one_row = jnp.where(lax.rem(lane_row, HALF) == HEAD, 1.0, 0.0)
    one_col = jnp.where(lax.rem(lane_col, HALF) == HEAD, 1.0, 0.0)
    far_k = jnp.zeros((ROWS, 128), F32)
    far_v = jnp.zeros((ROWS, 128), F32)
    for r in range(RATE):
        at = (iota((ROWS, 128), 0) * RATE + r).astype(F32)
        hot = jnp.where(hot_row & (at >= first_row) & (at < last_row), 1.0, 0.0)
        k_r = k_p[:, r * 128 : (r + 1) * 128] + hot
        v_r = v_p[:, r * 128 : (r + 1) * 128] + one_row
        near_k[r] = k_r.astype(BF16)
        near_v[r] = v_r.astype(BF16)
        far_k = jnp.where(shift_row == r, k_r, far_k)
        far_v = jnp.where(shift_row == r, v_r, far_v)
    own = in_z(0, core)
    kv[own, 0] = far_k.astype(BF16)
    kv[own, 1] = far_v.astype(BF16)

    def kv_copy(slot, i, dst):
        return remote(kv.at[slot], kv.at[slot], kv_send.at[i], kv_recv.at[slot], "seq", dst)

    def swap(i, source, target):
        return remote(source, target, swap_send.at[i], swap_recv.at[i], "seq", partner)

    def w_copy(owner, i):
        part = ws.at[owner, pl.ds(pl.multiple_of(core * HALF, HALF), HEAD)]
        return remote(part, part, w_send.at[i], w_recv.at[owner], "head", peer_h(i))

    def w_share(owner, half):
        part = ws.at[owner, pl.ds(pl.multiple_of(half * HALF, HALF), HEAD)]
        return remote(part, part, ws_send.at[owner], ws_recv.at[owner], "seq", sibling)

    for n, turn in enumerate(turns):
        kv_copy(own, n, in_seq(x_lo, turn, core)).start()
    kv_copy(own, 3, sibling).start()
    for n, turn in enumerate((1, 3)):
        dy_copy(head, 2 + n, in_head(x_hi, turn), True).start()
    loads[2].wait()
    q_p = nt(q_in[...], perm[...])
    q_pt = nt(perm[...], q_in[...])
    k_pt = nt(perm[...], k_in[...])
    v_pt = nt(perm[...], v_in[...])
    for r in range(RATE):
        near_kt[r] = k_pt[r * 128 : (r + 1) * 128].astype(BF16)
        near_vt[r] = (v_pt[r * 128 : (r + 1) * 128] + one_col).astype(BF16)
    q_rows = []
    q_cols = []
    for r in range(RATE):
        at = (iota((128, ROWS), 1) * RATE + r).astype(F32)
        hot = jnp.where(hot_col & (at >= first_col) & (at < last_col), SAME, 0.0)
        q_rows.append(q_p[:, r * 128 : (r + 1) * 128])
        q_cols.append(q_pt[r * 128 : (r + 1) * 128, :] + hot)
    for j in reversed(range(RATE)):
        q_j = to_slot(q_rows, shift_row, j)
        q_jt = to_slot(q_cols, shift_col, j)
        q_n[0, j] = jnp.where(lane_row < HALF, q_j, 0.0).astype(BF16)
        q_n[1, j] = jnp.where(lane_row < HALF, 0.0, q_j).astype(BF16)
        if j == 3:
            at = (iota((ROWS, 128), 0) * RATE + shift_row).astype(F32)
            hot = jnp.where(hot_row & (at >= first_row) & (at < last_row), SAME, 0.0)
            q_far[...] = (q_j + hot).astype(BF16)
            swap(0, q_far, q_got).start()
        q_t[0, j] = jnp.where(lane_col < HALF, q_jt, 0.0).astype(BF16)
        q_t[1, j] = jnp.where(lane_col < HALF, 0.0, q_jt).astype(BF16)

    halves = (slice(0, HALF), slice(HALF, 2 * HALF))

    def forward(keys, vals_t, q_of, e_of):
        top = [None, None]
        for b in range(4):
            for h in range(2):
                s = nn(keys(b), q_of(h))
                e_of(h)[b] = s
                m = jnp.max(s, axis=0, keepdims=True)
                top[h] = m if b == 0 else jnp.maximum(top[h], m)
        out = [jnp.zeros((HALF, ROWS), F32), jnp.zeros((HALF, ROWS), F32)]
        for b in range(4):
            for h in range(2):
                e = jnp.exp2((e_of(h)[b] - top[h]) * EXP2)
                e_of(h)[b] = e
                out[h] = out[h] + nn(vals_t(b)[halves[h]], e.astype(BF16))
        return [(top[h], out[h][HEAD : HEAD + 1], out[h]) for h in range(2)]


    @pl.loop(0, RATE)
    def _(j):
        tiles = forward(
            lambda b: near_k[b],
            lambda b: near_vt[b],
            lambda h: q_t[h, j],
            lambda h: e_near.at[h, j],
        )
        for h in range(2):
            top, total, out = tiles[h]
            top_n[h] = top
            sum_n[h] = total
            out_n[h] = out
            inverse = 1.0 / total
            fac_n[h, j] = inverse
            attn_t[j, halves[h]] = (out * inverse).astype(BF16)

        @pl.when(j == 0)
        def _():
            dy_copy(partner_h, 0, partner_h).wait_recv()
            for n, turn in enumerate((1, 3)):
                dy_copy(partner_h, 4 + n, in_head(x_hi, turn)).start()
            dy_copy(in_head(x_hi, 2), 0, partner_h).wait_recv()
            dy_copy(in_head(x_hi, 2), 6, partner_h).start()

    def share(i):
        slot = in_z(i + i // 2 - 2 * (i // 3), core)
        kv_copy(slot, 0, partner).wait_recv()
        kv_copy(slot, 3 + i, sibling).start()

    share(1)
    swap(0, q_far, q_got).wait_recv()
    q_j = q_got[...].astype(F32)
    q_jt = q_j.T
    q_n[0, 4] = jnp.where(lane_row < HALF, q_j, 0.0).astype(BF16)
    q_n[1, 4] = jnp.where(lane_row < HALF, 0.0, q_j).astype(BF16)
    q_t[0, 4] = jnp.where(lane_col < HALF, q_jt, 0.0).astype(BF16)
    q_t[1, 4] = jnp.where(lane_col < HALF, 0.0, q_jt).astype(BF16)

    def far_block(n):
        i = n // 2
        return in_z(i + i // 2 - 2 * (i // 3), lax.rem(n, 2))

    kv_copy(in_z(0, 1 - core), 0, partner).wait_recv()
    kv_copy(in_z(1, 1 - core), 0, partner).wait_recv()

    def turn_values(g):
        for b in range(4):
            far_vt[4 * g + b] = kv[far_block(4 * g + b), 1].T

    turn_values(0)

    @pl.loop(0, 4)
    def _(step):
        g = lax.rem(step, 2)
        own_q = step // 2

        @pl.when(step == 1)
        def _():
            for i in (2, 3):
                share(i)
            for dz in (3, 2):
                kv_copy(in_z(dz, 1 - core), 0, partner).wait_recv()
            turn_values(1)

        @pl.when(step == 2)
        def _():
            for h in range(2):
                top = jnp.maximum(top_f[0, h, 0], top_f[0, h, 1])
                w0 = jnp.exp2((top_f[0, h, 0] - top) * EXP2)
                w1 = jnp.exp2((top_f[0, h, 1] - top) * EXP2)
                m_far[h : h + 1] = top
                m_far[2 + h : 3 + h] = w0 * sum_f[0, h, 0] + w1 * sum_f[0, h, 1]
                o_far[halves[h]] = (w0 * out_f[0, h, 0] + w1 * out_f[0, h, 1]).astype(BF16)
            m_far[4:8] = jnp.zeros((4, ROWS), F32)
            swap(1, m_far, m_got).start()
            swap(2, o_far, o_got).start()

        tiles = forward(
            lambda b: kv[far_block(4 * g + b), 0],
            lambda b: far_vt[4 * g + b],
            lambda h: q_t[h, 4 - own_q],
            lambda h: e_far.at[own_q, h, pl.ds(4 * g, 4)],
        )
        for h in range(2):
            top, total, out = tiles[h]
            top_f[own_q, h, g] = top
            sum_f[own_q, h, g] = total
            out_f[own_q, h, g] = out

    for turn in (1, 3):
        for x in range(2):
            dy_copy(in_head(x, turn), 0, partner_h).wait_recv()
    dy_copy(in_head(1 - x_hi, 2), 0, partner_h).wait_recv()
    loads[3].wait()
    loads[4].wait()
    loads[5].wait()
    zeros16 = jnp.zeros((16, WIDTH), BF16)
    for h in range(NHEAD):
        ws[h, 48:64] = zeros16
        ws[h, 112:128] = zeros16
    rm_row = iota((128, 128), 0)
    rm_col = iota((128, 128), 1)
    to_rm = jnp.where(rm_col == lax.rem(rm_row, 32) * RATE + rm_row // 32, 1.0, 0.0).astype(BF16)

    for h in range(NHEAD):
        rows = nn(to_rm, raw[h]).astype(BF16)
        for r in range(RATE):
            dys[r, h * 32 : (h + 1) * 32] = rows[r * 32 : (r + 1) * 32]
    w_own = ws[head]
    g_rows = []
    g_cols = []
    for r in range(RATE):
        g_rows.append(nt(dys[r], w_own))
        g_cols.append(nt(w_own, dys[r]))
    for j in reversed(range(RATE)):
        g_j = to_slot(g_rows, shift_row, j)
        g_jt = to_slot(g_cols, shift_col, j)
        g_n[0, j] = jnp.where(lane_row < HALF, g_j, 0.0).astype(BF16)
        g_n[1, j] = jnp.where(lane_row < HALF, 0.0, g_j).astype(BF16)
        g_t[0, j] = jnp.where(lane_col < HALF, g_jt, 0.0).astype(BF16)
        g_t[1, j] = jnp.where(lane_col < HALF, 0.0, g_jt).astype(BF16)
        if j == 3:
            g_far[...] = g_j.astype(BF16)
            swap(3, g_far, g_got).start()
    swap(1, m_far, m_got).wait_recv()
    swap(2, o_far, o_got).wait_recv()
    for h in range(2):
        tops = [top_n[h], top_f[1, h, 0], top_f[1, h, 1], m_got[h : h + 1]]
        sums = [sum_n[h], sum_f[1, h, 0], sum_f[1, h, 1], m_got[2 + h : 3 + h]]
        outs = [out_n[h], out_f[1, h, 0], out_f[1, h, 1], o_got[halves[h]].astype(F32)]
        top = tops[0]
        for other in tops[1:]:
            top = jnp.maximum(top, other)
        weights = [jnp.exp2((other - top) * EXP2) for other in tops]
        total = weights[0] * sums[0]
        out = weights[0] * outs[0]
        for n in range(1, 4):
            total = total + weights[n] * sums[n]
            out = out + weights[n] * outs[n]
        inverse = 1.0 / total
        fac_n[h, 3] = weights[0] * inverse
        for g in range(2):
            fac_f[1, h, g] = weights[1 + g] * inverse
        t_far[h : h + 1] = top
        t_far[2 + h : 3 + h] = inverse
        attn_t[3, halves[h]] = (out * inverse).astype(BF16)

    for j in range(RATE):
        for h in range(2):
            product = g_t[h, j, halves[h], :].astype(F32) * attn_t[j, halves[h]].astype(F32)
            delta[h, j] = jnp.sum(product, axis=0, keepdims=True)
    t_far[4:5] = delta[0, 3]
    t_far[5:6] = delta[1, 3]
    t_far[6:8] = jnp.zeros((2, ROWS), F32)
    swap(4, t_far, t_got).start()

    attn_slots = [attn_t[j].astype(F32) for j in range(RATE)]
    attn_rt = [from_slot(attn_slots, shift_col, r) for r in range(RATE)]
    for r in range(RATE):
        attn_n[r] = attn_rt[r].T.astype(BF16)

    own_rows = pl.ds(pl.multiple_of(head * 32, 32), 32)

    def at_copy(slot, i):
        rows = pl.ds(pl.multiple_of(peer_h(i) * 32, 32), 32)
        return remote(
            attn_n.at[:, rows, :], attn_r.at[slot], at_send.at[i], at_recv.at[slot], "head", peer_h(i)
        )

    for n in range(1, NHEAD):
        at_copy(head, n).start()
    for r in range(RATE):
        attn_r[head, r] = attn_n[r, own_rows, :]

    weight_grad = jnp.zeros((128, WIDTH), F32)
    for r in range(RATE):
        weight_grad = weight_grad + nn(attn_rt[r].astype(BF16), dys[r])

    for half in range(2):
        for n in range(8):
            dwp[half, n] = weight_grad[n * 16 : (n + 1) * 16, half * 384 : (half + 1) * 384]

    def dx_copy(half):
        return remote(dwp.at[half], dwx, dx_sem.at[0], dx_sem.at[1], "seq", sibling)

    def dw_copy(sender, i):
        dst = peer_c(i)
        return remote(dwm.at[dst], dwr.at[sender], dw_send.at[i], dw_recv.at[sender], "seq", at_chip(dst))

    def df_copy(sender, i):
        part = dwf.at[core, sender]
        return remote(part, part, df_send.at[i], df_recv.at[sender], "seq", at_chip(peer_c(i)))

    def dc_copy(half):
        return remote(dwf.at[half], dwf.at[half], dc_sem.at[0], dc_sem.at[1], "seq", sibling)

    dx_copy(1 - core).start()

    def weight_over_cores():
        dx_copy(core).wait_recv()
        dwm[...] = dwp[core] + dwx[...]
        for n in range(1, 8):
            dw_copy(chip, n).start()

    def weight_over_chips():
        for n in range(1, 8):
            dw_copy(peer_c(n), n).wait_recv()
        dwr[chip] = dwm[chip]
        part = dwr[0]
        for n in range(1, 8):
            part = part + dwr[n]
        dwf[core, chip] = part.astype(BF16)
        for n in range(1, 8):
            df_copy(chip, n).start()

    def weight_to_sibling():
        for n in range(1, 8):
            df_copy(peer_c(n), n).wait_recv()
        dc_copy(core).start()

    def backward(count, keys_t, vals, queries, e_of, factor, put):
        dq = [[jnp.zeros((HALF, ROWS), F32) for h in range(2)] for _ in queries]
        pairs = [(n, h, j) for n, j in enumerate(queries) for h in range(2)]

        def products(b):
            return [nn(vals(b), g_t[h, j]) for _, h, j in pairs]

        ahead = products(0)
        for b in range(count):
            k_t = keys_t(b)
            now, ahead = ahead, products(b + 1) if b + 1 < count else None
            dk = jnp.zeros((ROWS, 128), F32)
            dv = jnp.zeros((ROWS, 128), F32)
            for (n, h, j), d_prob in zip(pairs, now, strict=True):
                p = e_of(n, h, b) * factor(n, h)
                ds = (p * (d_prob - delta[h, j])).astype(BF16)
                dv = dv + nn(p.astype(BF16), g_n[h, j])
                dk = dk + nn(ds, q_n[h, j])
                dq[n][h] = dq[n][h] + nn(k_t[halves[h]], ds)
            put(b, dk, dv)
        return dq

    acc_k[...] = jnp.zeros((4, ROWS, 128), F32)
    acc_v[...] = jnp.zeros((4, ROWS, 128), F32)

    def near_backward(j):
        def put(b, dk, dv):
            acc_k[b] = acc_k[b] + dk
            acc_v[b] = acc_v[b] + dv

        dq = backward(
            4,
            lambda b: near_kt[b],
            lambda b: near_v[b],
            [j],
            lambda n, h, b: e_near[h, j, b],
            lambda n, h: fac_n[h, j],
            put,
        )
        for h in range(2):
            acc_q[j, halves[h]] = dq[0][h]

    @pl.loop(0, EARLY)
    def _(j):
        near_backward(j)

        @pl.when(j == 0)
        def _():
            weight_over_cores()

    swap(3, g_far, g_got).wait_recv()
    swap(4, t_far, t_got).wait_recv()
    g_j = g_got[...].astype(F32)
    g_jt = g_j.T
    g_n[0, 4] = jnp.where(lane_row < HALF, g_j, 0.0).astype(BF16)
    g_n[1, 4] = jnp.where(lane_row < HALF, 0.0, g_j).astype(BF16)
    g_t[0, 4] = jnp.where(lane_col < HALF, g_jt, 0.0).astype(BF16)
    g_t[1, 4] = jnp.where(lane_col < HALF, 0.0, g_jt).astype(BF16)
    for h in range(2):
        delta[h, 4] = t_got[4 + h : 5 + h]
        for g in range(2):
            weight = jnp.exp2((top_f[0, h, g] - t_got[h : h + 1]) * EXP2)
            fac_f[0, h, g] = weight * t_got[2 + h : 3 + h]

    def gx_copy(slot):
        return remote(
            gkv_s.at[slot], gkv_x.at[slot], gx_send.at[slot], gx_recv.at[slot], "seq", sibling
        )

    def grad_copy(dz):
        return remote(
            gkv_s.at[in_z(dz, core)],
            gkv_r.at[dz],
            g_send.at[dz],
            g_recv.at[dz],
            "seq",
            in_seq(x_lo, dz, core),
        )

    def merge(i):
        dz = i + i // 2 - 2 * (i // 3)
        slot = in_z(dz, core)
        gx_copy(slot).wait_recv()
        for n in range(2):
            gkv_s[slot, n] = (gkv_s[slot, n].astype(F32) + gkv_x[slot, n].astype(F32)).astype(BF16)

        @pl.when(dz != 0)
        def _():
            grad_copy(dz).start()

    for j in (3, 4):
        acc_q[j] = jnp.zeros((128, ROWS), F32)

    @pl.loop(0, 4)
    def _(back):
        i = 3 - back
        dz = i + i // 2 - 2 * (i // 3)

        def put(b, dk, dv):
            slot = in_z(dz, b)
            gkv_s[slot, 0] = dk.astype(BF16)
            gkv_s[slot, 1] = dv.astype(BF16)

            @pl.when(core != b)
            def _():
                gx_copy(slot).start()

        dq = backward(
            2,
            lambda b: kv[in_z(dz, b), 0].T,
            lambda b: kv[in_z(dz, b), 1],
            [4, 3],
            lambda n, h, b: e_far[n, h, 2 * i + b],
            lambda n, h: fac_f[n, h, i // 2],
            put,
        )
        for n, j in enumerate((4, 3)):
            for h in range(2):
                acc_q[j, halves[h]] = acc_q[j, halves[h]] + dq[n][h]

        @pl.when(back > 0)
        def _():
            merge(i + 1)

        @pl.when(back == 0)
        def _():
            for n in range(1, NHEAD):
                w_copy(head, n).start()

        @pl.when(back == 2)
        def _():
            weight_over_chips()

    dq_far[...] = acc_q[4].astype(BF16)
    swap(5, dq_far, dq_got).start()
    acc_q[4] = acc_q[3]
    merge(0)

    @pl.loop(EARLY, RATE)
    def _(j):
        near_backward(j)

    for n in range(1, NHEAD):
        w_copy(peer_h(n), n).wait_recv()
        w_share(peer_h(n), core).start()
    swap(5, dq_far, dq_got).wait_recv()
    acc_q[3] = acc_q[3] + acc_q[4] + dq_got[...].astype(F32)
    dq_slots = [(acc_q[j] * SCALE).T for j in range(RATE)]
    dq_parts = [from_slot(dq_slots, shift_row, r).astype(BF16) for r in range(RATE)]
    dq_ref[...] = nn(jnp.concatenate(dq_parts, axis=1), perm[...]).astype(BF16)

    weight_to_sibling()
    for n in range(1, NHEAD):
        w_share(peer_h(n), 1 - core).wait_recv()
        at_copy(peer_h(n), n).wait_recv()
    from_rm = jnp.where(rm_row == lax.rem(rm_col, 32) * RATE + rm_col // 32, 1.0, 0.0).astype(BF16)
    result = jnp.zeros((128, WIDTH), F32)
    for h in range(NHEAD):
        rows = nn(from_rm, attn_r[h].reshape(128, 128)).astype(BF16)
        result = result + nn(rows, ws[h])
    lo_ref[...] = result.astype(BF16)

    for turn in turns:
        grad_copy(turn).wait_recv()
    far = []
    for n in range(2):
        total = gkv_s[own, n].astype(F32)
        for turn in turns:
            total = total + gkv_r[turn, n].astype(F32)
        far.append(total)
    sum_k, sum_v = far
    dk_parts = []
    dv_parts = []
    for r in range(RATE):
        mine = shift_row == r
        dk_parts.append(((acc_k[r] + jnp.where(mine, sum_k, 0.0)) * SCALE).astype(BF16))
        dv_parts.append((acc_v[r] + jnp.where(mine, sum_v, 0.0)).astype(BF16))
    dk_ref[...] = nn(jnp.concatenate(dk_parts, axis=1), perm[...]).astype(BF16)
    dv_ref[...] = nn(jnp.concatenate(dv_parts, axis=1), perm[...]).astype(BF16)

    dc_copy(1 - core).wait_recv()
    for half in range(2):
        whole = dwf[half].reshape(128, 384)
        dw_ref[0:48, half * 384 : (half + 1) * 384] = whole[0:48]
        dw_ref[48:96, half * 384 : (half + 1) * 384] = whole[64:112]

    dx_copy(1 - core).wait_send()
    dc_copy(core).wait_send()

    @pl.loop(0, 7)
    def _(i):
        kv_copy(own, i, partner).wait_send()

    @pl.loop(1, 8)
    def _(i):
        w_copy(head, i).wait_send()
        w_share(peer_h(i), core).wait_send()
        dy_copy(head, i - 1, partner_h).wait_send()
        at_copy(head, i).wait_send()
        dw_copy(chip, i).wait_send()
        df_copy(chip, i).wait_send()

    @pl.loop(0, 4)
    def _(i):
        gx_copy(i * 2 + 1 - core).wait_send()

    for turn in turns:
        grad_copy(turn).wait_send()
    swaps = ((q_far, q_got), (m_far, m_got), (o_far, o_got), (g_far, g_got), (t_far, t_got), (dq_far, dq_got))
    for i, (source, target) in enumerate(swaps):
        swap(i, source, target).wait_send()


def finish(*refs):
    for source, target in zip(refs[:5], refs[5:], strict=True):
        target[...] = source[...]


def body(queries, keys, values, slide_ids, head_shift_list, out_weight, d_y):
    vmem = pl.BlockSpec(memory_space=pltpu.VMEM)
    hbm = pl.BlockSpec(memory_space=pltpu.HBM)
    smem = pl.BlockSpec(memory_space=pltpu.SMEM)
    sems = pltpu.SemaphoreType.DMA
    results = pl.pallas_call(
        kernel,
        out_shape=(
            jax.ShapeDtypeStruct((128, WIDTH), BF16),
            jax.ShapeDtypeStruct((ROWS, 384), BF16),
            jax.ShapeDtypeStruct((ROWS, 384), BF16),
            jax.ShapeDtypeStruct((ROWS, 384), BF16),
            jax.ShapeDtypeStruct((96, WIDTH), BF16),
        ),
        in_specs=[hbm, hbm, hbm, vmem, smem, hbm, hbm],
        out_specs=(vmem,) * 5,
        scratch_shapes=[
            pltpu.VMEM((ROWS, 384), BF16),
            pltpu.VMEM((ROWS, 384), BF16),
            pltpu.VMEM((ROWS, 384), BF16),
            pltpu.VMEM((NHEAD, 128, WIDTH), BF16),
            pltpu.VMEM((4 * 128, 384), BF16),
            pltpu.VMEM((4, ROWS, 128), BF16),
            pltpu.VMEM((4, ROWS, 128), BF16),
            pltpu.VMEM((4, 128, ROWS), BF16),
            pltpu.VMEM((4, 128, ROWS), BF16),
            pltpu.VMEM((8, 2, ROWS, 128), BF16),
            pltpu.VMEM((8, 128, ROWS), BF16),
            pltpu.VMEM((RATE, ROWS, 128), BF16),
            pltpu.VMEM((2, 5, 128, ROWS), BF16),
            pltpu.VMEM((2, 5, ROWS, 128), BF16),
            pltpu.VMEM((2, 5, 128, ROWS), BF16),
            pltpu.VMEM((2, 5, ROWS, 128), BF16),
            pltpu.VMEM((2, RATE, 4, ROWS, ROWS), F32),
            pltpu.VMEM((2, 2, 8, ROWS, ROWS), F32),
            pltpu.VMEM((2, 1, ROWS), F32),
            pltpu.VMEM((2, 1, ROWS), F32),
            pltpu.VMEM((2, HALF, ROWS), F32),
            pltpu.VMEM((2, 2, 2, 1, ROWS), F32),
            pltpu.VMEM((2, 2, 2, 1, ROWS), F32),
            pltpu.VMEM((2, 2, 2, HALF, ROWS), F32),
            pltpu.VMEM((2, RATE, 1, ROWS), F32),
            pltpu.VMEM((2, 2, 2, 1, ROWS), F32),
            pltpu.VMEM((2, 5, 1, ROWS), F32),
            pltpu.VMEM((RATE, 128, ROWS), BF16),
            pltpu.VMEM((RATE, ROWS, 128), BF16),
            pltpu.VMEM((NHEAD, RATE, 32, 128), BF16),
            pltpu.VMEM((RATE, ROWS, WIDTH), BF16),
            pltpu.VMEM((NHEAD, 128, WIDTH), BF16),
            pltpu.VMEM((2, 8, 16, 384), F32),
            pltpu.VMEM((8, 16, 384), F32),
            pltpu.VMEM((8, 16, 384), F32),
            pltpu.VMEM((8, 16, 384), F32),
            pltpu.VMEM((2, 8, 16, 384), BF16),
            pltpu.VMEM((8, 2, ROWS, 128), BF16),
            pltpu.VMEM((8, 2, ROWS, 128), BF16),
            pltpu.VMEM((4, 2, ROWS, 128), BF16),
            pltpu.VMEM((ROWS, 128), BF16),
            pltpu.VMEM((ROWS, 128), BF16),
            pltpu.VMEM((ROWS, 128), BF16),
            pltpu.VMEM((ROWS, 128), BF16),
            pltpu.VMEM((128, ROWS), BF16),
            pltpu.VMEM((128, ROWS), BF16),
            pltpu.VMEM((8, ROWS), F32),
            pltpu.VMEM((8, ROWS), F32),
            pltpu.VMEM((8, ROWS), F32),
            pltpu.VMEM((8, ROWS), F32),
            pltpu.VMEM((128, ROWS), BF16),
            pltpu.VMEM((128, ROWS), BF16),
            pltpu.VMEM((4, ROWS, 128), F32),
            pltpu.VMEM((4, ROWS, 128), F32),
            pltpu.VMEM((5, 128, ROWS), F32),
            sems((6,)),
            sems((8,)),
            sems((8,)),
            sems((NHEAD,)),
            sems((NHEAD,)),
            sems((NHEAD,)),
            sems((NHEAD,)),
            sems((NHEAD,)),
            sems((NHEAD,)),
            sems((NHEAD,)),
            sems((NHEAD,)),
            sems((2,)),
            sems((8,)),
            sems((8,)),
            sems((8,)),
            sems((8,)),
            sems((2,)),
            sems((8,)),
            sems((8,)),
            sems((4,)),
            sems((4,)),
            sems((6,)),
            sems((6,)),
        ],
        compiler_params=pltpu.CompilerParams(
            collective_id=0, has_side_effects=True, vmem_limit_bytes=56 * 1024 * 1024
        ),
        cost_estimate=pl.CostEstimate(
            flops=3_000_000_000, bytes_accessed=4_000_000, transcendentals=5_000_000
        ),
    )(
        queries,
        keys,
        values,
        slide_ids.reshape(8, 128),
        head_shift_list,
        out_weight,
        d_y,
    )
    return pl.pallas_call(
        finish,
        out_shape=tuple(jax.ShapeDtypeStruct(r.shape, r.dtype) for r in results),
        in_specs=[vmem] * 5,
        out_specs=(vmem,) * 5,
    )(*results)


def solution(mesh):
    placed = (
        P("seq", "head"),
        P("seq", "head"),
        P("seq", "head"),
        P("seq"),
        P(),
        P("head", None),
        P(("seq", "head"), None),
    )
    return jax.shard_map(
        body,
        mesh=mesh,
        in_specs=placed,
        out_specs=(
            P(("seq", "head"), None),
            P("seq", "head"),
            P("seq", "head"),
            P("seq", "head"),
            P("head", None),
        ),
        check_vma=False,
    )
```

```python
import math

import jax
import jax.numpy as jnp
from jax import lax
from jax.experimental import pallas as pl
from jax.experimental.pallas import tpu as pltpu
from jax.sharding import PartitionSpec as P

HEAD = 48
HALF = 64
RATE = 4
ROWS = 256
WIDTH = 768
NSEQ = 16
NHEAD = 8
EARLY = 2
SAME = 8192.0
SCALE = 1.0 / math.sqrt(HEAD)
EXP2 = SCALE * math.log2(math.e)
F32 = jnp.float32
BF16 = jnp.bfloat16


def nt(a, b):
    return lax.dot_general(a, b, (((1,), (1,)), ((), ())), preferred_element_type=F32)


def nn(a, b):
    return jnp.dot(a, b, preferred_element_type=F32)


def iota(shape, dim):
    return lax.broadcasted_iota(jnp.int32, shape, dim)


def remote(src, dst, send, recv, axis, index):
    return pltpu.make_async_remote_copy(
        src_ref=src,
        dst_ref=dst,
        send_sem=send,
        recv_sem=recv,
        device_id={axis: index},
        device_id_type=pl.DeviceIdType.MESH,
    )


def kernel(
    q_ref,
    k_ref,
    v_ref,
    id_ref,
    shift_ref,
    w_ref,
    dy_ref,
    lo_ref,
    dq_ref,
    dk_ref,
    dv_ref,
    dw_ref,
    q_in,
    k_in,
    v_in,
    raw,
    perm,
    near_k,
    near_v,
    near_kt,
    near_vt,
    kv,
    far_vt,
    g_raw,
    q_t,
    q_n,
    g_t,
    g_n,
    e_near,
    e_far,
    top_n,
    sum_n,
    out_n,
    top_f,
    sum_f,
    out_f,
    fac_n,
    fac_f,
    delta,
    attn_t,
    attn_n,
    attn_r,
    dys,
    ws,
    dwp,
    dwx,
    dwm,
    dwr,
    dwf,
    gkv_s,
    gkv_x,
    gkv_r,
    q_far,
    q_got,
    g_far,
    g_got,
    o_far,
    o_got,
    m_far,
    m_got,
    t_far,
    t_got,
    dq_far,
    dq_got,
    acc_k,
    acc_v,
    acc_q,
    in_sem,
    kv_send,
    kv_recv,
    dy_send,
    dy_recv,
    w_send,
    w_recv,
    ws_send,
    ws_recv,
    at_send,
    at_recv,
    dx_sem,
    dw_send,
    dw_recv,
    df_send,
    df_recv,
    dc_sem,
    gx_send,
    gx_recv,
    g_send,
    g_recv,
    swap_send,
    swap_recv,
):
    seq = lax.axis_index("seq")
    head = lax.axis_index("head")

    x_lo, z, core = seq // 8, lax.rem(seq // 2, 4), lax.rem(seq, 2)
    x_hi, y = head // 4, lax.rem(head, 4)
    chip = seq // 2

    def at_chip(j):
        return j * 2 + core

    def in_seq(x, dz, c):
        return x * 8 + lax.rem(z + dz, 4) * 2 + c

    def in_z(dz, c):
        return lax.rem(z + dz, 4) * 2 + c

    def in_head(x, dy):
        return x * 4 + lax.rem(y + dy, 4)

    def peer_c(i):
        return lax.rem(chip + i, 8)

    def peer_h(i):
        return lax.rem(head + i, NHEAD)

    sibling = in_seq(x_lo, 0, 1 - core)
    partner = in_seq(1 - x_lo, 0, core)
    partner_h = in_head(1 - x_hi, 0)
    turns = (1, 3, 2)

    barrier = pltpu.get_barrier_semaphore()
    pl.semaphore_signal(
        barrier, inc=1, device_id={"seq": sibling}, device_id_type=pl.DeviceIdType.MESH
    )

    @pl.loop(1, 8)
    def _(i):
        pl.semaphore_signal(
            barrier,
            inc=1,
            device_id={"seq": at_chip(peer_c(i))},
            device_id_type=pl.DeviceIdType.MESH,
        )
        pl.semaphore_signal(
            barrier, inc=1, device_id={"head": peer_h(i)}, device_id_type=pl.DeviceIdType.MESH
        )

    loads = [
        pltpu.make_async_copy(source, target, in_sem.at[n])
        for n, (source, target) in enumerate(
            (
                (k_ref, k_in),
                (v_ref, v_in),
                (q_ref, q_in),
                (dy_ref, raw.at[head]),
                (w_ref.at[0:48], ws.at[head, 0:48]),
                (w_ref.at[48:96], ws.at[head, 64:112]),
            )
        )
    ]
    for load in loads:
        load.start()

    slide_col = lax.rem(iota((128, 128), 0), HALF) - HEAD
    below = jnp.zeros((128, 128), F32)
    upto = jnp.zeros((128, 128), F32)
    for s in range(8):
        ids = id_ref[s : s + 1, :]
        below = below + jnp.where(ids < slide_col, 1.0, 0.0)
        upto = upto + jnp.where(ids <= slide_col, 1.0, 0.0)
    ones = jnp.ones((8, 128), BF16)
    first_row = nt(ones, below.astype(BF16))[0:1, :]
    last_row = nt(ones, upto.astype(BF16))[0:1, :]
    first_col = jnp.sum(below, axis=1, keepdims=True)
    last_col = jnp.sum(upto, axis=1, keepdims=True)

    shift0 = shift_ref[2 * head]
    shift1 = shift_ref[2 * head + 1]
    lane_row = iota((1, 128), 1)
    lane_col = iota((128, 1), 0)
    shift_row = jnp.where(lane_row < HALF, shift0, shift1)
    shift_col = jnp.where(lane_col < HALF, shift0, shift1)
    hot_row = lax.rem(lane_row, HALF) >= HEAD
    hot_col = lax.rem(lane_col, HALF) >= HEAD

    def turned(shift, j):
        return jnp.bitwise_and(shift + 1 + j, RATE - 1)

    def to_slot(parts, shift, j):
        out = parts[0]
        for r in range(1, RATE):
            out = jnp.where(turned(shift, j) == r, parts[r], out)
        return out

    def from_slot(parts, shift, r):
        out = parts[0]
        for j in range(1, RATE):
            out = jnp.where(turned(shift, j) == r, parts[j], out)
        return out

    within = lax.rem(lane_col, HALF)
    source = (lane_col // HALF) * (RATE * HEAD) + within
    given = iota((128, 384), 1)
    for r in range(RATE):
        held = jnp.where(within < HEAD, source + r * HEAD, -1)
        perm[r * 128 : (r + 1) * 128] = jnp.where(given == held, 1.0, 0.0).astype(BF16)
    pl.semaphore_wait(barrier, 15)

    def dy_copy(owner, i, dst, first=False):
        source = dy_ref if first else raw.at[owner]
        return remote(source, raw.at[owner], dy_send.at[i], dy_recv.at[owner], "head", dst)

    dy_copy(head, 0, partner_h, True).start()
    dy_copy(head, 1, in_head(x_hi, 2), True).start()

    loads[0].wait()
    loads[1].wait()
    k_p = nt(k_in[...], perm[...])
    v_p = nt(v_in[...], perm[...])
    one_row = jnp.where(lax.rem(lane_row, HALF) == HEAD, 1.0, 0.0)
    one_col = jnp.where(lax.rem(lane_col, HALF) == HEAD, 1.0, 0.0)
    far_k = jnp.zeros((ROWS, 128), F32)
    far_v = jnp.zeros((ROWS, 128), F32)
    for r in range(RATE):
        at = (iota((ROWS, 128), 0) * RATE + r).astype(F32)
        hot = jnp.where(hot_row & (at >= first_row) & (at < last_row), 1.0, 0.0)
        k_r = k_p[:, r * 128 : (r + 1) * 128] + hot
        v_r = v_p[:, r * 128 : (r + 1) * 128] + one_row
        near_k[r] = k_r.astype(BF16)
        near_v[r] = v_r.astype(BF16)
        far_k = jnp.where(shift_row == r, k_r, far_k)
        far_v = jnp.where(shift_row == r, v_r, far_v)
    own = in_z(0, core)
    kv[own, 0] = far_k.astype(BF16)
    kv[own, 1] = far_v.astype(BF16)

    def kv_copy(slot, i, dst):
        return remote(kv.at[slot], kv.at[slot], kv_send.at[i], kv_recv.at[slot], "seq", dst)

    def swap(i, source, target):
        return remote(source, target, swap_send.at[i], swap_recv.at[i], "seq", partner)

    def w_copy(owner, i):
        part = ws.at[owner, pl.ds(pl.multiple_of(core * HALF, HALF), HEAD)]
        return remote(part, part, w_send.at[i], w_recv.at[owner], "head", peer_h(i))

    def w_share(owner, half):
        part = ws.at[owner, pl.ds(pl.multiple_of(half * HALF, HALF), HEAD)]
        return remote(part, part, ws_send.at[owner], ws_recv.at[owner], "seq", sibling)

    for n, turn in enumerate(turns):
        kv_copy(own, n, in_seq(x_lo, turn, core)).start()
    kv_copy(own, 3, sibling).start()
    for n, turn in enumerate((1, 3)):
        dy_copy(head, 2 + n, in_head(x_hi, turn), True).start()
    loads[2].wait()
    q_p = nt(q_in[...], perm[...])
    q_pt = nt(perm[...], q_in[...])
    k_pt = nt(perm[...], k_in[...])
    v_pt = nt(perm[...], v_in[...])
    for r in range(RATE):
        near_kt[r] = k_pt[r * 128 : (r + 1) * 128].astype(BF16)
        near_vt[r] = (v_pt[r * 128 : (r + 1) * 128] + one_col).astype(BF16)
    q_rows = []
    q_cols = []
    for r in range(RATE):
        at = (iota((128, ROWS), 1) * RATE + r).astype(F32)
        hot = jnp.where(hot_col & (at >= first_col) & (at < last_col), SAME, 0.0)
        q_rows.append(q_p[:, r * 128 : (r + 1) * 128])
        q_cols.append(q_pt[r * 128 : (r + 1) * 128, :] + hot)
    for j in reversed(range(RATE)):
        q_j = to_slot(q_rows, shift_row, j)
        q_jt = to_slot(q_cols, shift_col, j)
        q_n[0, j] = jnp.where(lane_row < HALF, q_j, 0.0).astype(BF16)
        q_n[1, j] = jnp.where(lane_row < HALF, 0.0, q_j).astype(BF16)
        if j == 3:
            at = (iota((ROWS, 128), 0) * RATE + shift_row).astype(F32)
            hot = jnp.where(hot_row & (at >= first_row) & (at < last_row), SAME, 0.0)
            q_far[...] = (q_j + hot).astype(BF16)
            swap(0, q_far, q_got).start()
        q_t[0, j] = jnp.where(lane_col < HALF, q_jt, 0.0).astype(BF16)
        q_t[1, j] = jnp.where(lane_col < HALF, 0.0, q_jt).astype(BF16)

    halves = (slice(0, HALF), slice(HALF, 2 * HALF))

    def forward(keys, vals_t, chains, q_of, e_of):
        top = {}
        for b in range(4):
            for c in chains:
                s = nn(keys(b), q_of(*c))
                e_of(*c)[b] = s
                m = jnp.max(s, axis=0, keepdims=True)
                top[c] = m if b == 0 else jnp.maximum(top[c], m)
        out = {c: jnp.zeros((HALF, ROWS), F32) for c in chains}
        for b in range(4):
            for c in chains:
                e = jnp.exp2((e_of(*c)[b] - top[c]) * EXP2)
                e_of(*c)[b] = e
                out[c] = out[c] + nn(vals_t(b)[halves[c[1]]], e.astype(BF16))
        return {c: (top[c], out[c][HEAD : HEAD + 1], out[c]) for c in chains}

    @pl.loop(0, 2)
    def _(pair):
        tiles = forward(
            lambda b: near_k[b],
            lambda b: near_vt[b],
            [(d, h) for d in range(2) for h in range(2)],
            lambda d, h: q_t[h, 2 * pair + d],
            lambda d, h: e_near.at[h, 2 * pair + d],
        )
        for (d, h), (top, total, out) in tiles.items():
            if d == 1:
                top_n[h] = top
                sum_n[h] = total
                out_n[h] = out
            inverse = 1.0 / total
            fac_n[h, 2 * pair + d] = inverse
            attn_t[2 * pair + d, halves[h]] = (out * inverse).astype(BF16)

        @pl.when(pair == 0)
        def _():
            dy_copy(partner_h, 0, partner_h).wait_recv()
            for n, turn in enumerate((1, 3)):
                dy_copy(partner_h, 4 + n, in_head(x_hi, turn)).start()
            dy_copy(in_head(x_hi, 2), 0, partner_h).wait_recv()
            dy_copy(in_head(x_hi, 2), 6, partner_h).start()

    def share(i):
        slot = in_z(i + i // 2 - 2 * (i // 3), core)
        kv_copy(slot, 0, partner).wait_recv()
        kv_copy(slot, 3 + i, sibling).start()

    share(1)
    swap(0, q_far, q_got).wait_recv()
    q_j = q_got[...].astype(F32)
    q_jt = q_j.T
    q_n[0, 4] = jnp.where(lane_row < HALF, q_j, 0.0).astype(BF16)
    q_n[1, 4] = jnp.where(lane_row < HALF, 0.0, q_j).astype(BF16)
    q_t[0, 4] = jnp.where(lane_col < HALF, q_jt, 0.0).astype(BF16)
    q_t[1, 4] = jnp.where(lane_col < HALF, 0.0, q_jt).astype(BF16)

    def far_block(n):
        i = n // 2
        return in_z(i + i // 2 - 2 * (i // 3), lax.rem(n, 2))

    kv_copy(in_z(0, 1 - core), 0, partner).wait_recv()
    kv_copy(in_z(1, 1 - core), 0, partner).wait_recv()

    def turn_values(g):
        for b in range(4):
            far_vt[4 * g + b] = kv[far_block(4 * g + b), 1].T

    turn_values(0)

    @pl.loop(0, 4)
    def _(step):
        g = lax.rem(step, 2)
        own_q = step // 2

        @pl.when(step == 1)
        def _():
            for i in (2, 3):
                share(i)
            for dz in (3, 2):
                kv_copy(in_z(dz, 1 - core), 0, partner).wait_recv()
            turn_values(1)

        @pl.when(step == 2)
        def _():
            for h in range(2):
                top = jnp.maximum(top_f[0, h, 0], top_f[0, h, 1])
                w0 = jnp.exp2((top_f[0, h, 0] - top) * EXP2)
                w1 = jnp.exp2((top_f[0, h, 1] - top) * EXP2)
                m_far[h : h + 1] = top
                m_far[2 + h : 3 + h] = w0 * sum_f[0, h, 0] + w1 * sum_f[0, h, 1]
                o_far[halves[h]] = (w0 * out_f[0, h, 0] + w1 * out_f[0, h, 1]).astype(BF16)
            m_far[4:8] = jnp.zeros((4, ROWS), F32)
            swap(1, m_far, m_got).start()
            swap(2, o_far, o_got).start()

        tiles = forward(
            lambda b: kv[far_block(4 * g + b), 0],
            lambda b: far_vt[4 * g + b],
            [(0, h) for h in range(2)],
            lambda d, h: q_t[h, 4 - own_q],
            lambda d, h: e_far.at[own_q, h, pl.ds(4 * g, 4)],
        )
        for (_, h), (top, total, out) in tiles.items():
            top_f[own_q, h, g] = top
            sum_f[own_q, h, g] = total
            out_f[own_q, h, g] = out

    for turn in (1, 3):
        for x in range(2):
            dy_copy(in_head(x, turn), 0, partner_h).wait_recv()
    dy_copy(in_head(1 - x_hi, 2), 0, partner_h).wait_recv()
    loads[3].wait()
    loads[4].wait()
    loads[5].wait()
    zeros16 = jnp.zeros((16, WIDTH), BF16)
    for h in range(NHEAD):
        ws[h, 48:64] = zeros16
        ws[h, 112:128] = zeros16
    rm_row = iota((128, 128), 0)
    rm_col = iota((128, 128), 1)
    to_rm = jnp.where(rm_col == lax.rem(rm_row, 32) * RATE + rm_row // 32, 1.0, 0.0).astype(BF16)

    for h in range(NHEAD):
        rows = nn(to_rm, raw[h]).astype(BF16)
        for r in range(RATE):
            dys[r, h * 32 : (h + 1) * 32] = rows[r * 32 : (r + 1) * 32]
    w_own = ws[head]
    g_rows = []
    g_cols = []
    for r in range(RATE):
        g_rows.append(nt(dys[r], w_own))
        g_cols.append(nt(w_own, dys[r]))
    for j in reversed(range(RATE)):
        g_j = to_slot(g_rows, shift_row, j)
        g_jt = to_slot(g_cols, shift_col, j)
        g_n[0, j] = jnp.where(lane_row < HALF, g_j, 0.0).astype(BF16)
        g_n[1, j] = jnp.where(lane_row < HALF, 0.0, g_j).astype(BF16)
        g_t[0, j] = jnp.where(lane_col < HALF, g_jt, 0.0).astype(BF16)
        g_t[1, j] = jnp.where(lane_col < HALF, 0.0, g_jt).astype(BF16)
        if j == 3:
            g_far[...] = g_j.astype(BF16)
            swap(3, g_far, g_got).start()
    swap(1, m_far, m_got).wait_recv()
    swap(2, o_far, o_got).wait_recv()
    for h in range(2):
        tops = [top_n[h], top_f[1, h, 0], top_f[1, h, 1], m_got[h : h + 1]]
        sums = [sum_n[h], sum_f[1, h, 0], sum_f[1, h, 1], m_got[2 + h : 3 + h]]
        outs = [out_n[h], out_f[1, h, 0], out_f[1, h, 1], o_got[halves[h]].astype(F32)]
        top = tops[0]
        for other in tops[1:]:
            top = jnp.maximum(top, other)
        weights = [jnp.exp2((other - top) * EXP2) for other in tops]
        total = weights[0] * sums[0]
        out = weights[0] * outs[0]
        for n in range(1, 4):
            total = total + weights[n] * sums[n]
            out = out + weights[n] * outs[n]
        inverse = 1.0 / total
        fac_n[h, 3] = weights[0] * inverse
        for g in range(2):
            fac_f[1, h, g] = weights[1 + g] * inverse
        t_far[h : h + 1] = top
        t_far[2 + h : 3 + h] = inverse
        attn_t[3, halves[h]] = (out * inverse).astype(BF16)

    for j in range(RATE):
        for h in range(2):
            product = g_t[h, j, halves[h], :].astype(F32) * attn_t[j, halves[h]].astype(F32)
            delta[h, j] = jnp.sum(product, axis=0, keepdims=True)
    t_far[4:5] = delta[0, 3]
    t_far[5:6] = delta[1, 3]
    t_far[6:8] = jnp.zeros((2, ROWS), F32)
    swap(4, t_far, t_got).start()

    attn_slots = [attn_t[j].astype(F32) for j in range(RATE)]
    attn_rt = [from_slot(attn_slots, shift_col, r) for r in range(RATE)]
    for r in range(RATE):
        attn_n[r] = attn_rt[r].T.astype(BF16)

    own_rows = pl.ds(pl.multiple_of(head * 32, 32), 32)

    def at_copy(slot, i):
        rows = pl.ds(pl.multiple_of(peer_h(i) * 32, 32), 32)
        return remote(
            attn_n.at[:, rows, :], attn_r.at[slot], at_send.at[i], at_recv.at[slot], "head", peer_h(i)
        )

    for n in range(1, NHEAD):
        at_copy(head, n).start()
    for r in range(RATE):
        attn_r[head, r] = attn_n[r, own_rows, :]

    weight_grad = jnp.zeros((128, WIDTH), F32)
    for r in range(RATE):
        weight_grad = weight_grad + nn(attn_rt[r].astype(BF16), dys[r])

    for half in range(2):
        for n in range(8):
            dwp[half, n] = weight_grad[n * 16 : (n + 1) * 16, half * 384 : (half + 1) * 384]

    def dx_copy(half):
        return remote(dwp.at[half], dwx, dx_sem.at[0], dx_sem.at[1], "seq", sibling)

    def dw_copy(sender, i):
        dst = peer_c(i)
        return remote(dwm.at[dst], dwr.at[sender], dw_send.at[i], dw_recv.at[sender], "seq", at_chip(dst))

    def df_copy(sender, i):
        part = dwf.at[core, sender]
        return remote(part, part, df_send.at[i], df_recv.at[sender], "seq", at_chip(peer_c(i)))

    def dc_copy(half):
        return remote(dwf.at[half], dwf.at[half], dc_sem.at[0], dc_sem.at[1], "seq", sibling)

    dx_copy(1 - core).start()

    def weight_over_cores():
        dx_copy(core).wait_recv()
        dwm[...] = dwp[core] + dwx[...]
        for n in range(1, 8):
            dw_copy(chip, n).start()

    def weight_over_chips():
        for n in range(1, 8):
            dw_copy(peer_c(n), n).wait_recv()
        dwr[chip] = dwm[chip]
        part = dwr[0]
        for n in range(1, 8):
            part = part + dwr[n]
        dwf[core, chip] = part.astype(BF16)
        for n in range(1, 8):
            df_copy(chip, n).start()

    def weight_to_sibling():
        for n in range(1, 8):
            df_copy(peer_c(n), n).wait_recv()
        dc_copy(core).start()

    def backward(count, keys_t, vals, queries, e_of, factor, put):
        dq = [[jnp.zeros((HALF, ROWS), F32) for h in range(2)] for _ in queries]
        pairs = [(n, h, j) for n, j in enumerate(queries) for h in range(2)]

        def products(b):
            return [nn(vals(b), g_t[h, j]) for _, h, j in pairs]

        ahead = products(0)
        for b in range(count):
            k_t = keys_t(b)
            now, ahead = ahead, products(b + 1) if b + 1 < count else None
            dk = jnp.zeros((ROWS, 128), F32)
            dv = jnp.zeros((ROWS, 128), F32)
            for (n, h, j), d_prob in zip(pairs, now, strict=True):
                p = e_of(n, h, b) * factor(n, h)
                ds = (p * (d_prob - delta[h, j])).astype(BF16)
                dv = dv + nn(p.astype(BF16), g_n[h, j])
                dk = dk + nn(ds, q_n[h, j])
                dq[n][h] = dq[n][h] + nn(k_t[halves[h]], ds)
            put(b, dk, dv)
        return dq

    acc_k[...] = jnp.zeros((4, ROWS, 128), F32)
    acc_v[...] = jnp.zeros((4, ROWS, 128), F32)

    def near_backward(j):
        def put(b, dk, dv):
            acc_k[b] = acc_k[b] + dk
            acc_v[b] = acc_v[b] + dv

        dq = backward(
            4,
            lambda b: near_kt[b],
            lambda b: near_v[b],
            [j],
            lambda n, h, b: e_near[h, j, b],
            lambda n, h: fac_n[h, j],
            put,
        )
        for h in range(2):
            acc_q[j, halves[h]] = dq[0][h]

    @pl.loop(0, EARLY)
    def _(j):
        near_backward(j)

        @pl.when(j == 0)
        def _():
            weight_over_cores()

    swap(3, g_far, g_got).wait_recv()
    swap(4, t_far, t_got).wait_recv()
    g_j = g_got[...].astype(F32)
    g_jt = g_j.T
    g_n[0, 4] = jnp.where(lane_row < HALF, g_j, 0.0).astype(BF16)
    g_n[1, 4] = jnp.where(lane_row < HALF, 0.0, g_j).astype(BF16)
    g_t[0, 4] = jnp.where(lane_col < HALF, g_jt, 0.0).astype(BF16)
    g_t[1, 4] = jnp.where(lane_col < HALF, 0.0, g_jt).astype(BF16)
    for h in range(2):
        delta[h, 4] = t_got[4 + h : 5 + h]
        for g in range(2):
            weight = jnp.exp2((top_f[0, h, g] - t_got[h : h + 1]) * EXP2)
            fac_f[0, h, g] = weight * t_got[2 + h : 3 + h]

    def gx_copy(slot):
        return remote(
            gkv_s.at[slot], gkv_x.at[slot], gx_send.at[slot], gx_recv.at[slot], "seq", sibling
        )

    def grad_copy(dz):
        return remote(
            gkv_s.at[in_z(dz, core)],
            gkv_r.at[dz],
            g_send.at[dz],
            g_recv.at[dz],
            "seq",
            in_seq(x_lo, dz, core),
        )

    def merge(i):
        dz = i + i // 2 - 2 * (i // 3)
        slot = in_z(dz, core)
        gx_copy(slot).wait_recv()
        for n in range(2):
            gkv_s[slot, n] = (gkv_s[slot, n].astype(F32) + gkv_x[slot, n].astype(F32)).astype(BF16)

        @pl.when(dz != 0)
        def _():
            grad_copy(dz).start()

    for j in (3, 4):
        acc_q[j] = jnp.zeros((128, ROWS), F32)

    @pl.loop(0, 4)
    def _(back):
        i = 3 - back
        dz = i + i // 2 - 2 * (i // 3)

        def put(b, dk, dv):
            slot = in_z(dz, b)
            gkv_s[slot, 0] = dk.astype(BF16)
            gkv_s[slot, 1] = dv.astype(BF16)

            @pl.when(core != b)
            def _():
                gx_copy(slot).start()

        dq = backward(
            2,
            lambda b: kv[in_z(dz, b), 0].T,
            lambda b: kv[in_z(dz, b), 1],
            [4, 3],
            lambda n, h, b: e_far[n, h, 2 * i + b],
            lambda n, h: fac_f[n, h, i // 2],
            put,
        )
        for n, j in enumerate((4, 3)):
            for h in range(2):
                acc_q[j, halves[h]] = acc_q[j, halves[h]] + dq[n][h]

        @pl.when(back > 0)
        def _():
            merge(i + 1)

        @pl.when(back == 0)
        def _():
            for n in range(1, NHEAD):
                w_copy(head, n).start()

        @pl.when(back == 2)
        def _():
            weight_over_chips()

    dq_far[...] = acc_q[4].astype(BF16)
    swap(5, dq_far, dq_got).start()
    acc_q[4] = acc_q[3]
    merge(0)

    @pl.loop(EARLY, RATE)
    def _(j):
        near_backward(j)

    for n in range(1, NHEAD):
        w_copy(peer_h(n), n).wait_recv()
        w_share(peer_h(n), core).start()
    swap(5, dq_far, dq_got).wait_recv()
    acc_q[3] = acc_q[3] + acc_q[4] + dq_got[...].astype(F32)
    dq_slots = [(acc_q[j] * SCALE).T for j in range(RATE)]
    dq_parts = [from_slot(dq_slots, shift_row, r).astype(BF16) for r in range(RATE)]
    dq_ref[...] = nn(jnp.concatenate(dq_parts, axis=1), perm[...]).astype(BF16)

    weight_to_sibling()
    for n in range(1, NHEAD):
        w_share(peer_h(n), 1 - core).wait_recv()
        at_copy(peer_h(n), n).wait_recv()
    from_rm = jnp.where(rm_row == lax.rem(rm_col, 32) * RATE + rm_col // 32, 1.0, 0.0).astype(BF16)
    result = jnp.zeros((128, WIDTH), F32)
    for h in range(NHEAD):
        rows = nn(from_rm, attn_r[h].reshape(128, 128)).astype(BF16)
        result = result + nn(rows, ws[h])
    lo_ref[...] = result.astype(BF16)

    for turn in turns:
        grad_copy(turn).wait_recv()
    far = []
    for n in range(2):
        total = gkv_s[own, n].astype(F32)
        for turn in turns:
            total = total + gkv_r[turn, n].astype(F32)
        far.append(total)
    sum_k, sum_v = far
    dk_parts = []
    dv_parts = []
    for r in range(RATE):
        mine = shift_row == r
        dk_parts.append(((acc_k[r] + jnp.where(mine, sum_k, 0.0)) * SCALE).astype(BF16))
        dv_parts.append((acc_v[r] + jnp.where(mine, sum_v, 0.0)).astype(BF16))
    dk_ref[...] = nn(jnp.concatenate(dk_parts, axis=1), perm[...]).astype(BF16)
    dv_ref[...] = nn(jnp.concatenate(dv_parts, axis=1), perm[...]).astype(BF16)

    dc_copy(1 - core).wait_recv()
    for half in range(2):
        whole = dwf[half].reshape(128, 384)
        dw_ref[0:48, half * 384 : (half + 1) * 384] = whole[0:48]
        dw_ref[48:96, half * 384 : (half + 1) * 384] = whole[64:112]

    dx_copy(1 - core).wait_send()
    dc_copy(core).wait_send()

    @pl.loop(0, 7)
    def _(i):
        kv_copy(own, i, partner).wait_send()

    @pl.loop(1, 8)
    def _(i):
        w_copy(head, i).wait_send()
        w_share(peer_h(i), core).wait_send()
        dy_copy(head, i - 1, partner_h).wait_send()
        at_copy(head, i).wait_send()
        dw_copy(chip, i).wait_send()
        df_copy(chip, i).wait_send()

    @pl.loop(0, 4)
    def _(i):
        gx_copy(i * 2 + 1 - core).wait_send()

    for turn in turns:
        grad_copy(turn).wait_send()
    swaps = ((q_far, q_got), (m_far, m_got), (o_far, o_got), (g_far, g_got), (t_far, t_got), (dq_far, dq_got))
    for i, (source, target) in enumerate(swaps):
        swap(i, source, target).wait_send()


def finish(*refs):
    for source, target in zip(refs[:5], refs[5:], strict=True):
        target[...] = source[...]


def body(queries, keys, values, slide_ids, head_shift_list, out_weight, d_y):
    vmem = pl.BlockSpec(memory_space=pltpu.VMEM)
    hbm = pl.BlockSpec(memory_space=pltpu.HBM)
    smem = pl.BlockSpec(memory_space=pltpu.SMEM)
    sems = pltpu.SemaphoreType.DMA
    results = pl.pallas_call(
        kernel,
        out_shape=(
            jax.ShapeDtypeStruct((128, WIDTH), BF16),
            jax.ShapeDtypeStruct((ROWS, 384), BF16),
            jax.ShapeDtypeStruct((ROWS, 384), BF16),
            jax.ShapeDtypeStruct((ROWS, 384), BF16),
            jax.ShapeDtypeStruct((96, WIDTH), BF16),
        ),
        in_specs=[hbm, hbm, hbm, vmem, smem, hbm, hbm],
        out_specs=(vmem,) * 5,
        scratch_shapes=[
            pltpu.VMEM((ROWS, 384), BF16),
            pltpu.VMEM((ROWS, 384), BF16),
            pltpu.VMEM((ROWS, 384), BF16),
            pltpu.VMEM((NHEAD, 128, WIDTH), BF16),
            pltpu.VMEM((4 * 128, 384), BF16),
            pltpu.VMEM((4, ROWS, 128), BF16),
            pltpu.VMEM((4, ROWS, 128), BF16),
            pltpu.VMEM((4, 128, ROWS), BF16),
            pltpu.VMEM((4, 128, ROWS), BF16),
            pltpu.VMEM((8, 2, ROWS, 128), BF16),
            pltpu.VMEM((8, 128, ROWS), BF16),
            pltpu.VMEM((RATE, ROWS, 128), BF16),
            pltpu.VMEM((2, 5, 128, ROWS), BF16),
            pltpu.VMEM((2, 5, ROWS, 128), BF16),
            pltpu.VMEM((2, 5, 128, ROWS), BF16),
            pltpu.VMEM((2, 5, ROWS, 128), BF16),
            pltpu.VMEM((2, RATE, 4, ROWS, ROWS), F32),
            pltpu.VMEM((2, 2, 8, ROWS, ROWS), F32),
            pltpu.VMEM((2, 1, ROWS), F32),
            pltpu.VMEM((2, 1, ROWS), F32),
            pltpu.VMEM((2, HALF, ROWS), F32),
            pltpu.VMEM((2, 2, 2, 1, ROWS), F32),
            pltpu.VMEM((2, 2, 2, 1, ROWS), F32),
            pltpu.VMEM((2, 2, 2, HALF, ROWS), F32),
            pltpu.VMEM((2, RATE, 1, ROWS), F32),
            pltpu.VMEM((2, 2, 2, 1, ROWS), F32),
            pltpu.VMEM((2, 5, 1, ROWS), F32),
            pltpu.VMEM((RATE, 128, ROWS), BF16),
            pltpu.VMEM((RATE, ROWS, 128), BF16),
            pltpu.VMEM((NHEAD, RATE, 32, 128), BF16),
            pltpu.VMEM((RATE, ROWS, WIDTH), BF16),
            pltpu.VMEM((NHEAD, 128, WIDTH), BF16),
            pltpu.VMEM((2, 8, 16, 384), F32),
            pltpu.VMEM((8, 16, 384), F32),
            pltpu.VMEM((8, 16, 384), F32),
            pltpu.VMEM((8, 16, 384), F32),
            pltpu.VMEM((2, 8, 16, 384), BF16),
            pltpu.VMEM((8, 2, ROWS, 128), BF16),
            pltpu.VMEM((8, 2, ROWS, 128), BF16),
            pltpu.VMEM((4, 2, ROWS, 128), BF16),
            pltpu.VMEM((ROWS, 128), BF16),
            pltpu.VMEM((ROWS, 128), BF16),
            pltpu.VMEM((ROWS, 128), BF16),
            pltpu.VMEM((ROWS, 128), BF16),
            pltpu.VMEM((128, ROWS), BF16),
            pltpu.VMEM((128, ROWS), BF16),
            pltpu.VMEM((8, ROWS), F32),
            pltpu.VMEM((8, ROWS), F32),
            pltpu.VMEM((8, ROWS), F32),
            pltpu.VMEM((8, ROWS), F32),
            pltpu.VMEM((128, ROWS), BF16),
            pltpu.VMEM((128, ROWS), BF16),
            pltpu.VMEM((4, ROWS, 128), F32),
            pltpu.VMEM((4, ROWS, 128), F32),
            pltpu.VMEM((5, 128, ROWS), F32),
            sems((6,)),
            sems((8,)),
            sems((8,)),
            sems((NHEAD,)),
            sems((NHEAD,)),
            sems((NHEAD,)),
            sems((NHEAD,)),
            sems((NHEAD,)),
            sems((NHEAD,)),
            sems((NHEAD,)),
            sems((NHEAD,)),
            sems((2,)),
            sems((8,)),
            sems((8,)),
            sems((8,)),
            sems((8,)),
            sems((2,)),
            sems((8,)),
            sems((8,)),
            sems((4,)),
            sems((4,)),
            sems((6,)),
            sems((6,)),
        ],
        compiler_params=pltpu.CompilerParams(
            collective_id=0, has_side_effects=True, vmem_limit_bytes=56 * 1024 * 1024
        ),
        cost_estimate=pl.CostEstimate(
            flops=3_000_000_000, bytes_accessed=4_000_000, transcendentals=5_000_000
        ),
    )(
        queries,
        keys,
        values,
        slide_ids.reshape(8, 128),
        head_shift_list,
        out_weight,
        d_y,
    )
    return pl.pallas_call(
        finish,
        out_shape=tuple(jax.ShapeDtypeStruct(r.shape, r.dtype) for r in results),
        in_specs=[vmem] * 5,
        out_specs=(vmem,) * 5,
    )(*results)


def solution(mesh):
    placed = (
        P("seq", "head"),
        P("seq", "head"),
        P("seq", "head"),
        P("seq"),
        P(),
        P("head", None),
        P(("seq", "head"), None),
    )
    return jax.shard_map(
        body,
        mesh=mesh,
        in_specs=placed,
        out_specs=(
            P(("seq", "head"), None),
            P("seq", "head"),
            P("seq", "head"),
            P("seq", "head"),
            P("head", None),
        ),
        check_vma=False,
    )
```

```python
import math

import jax
import jax.numpy as jnp
from jax import lax
from jax.experimental import pallas as pl
from jax.experimental.pallas import tpu as pltpu
from jax.sharding import PartitionSpec as P

HEAD = 48
HALF = 64
RATE = 4
ROWS = 256
WIDTH = 768
NSEQ = 16
NHEAD = 8
EARLY = 2
SAME = 8192.0
SCALE = 1.0 / math.sqrt(HEAD)
EXP2 = SCALE * math.log2(math.e)
F32 = jnp.float32
BF16 = jnp.bfloat16


def nt(a, b):
    return lax.dot_general(a, b, (((1,), (1,)), ((), ())), preferred_element_type=F32)


def nn(a, b):
    return jnp.dot(a, b, preferred_element_type=F32)


def iota(shape, dim):
    return lax.broadcasted_iota(jnp.int32, shape, dim)


def remote(src, dst, send, recv, axis, index):
    return pltpu.make_async_remote_copy(
        src_ref=src,
        dst_ref=dst,
        send_sem=send,
        recv_sem=recv,
        device_id={axis: index},
        device_id_type=pl.DeviceIdType.MESH,
    )


def kernel(
    q_ref,
    k_ref,
    v_ref,
    id_ref,
    shift_ref,
    w_ref,
    dy_ref,
    lo_ref,
    dq_ref,
    dk_ref,
    dv_ref,
    dw_ref,
    q_in,
    k_in,
    v_in,
    raw,
    perm,
    near_k,
    near_v,
    near_kt,
    near_vt,
    kv,
    far_vt,
    g_raw,
    q_t,
    q_n,
    g_t,
    g_n,
    e_near,
    e_far,
    top_n,
    sum_n,
    out_n,
    top_f,
    sum_f,
    out_f,
    fac_n,
    fac_f,
    delta,
    attn_t,
    attn_n,
    attn_r,
    dys,
    ws,
    dwp,
    dwx,
    dwm,
    dwr,
    dwf,
    gkv_s,
    gkv_x,
    gkv_r,
    q_far,
    q_got,
    g_far,
    g_got,
    o_far,
    o_got,
    m_far,
    m_got,
    t_far,
    t_got,
    dq_far,
    dq_got,
    acc_k,
    acc_v,
    acc_q,
    in_sem,
    kv_send,
    kv_recv,
    dy_send,
    dy_recv,
    w_send,
    w_recv,
    ws_send,
    ws_recv,
    at_send,
    at_recv,
    dx_sem,
    dw_send,
    dw_recv,
    df_send,
    df_recv,
    dc_sem,
    gx_send,
    gx_recv,
    g_send,
    g_recv,
    swap_send,
    swap_recv,
):
    seq = lax.axis_index("seq")
    head = lax.axis_index("head")

    x_lo, z, core = seq // 8, lax.rem(seq // 2, 4), lax.rem(seq, 2)
    x_hi, y = head // 4, lax.rem(head, 4)
    chip = seq // 2

    def at_chip(j):
        return j * 2 + core

    def in_seq(x, dz, c):
        return x * 8 + lax.rem(z + dz, 4) * 2 + c

    def in_z(dz, c):
        return lax.rem(z + dz, 4) * 2 + c

    def in_head(x, dy):
        return x * 4 + lax.rem(y + dy, 4)

    def peer_c(i):
        return lax.rem(chip + i, 8)

    def peer_h(i):
        return lax.rem(head + i, NHEAD)

    sibling = in_seq(x_lo, 0, 1 - core)
    partner = in_seq(1 - x_lo, 0, core)
    partner_h = in_head(1 - x_hi, 0)
    turns = (1, 3, 2)

    barrier = pltpu.get_barrier_semaphore()
    pl.semaphore_signal(
        barrier, inc=1, device_id={"seq": sibling}, device_id_type=pl.DeviceIdType.MESH
    )

    @pl.loop(1, 8)
    def _(i):
        pl.semaphore_signal(
            barrier,
            inc=1,
            device_id={"seq": at_chip(peer_c(i))},
            device_id_type=pl.DeviceIdType.MESH,
        )
        pl.semaphore_signal(
            barrier, inc=1, device_id={"head": peer_h(i)}, device_id_type=pl.DeviceIdType.MESH
        )

    loads = [
        pltpu.make_async_copy(source, target, in_sem.at[n])
        for n, (source, target) in enumerate(
            (
                (k_ref, k_in),
                (v_ref, v_in),
                (q_ref, q_in),
                (dy_ref, raw.at[head]),
                (w_ref.at[0:48], ws.at[head, 0:48]),
                (w_ref.at[48:96], ws.at[head, 64:112]),
            )
        )
    ]
    for load in loads:
        load.start()

    slide_col = lax.rem(iota((128, 128), 0), HALF) - HEAD
    below = jnp.zeros((128, 128), F32)
    upto = jnp.zeros((128, 128), F32)
    for s in range(8):
        ids = id_ref[s : s + 1, :]
        below = below + jnp.where(ids < slide_col, 1.0, 0.0)
        upto = upto + jnp.where(ids <= slide_col, 1.0, 0.0)
    ones = jnp.ones((8, 128), BF16)
    first_row = nt(ones, below.astype(BF16))[0:1, :]
    last_row = nt(ones, upto.astype(BF16))[0:1, :]
    first_col = jnp.sum(below, axis=1, keepdims=True)
    last_col = jnp.sum(upto, axis=1, keepdims=True)

    shift0 = shift_ref[2 * head]
    shift1 = shift_ref[2 * head + 1]
    lane_row = iota((1, 128), 1)
    lane_col = iota((128, 1), 0)
    shift_row = jnp.where(lane_row < HALF, shift0, shift1)
    shift_col = jnp.where(lane_col < HALF, shift0, shift1)
    hot_row = lax.rem(lane_row, HALF) >= HEAD
    hot_col = lax.rem(lane_col, HALF) >= HEAD

    def turned(shift, j):
        return jnp.bitwise_and(shift + 1 + j, RATE - 1)

    def to_slot(parts, shift, j):
        out = parts[0]
        for r in range(1, RATE):
            out = jnp.where(turned(shift, j) == r, parts[r], out)
        return out

    def from_slot(parts, shift, r):
        out = parts[0]
        for j in range(1, RATE):
            out = jnp.where(turned(shift, j) == r, parts[j], out)
        return out

    within = lax.rem(lane_col, HALF)
    source = (lane_col // HALF) * (RATE * HEAD) + within
    given = iota((128, 384), 1)
    for r in range(RATE):
        held = jnp.where(within < HEAD, source + r * HEAD, -1)
        perm[r * 128 : (r + 1) * 128] = jnp.where(given == held, 1.0, 0.0).astype(BF16)
    pl.semaphore_wait(barrier, 15)

    def dy_copy(owner, i, dst, first=False):
        source = dy_ref if first else raw.at[owner]
        return remote(source, raw.at[owner], dy_send.at[i], dy_recv.at[owner], "head", dst)

    dy_copy(head, 0, partner_h, True).start()
    dy_copy(head, 1, in_head(x_hi, 2), True).start()

    loads[0].wait()
    loads[1].wait()
    k_p = nt(k_in[...], perm[...])
    v_p = nt(v_in[...], perm[...])
    one_row = jnp.where(lax.rem(lane_row, HALF) == HEAD, 1.0, 0.0)
    one_col = jnp.where(lax.rem(lane_col, HALF) == HEAD, 1.0, 0.0)
    far_k = jnp.zeros((ROWS, 128), F32)
    far_v = jnp.zeros((ROWS, 128), F32)
    for r in range(RATE):
        at = (iota((ROWS, 128), 0) * RATE + r).astype(F32)
        hot = jnp.where(hot_row & (at >= first_row) & (at < last_row), 1.0, 0.0)
        k_r = k_p[:, r * 128 : (r + 1) * 128] + hot
        v_r = v_p[:, r * 128 : (r + 1) * 128] + one_row
        near_k[r] = k_r.astype(BF16)
        near_v[r] = v_r.astype(BF16)
        far_k = jnp.where(shift_row == r, k_r, far_k)
        far_v = jnp.where(shift_row == r, v_r, far_v)
    own = in_z(0, core)
    kv[own, 0] = far_k.astype(BF16)
    kv[own, 1] = far_v.astype(BF16)

    def kv_copy(slot, i, dst):
        return remote(kv.at[slot], kv.at[slot], kv_send.at[i], kv_recv.at[slot], "seq", dst)

    def swap(i, source, target):
        return remote(source, target, swap_send.at[i], swap_recv.at[i], "seq", partner)

    def w_copy(owner, i):
        part = ws.at[owner, pl.ds(pl.multiple_of(core * HALF, HALF), HEAD)]
        return remote(part, part, w_send.at[i], w_recv.at[owner], "head", peer_h(i))

    def w_share(owner, half):
        part = ws.at[owner, pl.ds(pl.multiple_of(half * HALF, HALF), HEAD)]
        return remote(part, part, ws_send.at[owner], ws_recv.at[owner], "seq", sibling)

    for n, turn in enumerate(turns):
        kv_copy(own, n, in_seq(x_lo, turn, core)).start()
    kv_copy(own, 3, sibling).start()
    for n, turn in enumerate((1, 3)):
        dy_copy(head, 2 + n, in_head(x_hi, turn), True).start()
    loads[2].wait()
    q_p = nt(q_in[...], perm[...])
    q_pt = nt(perm[...], q_in[...])
    k_pt = nt(perm[...], k_in[...])
    v_pt = nt(perm[...], v_in[...])
    for r in range(RATE):
        near_kt[r] = k_pt[r * 128 : (r + 1) * 128].astype(BF16)
        near_vt[r] = (v_pt[r * 128 : (r + 1) * 128] + one_col).astype(BF16)
    q_rows = []
    q_cols = []
    for r in range(RATE):
        at = (iota((128, ROWS), 1) * RATE + r).astype(F32)
        hot = jnp.where(hot_col & (at >= first_col) & (at < last_col), SAME, 0.0)
        q_rows.append(q_p[:, r * 128 : (r + 1) * 128])
        q_cols.append(q_pt[r * 128 : (r + 1) * 128, :] + hot)
    for j in reversed(range(RATE)):
        q_j = to_slot(q_rows, shift_row, j)
        q_jt = to_slot(q_cols, shift_col, j)
        q_n[0, j] = jnp.where(lane_row < HALF, q_j, 0.0).astype(BF16)
        q_n[1, j] = jnp.where(lane_row < HALF, 0.0, q_j).astype(BF16)
        if j == 3:
            at = (iota((ROWS, 128), 0) * RATE + shift_row).astype(F32)
            hot = jnp.where(hot_row & (at >= first_row) & (at < last_row), SAME, 0.0)
            q_far[...] = (q_j + hot).astype(BF16)
            swap(0, q_far, q_got).start()
        q_t[0, j] = jnp.where(lane_col < HALF, q_jt, 0.0).astype(BF16)
        q_t[1, j] = jnp.where(lane_col < HALF, 0.0, q_jt).astype(BF16)

    halves = (slice(0, HALF), slice(HALF, 2 * HALF))

    def forward(keys, vals_t, chains, q_of, e_of):
        top = {}
        for b in range(4):
            for c in chains:
                s = nn(keys(b), q_of(*c))
                e_of(*c)[b] = s
                m = jnp.max(s, axis=0, keepdims=True)
                top[c] = m if b == 0 else jnp.maximum(top[c], m)
        out = {c: jnp.zeros((HALF, ROWS), F32) for c in chains}
        for b in range(4):
            for c in chains:
                e = jnp.exp2((e_of(*c)[b] - top[c]) * EXP2)
                e_of(*c)[b] = e
                out[c] = out[c] + nn(vals_t(b)[halves[c[1]]], e.astype(BF16))
        return {c: (top[c], out[c][HEAD : HEAD + 1], out[c]) for c in chains}

    @pl.loop(0, 2)
    def _(pair):
        tiles = forward(
            lambda b: near_k[b],
            lambda b: near_vt[b],
            [(d, h) for d in range(2) for h in range(2)],
            lambda d, h: q_t[h, 2 * pair + d],
            lambda d, h: e_near.at[h, 2 * pair + d],
        )
        for (d, h), (top, total, out) in tiles.items():
            if d == 1:
                top_n[h] = top
                sum_n[h] = total
                out_n[h] = out
            inverse = 1.0 / total
            fac_n[h, 2 * pair + d] = inverse
            attn_t[2 * pair + d, halves[h]] = (out * inverse).astype(BF16)

        @pl.when(pair == 0)
        def _():
            dy_copy(partner_h, 0, partner_h).wait_recv()
            for n, turn in enumerate((1, 3)):
                dy_copy(partner_h, 4 + n, in_head(x_hi, turn)).start()
            dy_copy(in_head(x_hi, 2), 0, partner_h).wait_recv()
            dy_copy(in_head(x_hi, 2), 6, partner_h).start()

    def share(i):
        slot = in_z(i + i // 2 - 2 * (i // 3), core)
        kv_copy(slot, 0, partner).wait_recv()
        kv_copy(slot, 3 + i, sibling).start()

    share(1)
    swap(0, q_far, q_got).wait_recv()
    q_j = q_got[...].astype(F32)
    q_jt = q_j.T
    q_n[0, 4] = jnp.where(lane_row < HALF, q_j, 0.0).astype(BF16)
    q_n[1, 4] = jnp.where(lane_row < HALF, 0.0, q_j).astype(BF16)
    q_t[0, 4] = jnp.where(lane_col < HALF, q_jt, 0.0).astype(BF16)
    q_t[1, 4] = jnp.where(lane_col < HALF, 0.0, q_jt).astype(BF16)

    def far_block(n):
        i = n // 2
        return in_z(i + i // 2 - 2 * (i // 3), lax.rem(n, 2))

    kv_copy(in_z(0, 1 - core), 0, partner).wait_recv()
    kv_copy(in_z(1, 1 - core), 0, partner).wait_recv()

    def turn_values(g):
        for b in range(4):
            far_vt[4 * g + b] = kv[far_block(4 * g + b), 1].T

    turn_values(0)

    @pl.loop(0, 2)
    def _(g):
        @pl.when(g == 1)
        def _():
            for i in (2, 3):
                share(i)
            for dz in (3, 2):
                kv_copy(in_z(dz, 1 - core), 0, partner).wait_recv()
            turn_values(1)

        tiles = forward(
            lambda b: kv[far_block(4 * g + b), 0],
            lambda b: far_vt[4 * g + b],
            [(d, h) for d in range(2) for h in range(2)],
            lambda d, h: q_t[h, 4 - d],
            lambda d, h: e_far.at[d, h, pl.ds(4 * g, 4)],
        )
        for (d, h), (top, total, out) in tiles.items():
            top_f[d, h, g] = top
            sum_f[d, h, g] = total
            out_f[d, h, g] = out

    for h in range(2):
        top = jnp.maximum(top_f[0, h, 0], top_f[0, h, 1])
        w0 = jnp.exp2((top_f[0, h, 0] - top) * EXP2)
        w1 = jnp.exp2((top_f[0, h, 1] - top) * EXP2)
        m_far[h : h + 1] = top
        m_far[2 + h : 3 + h] = w0 * sum_f[0, h, 0] + w1 * sum_f[0, h, 1]
        o_far[halves[h]] = (w0 * out_f[0, h, 0] + w1 * out_f[0, h, 1]).astype(BF16)
    m_far[4:8] = jnp.zeros((4, ROWS), F32)
    swap(1, m_far, m_got).start()
    swap(2, o_far, o_got).start()

    for turn in (1, 3):
        for x in range(2):
            dy_copy(in_head(x, turn), 0, partner_h).wait_recv()
    dy_copy(in_head(1 - x_hi, 2), 0, partner_h).wait_recv()
    loads[3].wait()
    loads[4].wait()
    loads[5].wait()
    zeros16 = jnp.zeros((16, WIDTH), BF16)
    for h in range(NHEAD):
        ws[h, 48:64] = zeros16
        ws[h, 112:128] = zeros16
    rm_row = iota((128, 128), 0)
    rm_col = iota((128, 128), 1)
    to_rm = jnp.where(rm_col == lax.rem(rm_row, 32) * RATE + rm_row // 32, 1.0, 0.0).astype(BF16)

    for h in range(NHEAD):
        rows = nn(to_rm, raw[h]).astype(BF16)
        for r in range(RATE):
            dys[r, h * 32 : (h + 1) * 32] = rows[r * 32 : (r + 1) * 32]
    w_own = ws[head]
    g_rows = []
    g_cols = []
    for r in range(RATE):
        g_rows.append(nt(dys[r], w_own))
        g_cols.append(nt(w_own, dys[r]))
    for j in reversed(range(RATE)):
        g_j = to_slot(g_rows, shift_row, j)
        g_jt = to_slot(g_cols, shift_col, j)
        g_n[0, j] = jnp.where(lane_row < HALF, g_j, 0.0).astype(BF16)
        g_n[1, j] = jnp.where(lane_row < HALF, 0.0, g_j).astype(BF16)
        g_t[0, j] = jnp.where(lane_col < HALF, g_jt, 0.0).astype(BF16)
        g_t[1, j] = jnp.where(lane_col < HALF, 0.0, g_jt).astype(BF16)
        if j == 3:
            g_far[...] = g_j.astype(BF16)
            swap(3, g_far, g_got).start()
    swap(1, m_far, m_got).wait_recv()
    swap(2, o_far, o_got).wait_recv()
    for h in range(2):
        tops = [top_n[h], top_f[1, h, 0], top_f[1, h, 1], m_got[h : h + 1]]
        sums = [sum_n[h], sum_f[1, h, 0], sum_f[1, h, 1], m_got[2 + h : 3 + h]]
        outs = [out_n[h], out_f[1, h, 0], out_f[1, h, 1], o_got[halves[h]].astype(F32)]
        top = tops[0]
        for other in tops[1:]:
            top = jnp.maximum(top, other)
        weights = [jnp.exp2((other - top) * EXP2) for other in tops]
        total = weights[0] * sums[0]
        out = weights[0] * outs[0]
        for n in range(1, 4):
            total = total + weights[n] * sums[n]
            out = out + weights[n] * outs[n]
        inverse = 1.0 / total
        fac_n[h, 3] = weights[0] * inverse
        for g in range(2):
            fac_f[1, h, g] = weights[1 + g] * inverse
        t_far[h : h + 1] = top
        t_far[2 + h : 3 + h] = inverse
        attn_t[3, halves[h]] = (out * inverse).astype(BF16)

    for j in range(RATE):
        for h in range(2):
            product = g_t[h, j, halves[h], :].astype(F32) * attn_t[j, halves[h]].astype(F32)
            delta[h, j] = jnp.sum(product, axis=0, keepdims=True)
    t_far[4:5] = delta[0, 3]
    t_far[5:6] = delta[1, 3]
    t_far[6:8] = jnp.zeros((2, ROWS), F32)
    swap(4, t_far, t_got).start()

    attn_slots = [attn_t[j].astype(F32) for j in range(RATE)]
    attn_rt = [from_slot(attn_slots, shift_col, r) for r in range(RATE)]
    for r in range(RATE):
        attn_n[r] = attn_rt[r].T.astype(BF16)

    own_rows = pl.ds(pl.multiple_of(head * 32, 32), 32)

    def at_copy(slot, i):
        rows = pl.ds(pl.multiple_of(peer_h(i) * 32, 32), 32)
        return remote(
            attn_n.at[:, rows, :], attn_r.at[slot], at_send.at[i], at_recv.at[slot], "head", peer_h(i)
        )

    for n in range(1, NHEAD):
        at_copy(head, n).start()
    for r in range(RATE):
        attn_r[head, r] = attn_n[r, own_rows, :]

    weight_grad = jnp.zeros((128, WIDTH), F32)
    for r in range(RATE):
        weight_grad = weight_grad + nn(attn_rt[r].astype(BF16), dys[r])

    for half in range(2):
        for n in range(8):
            dwp[half, n] = weight_grad[n * 16 : (n + 1) * 16, half * 384 : (half + 1) * 384]

    def dx_copy(half):
        return remote(dwp.at[half], dwx, dx_sem.at[0], dx_sem.at[1], "seq", sibling)

    def dw_copy(sender, i):
        dst = peer_c(i)
        return remote(dwm.at[dst], dwr.at[sender], dw_send.at[i], dw_recv.at[sender], "seq", at_chip(dst))

    def df_copy(sender, i):
        part = dwf.at[core, sender]
        return remote(part, part, df_send.at[i], df_recv.at[sender], "seq", at_chip(peer_c(i)))

    def dc_copy(half):
        return remote(dwf.at[half], dwf.at[half], dc_sem.at[0], dc_sem.at[1], "seq", sibling)

    dx_copy(1 - core).start()

    def weight_over_cores():
        dx_copy(core).wait_recv()
        dwm[...] = dwp[core] + dwx[...]
        for n in range(1, 8):
            dw_copy(chip, n).start()

    def weight_over_chips():
        for n in range(1, 8):
            dw_copy(peer_c(n), n).wait_recv()
        dwr[chip] = dwm[chip]
        part = dwr[0]
        for n in range(1, 8):
            part = part + dwr[n]
        dwf[core, chip] = part.astype(BF16)
        for n in range(1, 8):
            df_copy(chip, n).start()

    def weight_to_sibling():
        for n in range(1, 8):
            df_copy(peer_c(n), n).wait_recv()
        dc_copy(core).start()

    def backward(count, keys_t, vals, queries, e_of, factor, put):
        dq = [[jnp.zeros((HALF, ROWS), F32) for h in range(2)] for _ in queries]
        pairs = [(n, h, j) for n, j in enumerate(queries) for h in range(2)]

        def products(b):
            return [nn(vals(b), g_t[h, j]) for _, h, j in pairs]

        ahead = products(0)
        for b in range(count):
            k_t = keys_t(b)
            now, ahead = ahead, products(b + 1) if b + 1 < count else None
            dk = jnp.zeros((ROWS, 128), F32)
            dv = jnp.zeros((ROWS, 128), F32)
            for (n, h, j), d_prob in zip(pairs, now, strict=True):
                p = e_of(n, h, b) * factor(n, h)
                ds = (p * (d_prob - delta[h, j])).astype(BF16)
                dv = dv + nn(p.astype(BF16), g_n[h, j])
                dk = dk + nn(ds, q_n[h, j])
                dq[n][h] = dq[n][h] + nn(k_t[halves[h]], ds)
            put(b, dk, dv)
        return dq

    acc_k[...] = jnp.zeros((4, ROWS, 128), F32)
    acc_v[...] = jnp.zeros((4, ROWS, 128), F32)

    def near_backward(j):
        def put(b, dk, dv):
            acc_k[b] = acc_k[b] + dk
            acc_v[b] = acc_v[b] + dv

        dq = backward(
            4,
            lambda b: near_kt[b],
            lambda b: near_v[b],
            [j],
            lambda n, h, b: e_near[h, j, b],
            lambda n, h: fac_n[h, j],
            put,
        )
        for h in range(2):
            acc_q[j, halves[h]] = dq[0][h]

    @pl.loop(0, EARLY)
    def _(j):
        near_backward(j)

        @pl.when(j == 0)
        def _():
            weight_over_cores()

    swap(3, g_far, g_got).wait_recv()
    swap(4, t_far, t_got).wait_recv()
    g_j = g_got[...].astype(F32)
    g_jt = g_j.T
    g_n[0, 4] = jnp.where(lane_row < HALF, g_j, 0.0).astype(BF16)
    g_n[1, 4] = jnp.where(lane_row < HALF, 0.0, g_j).astype(BF16)
    g_t[0, 4] = jnp.where(lane_col < HALF, g_jt, 0.0).astype(BF16)
    g_t[1, 4] = jnp.where(lane_col < HALF, 0.0, g_jt).astype(BF16)
    for h in range(2):
        delta[h, 4] = t_got[4 + h : 5 + h]
        for g in range(2):
            weight = jnp.exp2((top_f[0, h, g] - t_got[h : h + 1]) * EXP2)
            fac_f[0, h, g] = weight * t_got[2 + h : 3 + h]

    def gx_copy(slot):
        return remote(
            gkv_s.at[slot], gkv_x.at[slot], gx_send.at[slot], gx_recv.at[slot], "seq", sibling
        )

    def grad_copy(dz):
        return remote(
            gkv_s.at[in_z(dz, core)],
            gkv_r.at[dz],
            g_send.at[dz],
            g_recv.at[dz],
            "seq",
            in_seq(x_lo, dz, core),
        )

    def merge(i):
        dz = i + i // 2 - 2 * (i // 3)
        slot = in_z(dz, core)
        gx_copy(slot).wait_recv()
        for n in range(2):
            gkv_s[slot, n] = (gkv_s[slot, n].astype(F32) + gkv_x[slot, n].astype(F32)).astype(BF16)

        @pl.when(dz != 0)
        def _():
            grad_copy(dz).start()

    for j in (3, 4):
        acc_q[j] = jnp.zeros((128, ROWS), F32)

    @pl.loop(0, 4)
    def _(back):
        i = 3 - back
        dz = i + i // 2 - 2 * (i // 3)

        def put(b, dk, dv):
            slot = in_z(dz, b)
            gkv_s[slot, 0] = dk.astype(BF16)
            gkv_s[slot, 1] = dv.astype(BF16)

            @pl.when(core != b)
            def _():
                gx_copy(slot).start()

        dq = backward(
            2,
            lambda b: kv[in_z(dz, b), 0].T,
            lambda b: kv[in_z(dz, b), 1],
            [4, 3],
            lambda n, h, b: e_far[n, h, 2 * i + b],
            lambda n, h: fac_f[n, h, i // 2],
            put,
        )
        for n, j in enumerate((4, 3)):
            for h in range(2):
                acc_q[j, halves[h]] = acc_q[j, halves[h]] + dq[n][h]

        @pl.when(back > 0)
        def _():
            merge(i + 1)

        @pl.when(back == 0)
        def _():
            for n in range(1, NHEAD):
                w_copy(head, n).start()

        @pl.when(back == 2)
        def _():
            weight_over_chips()

    dq_far[...] = acc_q[4].astype(BF16)
    swap(5, dq_far, dq_got).start()
    acc_q[4] = acc_q[3]
    merge(0)

    @pl.loop(EARLY, RATE)
    def _(j):
        near_backward(j)

    for n in range(1, NHEAD):
        w_copy(peer_h(n), n).wait_recv()
        w_share(peer_h(n), core).start()
    swap(5, dq_far, dq_got).wait_recv()
    acc_q[3] = acc_q[3] + acc_q[4] + dq_got[...].astype(F32)
    dq_slots = [(acc_q[j] * SCALE).T for j in range(RATE)]
    dq_parts = [from_slot(dq_slots, shift_row, r).astype(BF16) for r in range(RATE)]
    dq_ref[...] = nn(jnp.concatenate(dq_parts, axis=1), perm[...]).astype(BF16)

    weight_to_sibling()
    for n in range(1, NHEAD):
        w_share(peer_h(n), 1 - core).wait_recv()
        at_copy(peer_h(n), n).wait_recv()
    from_rm = jnp.where(rm_row == lax.rem(rm_col, 32) * RATE + rm_col // 32, 1.0, 0.0).astype(BF16)
    result = jnp.zeros((128, WIDTH), F32)
    for h in range(NHEAD):
        rows = nn(from_rm, attn_r[h].reshape(128, 128)).astype(BF16)
        result = result + nn(rows, ws[h])
    lo_ref[...] = result.astype(BF16)

    for turn in turns:
        grad_copy(turn).wait_recv()
    far = []
    for n in range(2):
        total = gkv_s[own, n].astype(F32)
        for turn in turns:
            total = total + gkv_r[turn, n].astype(F32)
        far.append(total)
    sum_k, sum_v = far
    dk_parts = []
    dv_parts = []
    for r in range(RATE):
        mine = shift_row == r
        dk_parts.append(((acc_k[r] + jnp.where(mine, sum_k, 0.0)) * SCALE).astype(BF16))
        dv_parts.append((acc_v[r] + jnp.where(mine, sum_v, 0.0)).astype(BF16))
    dk_ref[...] = nn(jnp.concatenate(dk_parts, axis=1), perm[...]).astype(BF16)
    dv_ref[...] = nn(jnp.concatenate(dv_parts, axis=1), perm[...]).astype(BF16)

    dc_copy(1 - core).wait_recv()
    for half in range(2):
        whole = dwf[half].reshape(128, 384)
        dw_ref[0:48, half * 384 : (half + 1) * 384] = whole[0:48]
        dw_ref[48:96, half * 384 : (half + 1) * 384] = whole[64:112]

    dx_copy(1 - core).wait_send()
    dc_copy(core).wait_send()

    @pl.loop(0, 7)
    def _(i):
        kv_copy(own, i, partner).wait_send()

    @pl.loop(1, 8)
    def _(i):
        w_copy(head, i).wait_send()
        w_share(peer_h(i), core).wait_send()
        dy_copy(head, i - 1, partner_h).wait_send()
        at_copy(head, i).wait_send()
        dw_copy(chip, i).wait_send()
        df_copy(chip, i).wait_send()

    @pl.loop(0, 4)
    def _(i):
        gx_copy(i * 2 + 1 - core).wait_send()

    for turn in turns:
        grad_copy(turn).wait_send()
    swaps = ((q_far, q_got), (m_far, m_got), (o_far, o_got), (g_far, g_got), (t_far, t_got), (dq_far, dq_got))
    for i, (source, target) in enumerate(swaps):
        swap(i, source, target).wait_send()


def finish(*refs):
    for source, target in zip(refs[:5], refs[5:], strict=True):
        target[...] = source[...]


def body(queries, keys, values, slide_ids, head_shift_list, out_weight, d_y):
    vmem = pl.BlockSpec(memory_space=pltpu.VMEM)
    hbm = pl.BlockSpec(memory_space=pltpu.HBM)
    smem = pl.BlockSpec(memory_space=pltpu.SMEM)
    sems = pltpu.SemaphoreType.DMA
    results = pl.pallas_call(
        kernel,
        out_shape=(
            jax.ShapeDtypeStruct((128, WIDTH), BF16),
            jax.ShapeDtypeStruct((ROWS, 384), BF16),
            jax.ShapeDtypeStruct((ROWS, 384), BF16),
            jax.ShapeDtypeStruct((ROWS, 384), BF16),
            jax.ShapeDtypeStruct((96, WIDTH), BF16),
        ),
        in_specs=[hbm, hbm, hbm, vmem, smem, hbm, hbm],
        out_specs=(vmem,) * 5,
        scratch_shapes=[
            pltpu.VMEM((ROWS, 384), BF16),
            pltpu.VMEM((ROWS, 384), BF16),
            pltpu.VMEM((ROWS, 384), BF16),
            pltpu.VMEM((NHEAD, 128, WIDTH), BF16),
            pltpu.VMEM((4 * 128, 384), BF16),
            pltpu.VMEM((4, ROWS, 128), BF16),
            pltpu.VMEM((4, ROWS, 128), BF16),
            pltpu.VMEM((4, 128, ROWS), BF16),
            pltpu.VMEM((4, 128, ROWS), BF16),
            pltpu.VMEM((8, 2, ROWS, 128), BF16),
            pltpu.VMEM((8, 128, ROWS), BF16),
            pltpu.VMEM((RATE, ROWS, 128), BF16),
            pltpu.VMEM((2, 5, 128, ROWS), BF16),
            pltpu.VMEM((2, 5, ROWS, 128), BF16),
            pltpu.VMEM((2, 5, 128, ROWS), BF16),
            pltpu.VMEM((2, 5, ROWS, 128), BF16),
            pltpu.VMEM((2, RATE, 4, ROWS, ROWS), F32),
            pltpu.VMEM((2, 2, 8, ROWS, ROWS), F32),
            pltpu.VMEM((2, 1, ROWS), F32),
            pltpu.VMEM((2, 1, ROWS), F32),
            pltpu.VMEM((2, HALF, ROWS), F32),
            pltpu.VMEM((2, 2, 2, 1, ROWS), F32),
            pltpu.VMEM((2, 2, 2, 1, ROWS), F32),
            pltpu.VMEM((2, 2, 2, HALF, ROWS), F32),
            pltpu.VMEM((2, RATE, 1, ROWS), F32),
            pltpu.VMEM((2, 2, 2, 1, ROWS), F32),
            pltpu.VMEM((2, 5, 1, ROWS), F32),
            pltpu.VMEM((RATE, 128, ROWS), BF16),
            pltpu.VMEM((RATE, ROWS, 128), BF16),
            pltpu.VMEM((NHEAD, RATE, 32, 128), BF16),
            pltpu.VMEM((RATE, ROWS, WIDTH), BF16),
            pltpu.VMEM((NHEAD, 128, WIDTH), BF16),
            pltpu.VMEM((2, 8, 16, 384), F32),
            pltpu.VMEM((8, 16, 384), F32),
            pltpu.VMEM((8, 16, 384), F32),
            pltpu.VMEM((8, 16, 384), F32),
            pltpu.VMEM((2, 8, 16, 384), BF16),
            pltpu.VMEM((8, 2, ROWS, 128), BF16),
            pltpu.VMEM((8, 2, ROWS, 128), BF16),
            pltpu.VMEM((4, 2, ROWS, 128), BF16),
            pltpu.VMEM((ROWS, 128), BF16),
            pltpu.VMEM((ROWS, 128), BF16),
            pltpu.VMEM((ROWS, 128), BF16),
            pltpu.VMEM((ROWS, 128), BF16),
            pltpu.VMEM((128, ROWS), BF16),
            pltpu.VMEM((128, ROWS), BF16),
            pltpu.VMEM((8, ROWS), F32),
            pltpu.VMEM((8, ROWS), F32),
            pltpu.VMEM((8, ROWS), F32),
            pltpu.VMEM((8, ROWS), F32),
            pltpu.VMEM((128, ROWS), BF16),
            pltpu.VMEM((128, ROWS), BF16),
            pltpu.VMEM((4, ROWS, 128), F32),
            pltpu.VMEM((4, ROWS, 128), F32),
            pltpu.VMEM((5, 128, ROWS), F32),
            sems((6,)),
            sems((8,)),
            sems((8,)),
            sems((NHEAD,)),
            sems((NHEAD,)),
            sems((NHEAD,)),
            sems((NHEAD,)),
            sems((NHEAD,)),
            sems((NHEAD,)),
            sems((NHEAD,)),
            sems((NHEAD,)),
            sems((2,)),
            sems((8,)),
            sems((8,)),
            sems((8,)),
            sems((8,)),
            sems((2,)),
            sems((8,)),
            sems((8,)),
            sems((4,)),
            sems((4,)),
            sems((6,)),
            sems((6,)),
        ],
        compiler_params=pltpu.CompilerParams(
            collective_id=0, has_side_effects=True, vmem_limit_bytes=56 * 1024 * 1024
        ),
        cost_estimate=pl.CostEstimate(
            flops=3_000_000_000, bytes_accessed=4_000_000, transcendentals=5_000_000
        ),
    )(
        queries,
        keys,
        values,
        slide_ids.reshape(8, 128),
        head_shift_list,
        out_weight,
        d_y,
    )
    return pl.pallas_call(
        finish,
        out_shape=tuple(jax.ShapeDtypeStruct(r.shape, r.dtype) for r in results),
        in_specs=[vmem] * 5,
        out_specs=(vmem,) * 5,
    )(*results)


def solution(mesh):
    placed = (
        P("seq", "head"),
        P("seq", "head"),
        P("seq", "head"),
        P("seq"),
        P(),
        P("head", None),
        P(("seq", "head"), None),
    )
    return jax.shard_map(
        body,
        mesh=mesh,
        in_specs=placed,
        out_specs=(
            P(("seq", "head"), None),
            P("seq", "head"),
            P("seq", "head"),
            P("seq", "head"),
            P("head", None),
        ),
        check_vma=False,
    )
```
